512 devices in a mesh: dp: 128 (over z, x, core), tensor: 4 (over y).
Axes of the slice: x: 4, y: 4, z: 16, core: 2. Of those that a mesh axis runs over, the one named last changes fastest.
Arguments:
- tokens: bfloat16 [32768, 1536], P('dp'), may hold values from -6 to 6
- targets: bfloat16 [32768, 1536], P('dp'), may hold values from -6 to 6
- modulation: bfloat16 [256, 3, 1536], P('dp'), may hold values from -2.5 to 2.5
- live_block_count: int32 [128], P('dp'), may hold values from 2 to 4, as said below
- preferred_blocks: int32 [128], P('dp'), may hold values from 1 to 3, as said below
- last_block_rows: int32 [128, 2], P('dp'), may hold values from 1 to 64
- up_projection_weight: bfloat16 [1536, 6144], P('dp', 'tensor'), may hold values from -0.15625 to 0.15625
- down_weight_transposed: bfloat16 [1536, 6144], P('dp', 'tensor'), may hold values from -0.078125 to 0.078125
- adapter_input_factor: bfloat16 [1536, 64], replicated, may hold values from -0.15625 to 0.15625
- adapter_output_factor: bfloat16 [64, 6144], P(None, 'tensor'), may hold values from -0.75 to 0.75
Outputs:
- losses: float32 [128], P('dp')
- grad_tokens: bfloat16 [32768, 1536], P('dp')
- grad_lora_a: float32 [1536, 64], replicated
- grad_lora_b: float32 [64, 6144], P(None, 'tensor')
The draws below stay inside these ranges and needn't reach their ends.
Inputs may be any that keep to these rules, and one draw needn't show every extreme that they name: `live_block_count`: device i of dp and device (i + 64) modulo 128 together hold 6 live blocks; some pair holds 4. `preferred_blocks`: at most live_block_count - 1 for each pair, so the loser has a block too.
All inputs are finite; a program needn't handle non-finite values.
Results may differ from the reference program's by a relative error of at most 0.035.
Values may be sent and summed in bfloat16 or wider, within the bound.
No kernel may reach another device: no remote copies, remote signals or barrier semaphores. Data moves between devices by JAX's collectives and lax.ppermute only.
A program may use at most 64 MiB of HBM per device.

```python
import jax
import jax.numpy as jnp
from jax import lax

MODEL_WIDTH = 1536
HIDDEN_UNITS = 6144
LOW_RANK_SIZE = 64
BLK = 64
HOLD = 3
CAP = 4
SAMPLES = 256
ROWS = 32768
N_DP = 128
N_TENSOR = 4


def pair_loads(key):
    half = N_DP // 2
    offset = jax.random.randint(key, (half,), -1, 2)
    offset = offset.at[0].set(1)
    return jnp.concatenate([HOLD + offset, HOLD - offset]).astype(jnp.int32)


def draw_live_block_count(key, part):
    return pair_loads(key)


def draw_preferred_blocks(key, part):
    loads = pair_loads(key)
    key = jax.random.fold_in(key, 7)
    spread = jax.random.randint(key, (N_DP,), 0, 1 << 20)
    chosen = 1 + spread % (loads - 1)
    chosen = chosen.at[0].set(loads[0] - 1)
    return chosen.astype(jnp.int32)


def draw_last_block_rows(key, part):
    key = jax.random.fold_in(key, 11)
    rows = jax.random.randint(key, (N_DP, 2), 1, BLK + 1)
    rows = rows.at[0, 0].set(BLK)
    rows = rows.at[0, 1].set(1)
    return rows.astype(jnp.int32)


def shard_levels(rng, shape, split, least, high):
    def one(dim, blocks):
        steps = jax.random.uniform(jax.random.fold_in(jax.random.fold_in(rng, 6), dim), (blocks,), jnp.float32, least / len(split), high / len(split))
        return jnp.repeat(jnp.exp(steps), shape[dim] // blocks).reshape((-1,) + (1,) * (len(shape) - dim - 1))

    loudness = one(*split[0])
    for cut in split[1:]:
        loudness = loudness * one(*cut)
    return loudness


def noise(rng, shape, deviation, limit, pieces=(), held_as=jnp.bfloat16):
    array = jax.random.normal(rng, shape, jnp.float32) * deviation
    if len(pieces) > 0:
        array = shard_levels(rng, shape, pieces, -0.22, 0.18) * array
    return jnp.clip(array, min=-limit, max=limit).astype(held_as)


def setup_inputs(seed: int = 0) -> dict:
    splits = jax.random.split(jax.random.key(seed), 11)
    tokens = noise(splits[0], (ROWS, MODEL_WIDTH), 1.0, 6.0, ((0, 128),))
    targets = noise(splits[1], (ROWS, MODEL_WIDTH), 1.0, 6.0, ((0, 128),))
    modulation = noise(splits[2], (SAMPLES, 3, MODEL_WIDTH), 0.5, 2.5, ((0, 128),))
    live_block_count = draw_live_block_count(jax.random.fold_in(splits[10], 71), 0)
    preferred_blocks = draw_preferred_blocks(jax.random.fold_in(splits[10], 71), 0)
    last_block_rows = draw_last_block_rows(jax.random.fold_in(splits[10], 71), 0)
    up_projection_weight = noise(splits[6], (MODEL_WIDTH, HIDDEN_UNITS), MODEL_WIDTH ** -0.5, 0.15625, ((0, 128), (1, 4)))
    down_weight_transposed = noise(splits[7], (MODEL_WIDTH, HIDDEN_UNITS), HIDDEN_UNITS ** -0.5, 0.078125, ((0, 128), (1, 4)))
    adapter_input_factor = noise(splits[8], (MODEL_WIDTH, LOW_RANK_SIZE), MODEL_WIDTH ** -0.5, 0.15625)
    adapter_output_factor = noise(splits[9], (LOW_RANK_SIZE, HIDDEN_UNITS), LOW_RANK_SIZE ** -0.5, 0.75, ((1, 4),))
    return {"tokens": tokens, "targets": targets, "modulation": modulation, "live_block_count": live_block_count, "preferred_blocks": preferred_blocks, "last_block_rows": last_block_rows, "up_projection_weight": up_projection_weight, "down_weight_transposed": down_weight_transposed, "adapter_input_factor": adapter_input_factor, "adapter_output_factor": adapter_output_factor}


EPS = 1e-06
BETA = 20.0
LOSS_SCALE = 4096.0

def settle_gradients(value):
    return lax.optimization_barrier(value.astype(jnp.bfloat16)).astype(jnp.float32)

def layer_norm(image_blocks):
    wide = image_blocks.astype(jnp.float32)
    center = wide - lax.optimization_barrier(jnp.mean(wide, axis=-1, keepdims=True))
    inverse_deviation = lax.rsqrt(lax.optimization_barrier(jnp.mean(center * center, axis=-1, keepdims=True)) + EPS)
    return (center * inverse_deviation, inverse_deviation)

def gelu_and_slope(pre):

    def act(value):
        return jax.nn.gelu(value, approximate=True)
    value, back = jax.vjp(act, pre)
    return (value, back(jnp.ones_like(pre))[0])

def contract_trailing(left, right):
    return lax.dot_general(left, right, (((1,), (1,)), ((), ())), preferred_element_type=jnp.float32)

def device_partial_sum(left, right):
    group = left.shape[1] // N_TENSOR
    total = jnp.zeros((left.shape[0], right.shape[0]), jnp.float32)
    for part in range(N_TENSOR):
        total = total + settle_gradients(contract_trailing(left[:, part * group:(part + 1) * group], right[:, part * group:(part + 1) * group]))
    return total

def slot_layout(live_block_count, preferred_blocks, last_block_rows):
    slots = jnp.arange(CAP, dtype=jnp.int32)[None, :]
    count = live_block_count[:, None]
    wins = preferred_blocks[:, None]
    flags = (slots >= wins).astype(jnp.int32)
    last = jnp.where(flags == 0, wins - 1, count - 1)
    tail = jnp.where(flags == 0, last_block_rows[:, 0:1], last_block_rows[:, 1:2])
    live = jnp.where(slots < count, jnp.where(slots == last, tail, BLK), 0)
    masks = (jnp.arange(BLK, dtype=jnp.int32)[None, None, :] < live[:, :, None]).astype(jnp.float32)
    return (flags, live, masks)

def forward_pass(image_blocks, modulation_slots, up_projection_weight, down_weight_transposed, adapter_input_factor, adapter_output_factor):
    modulation_vectors = modulation_slots.astype(jnp.float32)
    shift = modulation_vectors[:, None, 0]
    modulation_scale = 1.0 + modulation_vectors[:, None, 1]
    output_gate = modulation_vectors[:, None, 2]
    normalized_input, inverse_deviation = layer_norm(image_blocks)
    count_rows = image_blocks.shape[0] * image_blocks.shape[1]
    modulated_input = (normalized_input * modulation_scale + shift).astype(jnp.bfloat16).reshape(count_rows, image_blocks.shape[2])
    low_rank_hidden = jnp.dot(modulated_input, adapter_input_factor, preferred_element_type=jnp.float32).astype(jnp.bfloat16)
    reference_preactivation = jnp.dot(modulated_input, up_projection_weight, preferred_element_type=jnp.float32)
    policy_preactivation = reference_preactivation + jnp.dot(low_rank_hidden, adapter_output_factor, preferred_element_type=jnp.float32)
    act_pol, policy_activation_slope = gelu_and_slope(policy_preactivation)
    hid_pol = act_pol.astype(jnp.bfloat16)
    hid_ref = jax.nn.gelu(reference_preactivation, approximate=True).astype(jnp.bfloat16)
    sum_pol = device_partial_sum(hid_pol, down_weight_transposed).reshape(image_blocks.shape)
    sum_ref = device_partial_sum(hid_ref, down_weight_transposed).reshape(image_blocks.shape)
    wide = image_blocks.astype(jnp.float32)
    return (normalized_input, inverse_deviation, modulation_scale, output_gate, modulated_input, low_rank_hidden, policy_activation_slope, wide + output_gate * sum_pol, wide + output_gate * sum_ref)

def reference(tokens, targets, modulation, live_block_count, preferred_blocks, last_block_rows, up_projection_weight, down_weight_transposed, adapter_input_factor, adapter_output_factor):
    flags, live, masks = slot_layout(live_block_count, preferred_blocks, last_block_rows)
    token_blocks = tokens.reshape(N_DP, CAP, BLK, MODEL_WIDTH)
    target_blocks = targets.reshape(N_DP, CAP, BLK, MODEL_WIDTH)
    mod_pairs = modulation.reshape(N_DP, 2, 3, MODEL_WIDTH)
    modulation_slots = jnp.where(flags[:, :, None, None] == 0, mod_pairs[:, 0:1], mod_pairs[:, 1:2])

    def errors(item):
        image_blocks, goals, modulation_vectors, mask = item
        step_result = forward_pass(image_blocks, modulation_vectors, up_projection_weight, down_weight_transposed, adapter_input_factor, adapter_output_factor)
        goal = goals.astype(jnp.float32)
        miss_pol = step_result[7] - goal
        miss_ref = step_result[8] - goal
        return (lax.optimization_barrier(jnp.sum(mask[:, :, None] * miss_pol * miss_pol, axis=(1, 2))), lax.optimization_barrier(jnp.sum(mask[:, :, None] * miss_ref * miss_ref, axis=(1, 2))))
    err_pol, err_ref = lax.map(errors, (token_blocks, target_blocks, modulation_slots, masks))
    ids = (2 * jnp.arange(N_DP, dtype=jnp.int32)[:, None] + flags).reshape(-1)
    picks = (ids[:, None] == jnp.arange(2 * N_DP, dtype=jnp.int32)[None, :]).astype(jnp.float32)
    tot_pol = lax.optimization_barrier(jnp.sum(err_pol.reshape(-1)[:, None] * picks, axis=0))
    tot_ref = lax.optimization_barrier(jnp.sum(err_ref.reshape(-1)[:, None] * picks, axis=0))
    rows_of = lax.optimization_barrier(jnp.sum(live.reshape(-1)[:, None].astype(jnp.float32) * picks, axis=0))
    scale_rows = 1.0 / (MODEL_WIDTH * rows_of)
    pair_gap = ((tot_pol - tot_ref) * scale_rows).reshape(N_DP, 2)
    inside = -BETA * (pair_gap[:, 0] - pair_gap[:, 1])
    losses = jax.nn.softplus(-inside)
    weight = BETA * LOSS_SCALE * jax.nn.sigmoid(-inside)
    coef = jnp.stack([weight, -weight], axis=1).reshape(2 * N_DP) * scale_rows
    slot_coef = coef[ids].reshape(N_DP, CAP)

    def backward(carry, item):
        image_blocks, goals, modulation_vectors, mask, factor = item
        normalized_input, inverse_deviation, modulation_scale, output_gate, modulated_input, low_rank_hidden, policy_activation_slope, policy_output, ignored_value = forward_pass(image_blocks, modulation_vectors, up_projection_weight, down_weight_transposed, adapter_input_factor, adapter_output_factor)
        out_grad = factor[:, None, None] * 2.0 * mask[:, :, None] * (policy_output - goals.astype(jnp.float32))
        count_rows = image_blocks.shape[0] * image_blocks.shape[1]
        dy = (output_gate * out_grad).astype(jnp.bfloat16).reshape(count_rows, MODEL_WIDTH)
        dh = jnp.dot(dy, down_weight_transposed, preferred_element_type=jnp.float32)
        preactivation_gradient = (dh * policy_activation_slope).astype(jnp.bfloat16)
        grad_b = lax.dot_general(low_rank_hidden, preactivation_gradient, (((0,), (0,)), ((), ())), preferred_element_type=jnp.float32)
        low_rank_gradient = device_partial_sum(preactivation_gradient, adapter_output_factor).astype(jnp.bfloat16)
        modulation_gradient = device_partial_sum(preactivation_gradient, up_projection_weight) + contract_trailing(low_rank_gradient, adapter_input_factor)
        dn = modulation_gradient.reshape(image_blocks.shape) * modulation_scale
        back = inverse_deviation * (dn - lax.optimization_barrier(jnp.sum(dn, axis=-1, keepdims=True)) / MODEL_WIDTH - normalized_input * lax.optimization_barrier(jnp.sum(dn * normalized_input, axis=-1, keepdims=True)) / MODEL_WIDTH)
        grad = (out_grad + back).astype(jnp.bfloat16)
        grad_a = lax.dot_general(modulated_input, low_rank_gradient, (((0,), (0,)), ((), ())), preferred_element_type=jnp.float32)
        return ((carry[0] + grad_a, carry[1] + grad_b), grad)
    start = (jnp.zeros((MODEL_WIDTH, LOW_RANK_SIZE), jnp.float32), jnp.zeros((LOW_RANK_SIZE, HIDDEN_UNITS), jnp.float32))
    totals, grads = lax.scan(backward, start, (token_blocks, target_blocks, modulation_slots, masks, slot_coef))
    return (losses, grads.reshape(N_DP * CAP * BLK, MODEL_WIDTH), totals[0] / N_DP, totals[1] / N_DP)
```

```python
import jax
import jax.numpy as jnp
from jax import lax
from jax.sharding import Mesh
from jax.sharding import PartitionSpec as P

BLK = 64
CAP = 4
EPS = 1e-06
BETA = 20.0
LOSS_SCALE = 4096.0
ROOT = 0.7978845608028654
CUBE = 0.044715
BF16 = jnp.bfloat16
F32 = jnp.float32
DP = ("z", "x", "c")
SWAP = [(0, 1), (1, 0)]


def gelu(pre):
    th = jnp.tanh(ROOT * (pre + CUBE * pre * pre * pre))
    return 0.5 * pre * (1.0 + th)


def gelu_and_slope(pre):
    square = pre * pre
    th = jnp.tanh(ROOT * (pre + CUBE * pre * square))
    half = 0.5 * (1.0 + th)
    slope = half + 0.5 * pre * (1.0 - th * th) * (ROOT * (1.0 + 3.0 * CUBE * square))
    return pre * half, slope


def rows_by_rows(left, right):
    return lax.dot_general(left, right, (((1,), (1,)), ((), ())), preferred_element_type=F32)


def columns_by_columns(left, right):
    return lax.dot_general(left, right, (((0,), (0,)), ((), ())), preferred_element_type=F32)


def product(left, right):
    return jnp.dot(left, right, preferred_element_type=F32)


def spread(value, axes, n):
    return lax.all_to_all(jnp.broadcast_to(value[None], (n, *value.shape)), axes, 0, 0, tiled=True)


def per_device(
    tokens,
    targets,
    modulation,
    live_block_count,
    preferred_blocks,
    last_block_rows,
    up_rows,
    down_rows,
    factor_in,
    factor_out,
):
    width = tokens.shape[1]
    n_z, n_x, n_c, n_t = (lax.axis_size(a) for a in ("z", "x", "c", "t"))
    n_dp = n_z * n_x * n_c
    core = lax.axis_index("c")
    group = lax.axis_index("t")
    thin, hidden = up_rows.shape
    half = hidden // n_c

    down_split = down_rows.reshape(thin, n_c, half).transpose(1, 0, 2)
    down_sent = jnp.broadcast_to(down_split[None], (n_x, n_c, thin, half)).reshape(n_x * n_c, thin, half)
    down_near = lax.all_to_all(down_sent, ("x", "c"), 0, 0, tiled=True)
    down_own = lax.all_gather(down_near.reshape(n_x * n_c * thin, half), "z", axis=0, tiled=True)

    up_keep = lax.dynamic_slice_in_dim(up_rows, core * half, half, axis=1)
    up_give = lax.dynamic_slice_in_dim(up_rows, (1 - core) * half, half, axis=1)
    up_got = lax.ppermute(up_give, "c", SWAP)
    up_pair = jnp.where(
        core == 0, jnp.concatenate([up_keep, up_got], 0), jnp.concatenate([up_got, up_keep], 0)
    )
    up_line = lax.all_gather(up_pair, "z", axis=0, tiled=True)
    up_all = spread(up_line, "x", n_x).reshape(n_x, n_z, n_c * thin, half)
    up_own = up_all.transpose(1, 0, 2, 3).reshape(width, half)
    up_other = lax.ppermute(up_own, "c", SWAP)
    down_other = lax.ppermute(down_own, "c", SWAP)

    count = live_block_count[0]
    wins = preferred_blocks[0]
    slots = jnp.arange(CAP, dtype=jnp.int32)
    flags = (slots >= wins).astype(jnp.int32)
    last = jnp.where(flags == 0, wins - 1, count - 1)
    tail = jnp.where(flags == 0, last_block_rows[0, 0], last_block_rows[0, 1])
    live = jnp.where(slots < count, jnp.where(slots == last, tail, BLK), 0)
    rows_first = jnp.sum(jnp.where(flags == 0, live, 0)).astype(F32)
    rows_second = jnp.sum(jnp.where(flags == 1, live, 0)).astype(F32)
    scale_first = 1.0 / (width * rows_first)
    scale_second = 1.0 / (width * rows_second)

    vectors = modulation.astype(F32)
    pick = (flags == 0)[:, None, None]
    shift = jnp.where(pick, vectors[0, 0][None, None], vectors[1, 0][None, None])
    scale = 1.0 + jnp.where(pick, vectors[0, 1][None, None], vectors[1, 1][None, None])

    def normalise(rows):
        wide = rows.astype(F32)
        center = wide - jnp.mean(wide, axis=-1, keepdims=True)
        inverse = lax.rsqrt(jnp.mean(center * center, axis=-1, keepdims=True) + EPS)
        return center * inverse, inverse

    normed, _ = normalise(tokens.reshape(CAP, BLK, width))
    modded = (normed * scale + shift).astype(BF16).reshape(CAP * BLK, width)
    low = product(modded, factor_in).astype(BF16)

    factor_own = lax.dynamic_slice_in_dim(factor_out, core * half, half, axis=1)
    factor_other = lax.dynamic_slice_in_dim(factor_out, (1 - core) * half, half, axis=1)

    def activate(w_up, factor):
        pre_ref = product(modded, w_up)
        pre_pol = pre_ref + product(low, factor)
        act, slope = gelu_and_slope(pre_pol)
        return act.astype(BF16), gelu(pre_ref).astype(BF16), slope

    pol_own, ref_own, slope_own = activate(up_own, factor_own)
    pol_other, ref_other, slope_other = activate(up_other, factor_other)

    part_pol = rows_by_rows(pol_own, down_own) + rows_by_rows(pol_other, down_other)
    part_ref = rows_by_rows(ref_own, down_own) + rows_by_rows(ref_other, down_other)
    parts = jnp.concatenate(
        [
            part_pol.astype(BF16).reshape(CAP, BLK, width),
            part_ref.astype(BF16).reshape(CAP, BLK, width),
        ],
        axis=1,
    )
    parts = lax.all_to_all(parts, "t", 0, 0, tiled=True)
    sums = jnp.sum(parts.astype(F32), axis=0)

    flag = (group >= wins).astype(jnp.int32)
    x_own = lax.dynamic_slice_in_dim(tokens, group * BLK, BLK, axis=0)
    t_own = lax.dynamic_slice_in_dim(targets, group * BLK, BLK, axis=0).astype(F32)
    vec_own = jnp.where(flag == 0, vectors[0], vectors[1])
    live_own = lax.dynamic_slice_in_dim(live, group, 1)
    mask = (jnp.arange(BLK, dtype=jnp.int32)[:, None] < live_own[None, :]).astype(F32)
    gate = vec_own[2][None]
    base = x_own.astype(F32) - t_own
    miss_pol = base + gate * sums[:BLK]
    miss_ref = base + gate * sums[BLK:]
    excess = jnp.sum(mask * (miss_pol - miss_ref) * (miss_pol + miss_ref))
    grad_unit = 2.0 * mask * miss_pol
    dy_unit = (gate * grad_unit).astype(BF16)
    high = excess.astype(BF16)
    rest = excess - high.astype(F32)
    middle = rest.astype(BF16)
    lowest = (rest - middle.astype(F32)).astype(BF16)
    note = jnp.zeros((16, width), BF16)
    line = jnp.arange(16, dtype=jnp.int32)[:, None]
    note = jnp.where(line == 0, high, jnp.where(line == 1, middle, jnp.where(line == 2, lowest, note)))
    shared = spread(jnp.concatenate([dy_unit, note], 0), "t", n_t)
    dy = shared[:, :BLK].reshape(CAP * BLK, width)
    excesses = jnp.sum(shared[:, BLK : BLK + 3, 0].astype(F32), axis=1)
    gap_first = jnp.sum(jnp.where(flags == 0, excesses, 0.0)) * scale_first
    gap_second = jnp.sum(jnp.where(flags == 1, excesses, 0.0)) * scale_second
    inside = -BETA * (gap_first - gap_second)
    losses = jax.nn.softplus(-inside)[None]
    weight = BETA * LOSS_SCALE * jax.nn.sigmoid(-inside)
    coef = jnp.where(flags == 0, weight * scale_first, -weight * scale_second)
    coef_rows = jnp.broadcast_to(coef[:, None], (CAP, BLK)).reshape(CAP * BLK, 1)
    coef_own = jnp.where(flag == 0, weight * scale_first, -weight * scale_second)

    dpre_own = (product(dy, down_own) * coef_rows * slope_own).astype(BF16)
    dpre_other = (product(dy, down_other) * coef_rows * slope_other).astype(BF16)
    dlow = (rows_by_rows(dpre_own, factor_own) + rows_by_rows(dpre_other, factor_other)).astype(BF16)
    dm_part = (
        rows_by_rows(dpre_own, up_own) + rows_by_rows(dpre_other, up_other) + rows_by_rows(dlow, factor_in)
    ).astype(BF16)
    grad_a = columns_by_columns(dlow, modded).astype(BF16)
    b_own = columns_by_columns(low, dpre_own).astype(BF16)
    b_other = columns_by_columns(low, dpre_other).astype(BF16)
    grad_b = jnp.where(
        core == 0, jnp.concatenate([b_own, b_other], 1), jnp.concatenate([b_other, b_own], 1)
    )
    rank = grad_a.shape[0]
    slab = rank // n_t
    back = lax.all_to_all(
        jnp.concatenate([dm_part.reshape(CAP, BLK, width), grad_a.reshape(n_t, slab, width)], 1),
        "t",
        0,
        0,
        tiled=True,
    )
    back = jnp.sum(back.astype(F32), axis=0)
    normed_own, inverse_own = normalise(x_own)
    dn = back[:BLK] * (1.0 + vec_own[1][None])
    mean_one = jnp.mean(dn, axis=-1, keepdims=True)
    mean_two = jnp.mean(dn * normed_own, axis=-1, keepdims=True)
    grad_block = coef_own * grad_unit + inverse_own * (dn - mean_one - normed_own * mean_two)

    pile = jnp.concatenate([grad_b, back[BLK:].astype(BF16)], 0)
    lines = pile.shape[0]
    share = lines * width // n_dp
    pieces = lax.all_to_all(pile.reshape(n_dp, share), DP, 0, 0, tiled=True)
    total = (jnp.sum(pieces.astype(F32), axis=0) / n_dp).astype(BF16)
    pile = spread(total, DP, n_dp).reshape(lines, width)
    sum_b = pile[:rank].astype(F32)
    final = spread(jnp.concatenate([grad_block.astype(BF16), pile[rank:]], 0), "t", n_t)
    grad_tokens = final[:, :BLK].reshape(CAP * BLK, width)
    sum_a = final[:, BLK:].reshape(rank, width).astype(F32).T
    return losses, grad_tokens, sum_a, sum_b


def solution(mesh):
    n_dp, n_t = mesh.devices.shape
    fine = Mesh(mesh.devices.reshape(n_dp // 8, 4, 2, n_t), ("z", "x", "c", "t"))
    return jax.shard_map(
        per_device,
        mesh=fine,
        in_specs=(
            P(DP, None),
            P(DP, None),
            P(DP, None, None),
            P(DP),
            P(DP),
            P(DP, None),
            P(DP, "t"),
            P(DP, "t"),
            P(),
            P(None, "t"),
        ),
        out_specs=(P(DP), P(DP, None), P(), P(None, "t")),
        check_vma=False,
    )
```

```python
import jax
import jax.numpy as jnp
from jax import lax
from jax.sharding import Mesh
from jax.sharding import PartitionSpec as P

BLK = 64
CAP = 4
EPS = 1e-06
BETA = 20.0
LOSS_SCALE = 4096.0
ROOT = 0.7978845608028654
CUBE = 0.044715
BF16 = jnp.bfloat16
F32 = jnp.float32
DP = ("z", "x", "c")
CHIPS = ("z", "x")
LANES = 128
SWAP = [(0, 1), (1, 0)]


def gelu(pre):
    th = jnp.tanh(ROOT * (pre + CUBE * pre * pre * pre))
    return 0.5 * pre * (1.0 + th)


def gelu_and_slope(pre):
    square = pre * pre
    th = jnp.tanh(ROOT * (pre + CUBE * pre * square))
    half = 0.5 * (1.0 + th)
    slope = half + 0.5 * pre * (1.0 - th * th) * (ROOT * (1.0 + 3.0 * CUBE * square))
    return pre * half, slope


def rows_by_rows(left, right):
    return lax.dot_general(left, right, (((1,), (1,)), ((), ())), preferred_element_type=F32)


def columns_by_columns(left, right):
    return lax.dot_general(left, right, (((0,), (0,)), ((), ())), preferred_element_type=F32)


def product(left, right):
    return jnp.dot(left, right, preferred_element_type=F32)


def spread(value, axes, n):
    return lax.all_to_all(jnp.broadcast_to(value[None], (n, *value.shape)), axes, 0, 0, tiled=True)


def per_device(
    tokens,
    targets,
    modulation,
    live_block_count,
    preferred_blocks,
    last_block_rows,
    up_rows,
    down_rows,
    factor_in,
    factor_out,
):
    width = tokens.shape[1]
    n_z, n_x, n_c, n_t = (lax.axis_size(a) for a in ("z", "x", "c", "t"))
    n_dp = n_z * n_x * n_c
    core = lax.axis_index("c")
    group = lax.axis_index("t")
    thin, hidden = up_rows.shape
    half = hidden // n_c

    both = jnp.concatenate([up_rows, down_rows], axis=0)
    keep = lax.dynamic_slice_in_dim(both, core * half, half, axis=1)
    got = lax.ppermute(lax.dynamic_slice_in_dim(both, (1 - core) * half, half, axis=1), "c", SWAP)
    first = jnp.where(core == 0, keep, got)
    second = jnp.where(core == 0, got, keep)
    up_pair = jnp.concatenate([first[:thin], second[:thin]], axis=0)
    down_pair = jnp.concatenate([first[thin:], second[thin:]], axis=0)

    def whole(line):
        rows = spread(line, "x", n_x).reshape(n_x, n_z, n_c * thin, half)
        return rows.transpose(1, 0, 2, 3).reshape(width, half)

    up_line = lax.all_gather(up_pair, "z", axis=0, tiled=True)
    down_pair, up_line = lax.optimization_barrier((down_pair, up_line))
    down_line = lax.all_gather(down_pair, "z", axis=0, tiled=True)
    up_own = whole(up_line)
    up_other = lax.ppermute(up_own, "c", SWAP)
    down_own = whole(down_line)
    down_other = lax.ppermute(down_own, "c", SWAP)

    count = live_block_count[0]
    wins = preferred_blocks[0]
    slots = jnp.arange(CAP, dtype=jnp.int32)
    flags = (slots >= wins).astype(jnp.int32)
    last = jnp.where(flags == 0, wins - 1, count - 1)
    tail = jnp.where(flags == 0, last_block_rows[0, 0], last_block_rows[0, 1])
    live = jnp.where(slots < count, jnp.where(slots == last, tail, BLK), 0)
    rows_first = jnp.sum(jnp.where(flags == 0, live, 0)).astype(F32)
    rows_second = jnp.sum(jnp.where(flags == 1, live, 0)).astype(F32)
    scale_first = 1.0 / (width * rows_first)
    scale_second = 1.0 / (width * rows_second)

    vectors = modulation.astype(F32)
    pick = (flags == 0)[:, None, None]
    shift = jnp.where(pick, vectors[0, 0][None, None], vectors[1, 0][None, None])
    scale = 1.0 + jnp.where(pick, vectors[0, 1][None, None], vectors[1, 1][None, None])

    def normalise(rows):
        wide = rows.astype(F32)
        center = wide - jnp.mean(wide, axis=-1, keepdims=True)
        inverse = lax.rsqrt(jnp.mean(center * center, axis=-1, keepdims=True) + EPS)
        return center * inverse, inverse

    normed, _ = normalise(tokens.reshape(CAP, BLK, width))
    modded = (normed * scale + shift).astype(BF16).reshape(CAP * BLK, width)
    low = product(modded, factor_in).astype(BF16)

    factor_own = lax.dynamic_slice_in_dim(factor_out, core * half, half, axis=1)
    factor_other = lax.dynamic_slice_in_dim(factor_out, (1 - core) * half, half, axis=1)

    def activate(w_up, factor):
        pre_ref = product(modded, w_up)
        pre_pol = pre_ref + product(low, factor)
        act, slope = gelu_and_slope(pre_pol)
        return act.astype(BF16), gelu(pre_ref).astype(BF16), slope

    pol_own, ref_own, slope_own = activate(up_own, factor_own)
    pol_other, ref_other, slope_other = activate(up_other, factor_other)

    part_pol = rows_by_rows(pol_own, down_own) + rows_by_rows(pol_other, down_other)
    part_ref = rows_by_rows(ref_own, down_own) + rows_by_rows(ref_other, down_other)
    parts = jnp.concatenate(
        [
            part_pol.astype(BF16).reshape(CAP, BLK, width),
            part_ref.astype(BF16).reshape(CAP, BLK, width),
        ],
        axis=1,
    )
    parts = lax.all_to_all(parts, "t", 0, 0, tiled=True)
    sums = jnp.sum(parts.astype(F32), axis=0)

    flag = (group >= wins).astype(jnp.int32)
    x_own = lax.dynamic_slice_in_dim(tokens, group * BLK, BLK, axis=0)
    t_own = lax.dynamic_slice_in_dim(targets, group * BLK, BLK, axis=0).astype(F32)
    vec_own = jnp.where(flag == 0, vectors[0], vectors[1])
    live_own = lax.dynamic_slice_in_dim(live, group, 1)
    mask = (jnp.arange(BLK, dtype=jnp.int32)[:, None] < live_own[None, :]).astype(F32)
    gate = vec_own[2][None]
    base = x_own.astype(F32) - t_own
    miss_pol = base + gate * sums[:BLK]
    miss_ref = base + gate * sums[BLK:]
    excess = jnp.sum(mask * (miss_pol - miss_ref) * (miss_pol + miss_ref))
    grad_unit = 2.0 * mask * miss_pol
    dy_unit = (gate * grad_unit).astype(BF16)
    high = excess.astype(BF16)
    rest = excess - high.astype(F32)
    middle = rest.astype(BF16)
    lowest = (rest - middle.astype(F32)).astype(BF16)
    lane = lax.broadcasted_iota(jnp.int32, (BLK, LANES), 1)
    note = jnp.where(lane == 0, high, jnp.where(lane == 1, middle, lowest))
    shared = spread(jnp.concatenate([dy_unit, note], 1), "t", n_t)
    dy = shared[:, :, :width].reshape(CAP * BLK, width)
    excesses = jnp.sum(shared[:, 0, width : width + 3].astype(F32), axis=1)
    gap_first = jnp.sum(jnp.where(flags == 0, excesses, 0.0)) * scale_first
    gap_second = jnp.sum(jnp.where(flags == 1, excesses, 0.0)) * scale_second
    inside = -BETA * (gap_first - gap_second)
    losses = jax.nn.softplus(-inside)[None]
    weight = BETA * LOSS_SCALE * jax.nn.sigmoid(-inside)
    coef = jnp.where(flags == 0, weight * scale_first, -weight * scale_second)
    coef_rows = jnp.broadcast_to(coef[:, None], (CAP, BLK)).reshape(CAP * BLK, 1)
    coef_own = jnp.where(flag == 0, weight * scale_first, -weight * scale_second)

    dpre_own = (product(dy, down_own) * coef_rows * slope_own).astype(BF16)
    dpre_other = (product(dy, down_other) * coef_rows * slope_other).astype(BF16)
    dlow = (rows_by_rows(dpre_own, factor_own) + rows_by_rows(dpre_other, factor_other)).astype(BF16)
    dm_part = (
        rows_by_rows(dpre_own, up_own) + rows_by_rows(dpre_other, up_other) + rows_by_rows(dlow, factor_in)
    ).astype(BF16)
    grad_a = columns_by_columns(dlow, modded)
    b_own = columns_by_columns(low, dpre_own)
    b_other = columns_by_columns(low, dpre_other)
    rank = grad_a.shape[0]
    middle_column = width // n_c
    a_own = lax.dynamic_slice_in_dim(grad_a, core * middle_column, middle_column, axis=1)
    a_other = lax.dynamic_slice_in_dim(grad_a, (1 - core) * middle_column, middle_column, axis=1)
    given = lax.ppermute(jnp.concatenate([b_other, a_other], 0).astype(BF16), "c", SWAP)
    pile = (jnp.concatenate([b_own, a_own], 0) + given.astype(F32)).astype(BF16)

    chips = n_z * n_x
    pieces = lax.all_to_all(pile.reshape(chips, 2 * rank // chips, half), CHIPS, 0, 0, tiled=True)
    total = jnp.sum(pieces.astype(F32), axis=0) / n_dp
    place = lax.axis_index("z") * n_x + lax.axis_index("x")
    total = jnp.where(place < chips // 2, total, lax.psum(total, "t")).astype(BF16)
    mine = spread(total, CHIPS, chips).reshape(2 * rank, half)
    theirs = lax.ppermute(mine, "c", SWAP)
    ends = jnp.concatenate([mine, theirs], 1)
    flipped = jnp.concatenate([theirs, mine], 1)
    ends = jnp.where(core == 0, ends, flipped).astype(F32)
    sum_b = ends[:rank]
    sum_a = ends[rank:].T

    back = lax.all_to_all(dm_part.reshape(CAP, BLK, width), "t", 0, 0, tiled=True)
    back = jnp.sum(back.astype(F32), axis=0)
    normed_own, inverse_own = normalise(x_own)
    dn = back * (1.0 + vec_own[1][None])
    mean_one = jnp.mean(dn, axis=-1, keepdims=True)
    mean_two = jnp.mean(dn * normed_own, axis=-1, keepdims=True)
    grad_block = coef_own * grad_unit + inverse_own * (dn - mean_one - normed_own * mean_two)
    grad_tokens = spread(grad_block.astype(BF16), "t", n_t).reshape(CAP * BLK, width)
    return losses, grad_tokens, sum_a, sum_b


def solution(mesh):
    n_dp, n_t = mesh.devices.shape
    fine = Mesh(mesh.devices.reshape(n_dp // 8, 4, 2, n_t), ("z", "x", "c", "t"))
    return jax.shard_map(
        per_device,
        mesh=fine,
        in_specs=(
            P(DP, None),
            P(DP, None),
            P(DP, None, None),
            P(DP),
            P(DP),
            P(DP, None),
            P(DP, "t"),
            P(DP, "t"),
            P(),
            P(None, "t"),
        ),
        out_specs=(P(DP), P(DP, None), P(), P(None, "t")),
        check_vma=False,
    )
```

```python
import jax
import jax.numpy as jnp
from jax import lax
from jax.sharding import Mesh
from jax.sharding import PartitionSpec as P

BLK = 64
CAP = 4
EPS = 1e-06
BETA = 20.0
LOSS_SCALE = 4096.0
ROOT = 0.7978845608028654
CUBE = 0.044715
BF16 = jnp.bfloat16
F32 = jnp.float32
DP = ("z", "x", "c")
CHIPS = ("z", "x")
SWAP = [(0, 1), (1, 0)]


def gelu(pre):
    th = jnp.tanh(ROOT * (pre + CUBE * pre * pre * pre))
    return 0.5 * pre * (1.0 + th)


def gelu_and_slope(pre):
    square = pre * pre
    th = jnp.tanh(ROOT * (pre + CUBE * pre * square))
    half = 0.5 * (1.0 + th)
    slope = half + 0.5 * pre * (1.0 - th * th) * (ROOT * (1.0 + 3.0 * CUBE * square))
    return pre * half, slope


def rows_by_rows(left, right):
    return lax.dot_general(left, right, (((1,), (1,)), ((), ())), preferred_element_type=F32)


def columns_by_columns(left, right):
    return lax.dot_general(left, right, (((0,), (0,)), ((), ())), preferred_element_type=F32)


def product(left, right):
    return jnp.dot(left, right, preferred_element_type=F32)


def spread(value, axes, n):
    return lax.all_to_all(jnp.broadcast_to(value[None], (n, *value.shape)), axes, 0, 0, tiled=True)


def per_device(
    tokens,
    targets,
    modulation,
    live_block_count,
    preferred_blocks,
    last_block_rows,
    up_rows,
    down_rows,
    factor_in,
    factor_out,
):
    width = tokens.shape[1]
    n_z, n_x, n_c, n_t = (lax.axis_size(a) for a in ("z", "x", "c", "t"))
    n_dp = n_z * n_x * n_c
    core = lax.axis_index("c")
    group = lax.axis_index("t")
    thin, hidden = up_rows.shape
    half = hidden // n_c

    down_split = down_rows.reshape(thin, n_c, half).transpose(1, 0, 2)
    down_sent = jnp.broadcast_to(down_split[None], (n_x, n_c, thin, half)).reshape(n_x * n_c, thin, half)
    down_near = lax.all_to_all(down_sent, ("x", "c"), 0, 0, tiled=True)
    down_own = lax.all_gather(down_near.reshape(n_x * n_c * thin, half), "z", axis=0, tiled=True)

    up_rows, down_near = lax.optimization_barrier((up_rows, down_near))
    up_keep = lax.dynamic_slice_in_dim(up_rows, core * half, half, axis=1)
    up_give = lax.dynamic_slice_in_dim(up_rows, (1 - core) * half, half, axis=1)
    up_got = lax.ppermute(up_give, "c", SWAP)
    up_pair = jnp.where(
        core == 0, jnp.concatenate([up_keep, up_got], 0), jnp.concatenate([up_got, up_keep], 0)
    )
    up_line = lax.all_gather(up_pair, "z", axis=0, tiled=True)
    up_all = spread(up_line, "x", n_x).reshape(n_x, n_z, n_c * thin, half)
    up_own = up_all.transpose(1, 0, 2, 3).reshape(width, half)
    up_other = lax.ppermute(up_own, "c", SWAP)
    down_other = lax.ppermute(down_own, "c", SWAP)

    count = live_block_count[0]
    wins = preferred_blocks[0]
    slots = jnp.arange(CAP, dtype=jnp.int32)
    flags = (slots >= wins).astype(jnp.int32)
    last = jnp.where(flags == 0, wins - 1, count - 1)
    tail = jnp.where(flags == 0, last_block_rows[0, 0], last_block_rows[0, 1])
    live = jnp.where(slots < count, jnp.where(slots == last, tail, BLK), 0)
    rows_first = jnp.sum(jnp.where(flags == 0, live, 0)).astype(F32)
    rows_second = jnp.sum(jnp.where(flags == 1, live, 0)).astype(F32)
    scale_first = 1.0 / (width * rows_first)
    scale_second = 1.0 / (width * rows_second)

    vectors = modulation.astype(F32)
    pick = (flags == 0)[:, None, None]
    shift = jnp.where(pick, vectors[0, 0][None, None], vectors[1, 0][None, None])
    scale = 1.0 + jnp.where(pick, vectors[0, 1][None, None], vectors[1, 1][None, None])

    def normalise(rows):
        wide = rows.astype(F32)
        center = wide - jnp.mean(wide, axis=-1, keepdims=True)
        inverse = lax.rsqrt(jnp.mean(center * center, axis=-1, keepdims=True) + EPS)
        return center * inverse, inverse

    normed, _ = normalise(tokens.reshape(CAP, BLK, width))
    modded = (normed * scale + shift).astype(BF16).reshape(CAP * BLK, width)
    low = product(modded, factor_in).astype(BF16)

    factor_own = lax.dynamic_slice_in_dim(factor_out, core * half, half, axis=1)
    factor_other = lax.dynamic_slice_in_dim(factor_out, (1 - core) * half, half, axis=1)

    def activate(w_up, factor):
        pre_ref = product(modded, w_up)
        pre_pol = pre_ref + product(low, factor)
        act, slope = gelu_and_slope(pre_pol)
        return act.astype(BF16), gelu(pre_ref).astype(BF16), slope

    pol_own, ref_own, slope_own = activate(up_own, factor_own)
    pol_other, ref_other, slope_other = activate(up_other, factor_other)

    part_ref = (rows_by_rows(ref_own, down_own) + rows_by_rows(ref_other, down_other)).astype(BF16)
    part_ref, pol_other = lax.optimization_barrier((part_ref, pol_other))
    sum_ref = lax.psum_scatter(part_ref, "t", scatter_dimension=0, tiled=True).astype(F32)
    part_pol = (rows_by_rows(pol_own, down_own) + rows_by_rows(pol_other, down_other)).astype(BF16)
    sum_pol = lax.all_to_all(part_pol.reshape(CAP, BLK, width), "t", 0, 0, tiled=True)
    sum_pol = jnp.sum(sum_pol.astype(F32), axis=0)

    flag = (group >= wins).astype(jnp.int32)
    x_own = lax.dynamic_slice_in_dim(tokens, group * BLK, BLK, axis=0)
    t_own = lax.dynamic_slice_in_dim(targets, group * BLK, BLK, axis=0).astype(F32)
    vec_own = jnp.where(flag == 0, vectors[0], vectors[1])
    live_own = lax.dynamic_slice_in_dim(live, group, 1)
    mask = (jnp.arange(BLK, dtype=jnp.int32)[:, None] < live_own[None, :]).astype(F32)
    gate = vec_own[2][None]
    base = x_own.astype(F32) - t_own
    miss_pol = base + gate * sum_pol
    grad_unit = 2.0 * mask * miss_pol
    dy = spread((gate * grad_unit).astype(BF16), "t", n_t).reshape(CAP * BLK, width)

    dpre_own = (product(dy, down_own) * slope_own).astype(BF16)
    dpre_other = (product(dy, down_other) * slope_other).astype(BF16)
    dlow_part = (rows_by_rows(factor_own, dpre_own) + rows_by_rows(factor_other, dpre_other)).astype(BF16)
    rank = dlow_part.shape[0]

    miss_ref = base + gate * sum_ref
    excess = jnp.sum(mask * (miss_pol - miss_ref) * (miss_pol + miss_ref))
    high = excess.astype(BF16)
    rest = excess - high.astype(F32)
    middle = rest.astype(BF16)
    lowest = (rest - middle.astype(F32)).astype(BF16)
    lane = lax.broadcasted_iota(jnp.int32, (16, CAP * BLK), 1)
    note = jnp.where(lane == 0, high, jnp.where(lane == 1, middle, lowest))
    shared = spread(jnp.concatenate([dlow_part, note], 0), "t", n_t)

    dm_part = (
        rows_by_rows(dpre_own, up_own)
        + rows_by_rows(dpre_other, up_other)
        + lax.dot_general(dlow_part, factor_in, (((0,), (1,)), ((), ())), preferred_element_type=F32)
    ).astype(BF16)
    dm_sum = lax.psum_scatter(dm_part, "t", scatter_dimension=0, tiled=True).astype(F32)

    row_flags = jnp.broadcast_to(flags[:, None], (CAP, BLK)).reshape(CAP * BLK, 1)
    low_split = jnp.concatenate(
        [jnp.where(row_flags == 0, low, jnp.zeros_like(low)), jnp.where(row_flags == 1, low, jnp.zeros_like(low))], 1
    )
    b_own = columns_by_columns(low_split, dpre_own)
    b_other = columns_by_columns(low_split, dpre_other)

    excesses = jnp.sum(shared[:, rank, :3].astype(F32), axis=1)
    gap_first = jnp.sum(jnp.where(flags == 0, excesses, 0.0)) * scale_first
    gap_second = jnp.sum(jnp.where(flags == 1, excesses, 0.0)) * scale_second
    inside = -BETA * (gap_first - gap_second)
    losses = jax.nn.softplus(-inside)[None]
    weight = BETA * LOSS_SCALE * jax.nn.sigmoid(-inside)
    coef_first = weight * scale_first
    coef_second = -weight * scale_second
    coef_rows = jnp.where(row_flags.reshape(1, CAP * BLK) == 0, coef_first, coef_second)
    coef_own = jnp.where(flag == 0, coef_first, coef_second)

    dlow = (jnp.sum(shared[:, :rank].astype(F32), axis=0) * coef_rows).astype(BF16)
    grad_a = product(dlow, modded)
    middle_column = width // n_c
    a_own = lax.dynamic_slice_in_dim(grad_a, core * middle_column, middle_column, axis=1)
    a_other = lax.dynamic_slice_in_dim(grad_a, (1 - core) * middle_column, middle_column, axis=1)
    b_own = coef_first * b_own[:rank] + coef_second * b_own[rank:]
    b_other = coef_first * b_other[:rank] + coef_second * b_other[rank:]
    given = lax.ppermute(jnp.concatenate([b_other, a_other], 0).astype(BF16), "c", SWAP)
    pile = (jnp.concatenate([b_own, a_own], 0) + given.astype(F32)).astype(BF16)

    chips = n_z * n_x
    pieces = lax.all_to_all(pile.reshape(chips, 2 * rank // chips, half), CHIPS, 0, 0, tiled=True)
    total = (jnp.sum(pieces.astype(F32), axis=0) / n_dp).astype(BF16)
    mine = spread(total, CHIPS, chips).reshape(2 * rank, half)
    theirs = lax.ppermute(mine, "c", SWAP)
    ends = jnp.concatenate([mine, theirs], 1)
    flipped = jnp.concatenate([theirs, mine], 1)
    ends = jnp.where(core == 0, ends, flipped).astype(F32)
    sum_b = ends[:rank]
    sum_a = ends[rank:].T

    normed_own, inverse_own = normalise(x_own)
    dn = dm_sum * (1.0 + vec_own[1][None])
    mean_one = jnp.mean(dn, axis=-1, keepdims=True)
    mean_two = jnp.mean(dn * normed_own, axis=-1, keepdims=True)
    grad_block = coef_own * (grad_unit + inverse_own * (dn - mean_one - normed_own * mean_two))
    grad_block = grad_block.astype(BF16)
    blocks = [grad_block]
    for step in range(1, n_t):
        blocks.append(lax.ppermute(grad_block, "t", [(i, (i + step) % n_t) for i in range(n_t)]))
    blocks = jnp.stack(blocks)
    grad_tokens = jnp.concatenate(
        [lax.dynamic_index_in_dim(blocks, (group - slot) % n_t, 0, False) for slot in range(n_t)], 0
    )
    return losses, grad_tokens, sum_a, sum_b


def solution(mesh):
    n_dp, n_t = mesh.devices.shape
    fine = Mesh(mesh.devices.reshape(n_dp // 8, 4, 2, n_t), ("z", "x", "c", "t"))
    return jax.shard_map(
        per_device,
        mesh=fine,
        in_specs=(
            P(DP, None),
            P(DP, None),
            P(DP, None, None),
            P(DP),
            P(DP),
            P(DP, None),
            P(DP, "t"),
            P(DP, "t"),
            P(),
            P(None, "t"),
        ),
        out_specs=(P(DP), P(DP, None), P(), P(None, "t")),
        check_vma=False,
    )
```

```python
import jax
import jax.numpy as jnp
from jax import lax
from jax.experimental import pallas as pl
from jax.experimental.pallas import tpu as pltpu
from jax.sharding import Mesh
from jax.sharding import PartitionSpec as P

BLK = 64
CAP = 4
EPS = 1e-06
BETA = 20.0
LOSS_SCALE = 4096.0
ROOT = 0.7978845608028654
CUBE = 0.044715
BF16 = jnp.bfloat16
F32 = jnp.float32
DP = ("z", "x", "c")
CHIPS = ("z", "x")
SWAP = [(0, 1), (1, 0)]
EARLY = 16
NOTE = 16
VMEM_LIMIT = 40 * 1024 * 1024
SMEM = pltpu.SMEM


def gelu(pre):
    th = jnp.tanh(ROOT * (pre + CUBE * pre * pre * pre))
    return 0.5 * pre * (1.0 + th)


def gelu_and_slope(pre):
    square = pre * pre
    th = jnp.tanh(ROOT * (pre + CUBE * pre * square))
    half = 0.5 * (1.0 + th)
    slope = half + 0.5 * pre * (1.0 - th * th) * (ROOT * (1.0 + 3.0 * CUBE * square))
    return pre * half, slope


def rows_by_rows(left, right):
    return lax.dot_general(left, right, (((1,), (1,)), ((), ())), preferred_element_type=F32)


def product(left, right):
    return jnp.dot(left, right, preferred_element_type=F32)


def spread(value, axes, n):
    return lax.all_to_all(jnp.broadcast_to(value[None], (n, *value.shape)), axes, 0, 0, tiled=True)


def normalise(rows):
    wide = rows.astype(F32)
    center = wide - jnp.mean(wide, axis=-1, keepdims=True)
    inverse = lax.rsqrt(jnp.mean(center * center, axis=-1, keepdims=True) + EPS)
    return center * inverse, inverse


def params():
    return pltpu.CompilerParams(vmem_limit_bytes=VMEM_LIMIT)


def cost(flops, moved, tanh=0):
    return pl.CostEstimate(flops=flops, bytes_accessed=moved, transcendentals=tanh)


def whole(shape):
    return pl.BlockSpec(shape, lambda *_: (0,) * len(shape))


def input_kernel(wins_ref, x_ref, mod_ref, a_ref, modded_ref, low_ref, split_ref):
    wins = wins_ref[0]
    for slot in range(CAP):
        rows = slice(slot * BLK, (slot + 1) * BLK)
        normed, _ = normalise(x_ref[rows])
        first = slot < wins
        shift = jnp.where(first, mod_ref[0:1].astype(F32), mod_ref[3:4].astype(F32))
        scale = 1.0 + jnp.where(first, mod_ref[1:2].astype(F32), mod_ref[4:5].astype(F32))
        modded_ref[rows] = (normed * scale + shift).astype(BF16)
    modded = modded_ref[...]
    low_ref[...] = rows_by_rows(modded, a_ref[...]).astype(BF16)
    turned = rows_by_rows(a_ref[...], modded)
    second = lax.broadcasted_iota(jnp.int32, turned.shape, 1) // BLK >= wins
    rank = turned.shape[0]
    split_ref[:rank] = jnp.where(second, 0.0, turned).astype(BF16)
    split_ref[rank:] = jnp.where(second, turned, 0.0).astype(BF16)


def prepare(wins, tokens, mod, a_turned):
    rows, width = tokens.shape
    rank = a_turned.shape[0]
    return pl.pallas_call(
        input_kernel,
        out_shape=[
            jax.ShapeDtypeStruct((rows, width), BF16),
            jax.ShapeDtypeStruct((rows, rank), BF16),
            jax.ShapeDtypeStruct((2 * rank, rows), BF16),
        ],
        in_specs=[pl.BlockSpec(memory_space=SMEM)] + [pl.BlockSpec(memory_space=pltpu.VMEM)] * 3,
        compiler_params=params(),
        cost_estimate=cost(4 * rows * width * rank, 4 * rows * width),
    )(wins, tokens, mod, a_turned)


def up_kernel(modded_ref, low_ref, up_ref, b_ref, pol_ref, ref_ref, slope_ref):
    pre_ref = product(modded_ref[...], up_ref[...])
    pre_pol = pre_ref + product(low_ref[...], b_ref[...])
    act, slope = gelu_and_slope(pre_pol)
    pol_ref[...] = act.astype(BF16)
    slope_ref[...] = slope
    ref_ref[...] = gelu(pre_ref).astype(BF16)


def activate(modded, low, up, factor):
    rows, width = modded.shape
    rank, half = factor.shape
    step = 256
    cut = pl.BlockSpec((rows, step), lambda i: (0, i))
    return pl.pallas_call(
        up_kernel,
        grid=(half // step,),
        out_shape=[
            jax.ShapeDtypeStruct((rows, half), BF16),
            jax.ShapeDtypeStruct((rows, half), BF16),
            jax.ShapeDtypeStruct((rows, half), F32),
        ],
        in_specs=[
            whole((rows, width)),
            whole((rows, rank)),
            pl.BlockSpec((width, step), lambda i: (0, i)),
            pl.BlockSpec((rank, step), lambda i: (0, i)),
        ],
        out_specs=[cut, cut, cut],
        compiler_params=params(),
        cost_estimate=cost(2 * rows * width * half, 2 * width * half + 10 * rows * half, 2 * rows * half),
    )(modded, low, up, factor)


def down_kernel(left_ref, right_ref, own_ref, other_ref, out_ref):
    total = rows_by_rows(left_ref[...], own_ref[...]) + rows_by_rows(right_ref[...], other_ref[...])
    out_ref[...] = total.astype(BF16)


def lower(left, right, own, other):
    rows, half = left.shape
    width = own.shape[0]
    step = 512
    cut = pl.BlockSpec((step, half), lambda i: (i, 0))
    return pl.pallas_call(
        down_kernel,
        grid=(width // step,),
        out_shape=jax.ShapeDtypeStruct((rows, width), BF16),
        in_specs=[whole((rows, half)), whole((rows, half)), cut, cut],
        out_specs=pl.BlockSpec((rows, step), lambda i: (0, i)),
        compiler_params=params(),
        cost_estimate=cost(4 * rows * width * half, 4 * width * half + 2 * rows * width),
    )(left, right, own, other)


def miss_kernel(got_ref, ref_ref, x_ref, t_ref, gate_ref, mask_ref, unit_ref, send_ref):
    total = jnp.sum(got_ref[...].astype(F32), axis=0)
    gate = gate_ref[...]
    unit = 2.0 * mask_ref[...] * (x_ref[...].astype(F32) - t_ref[...].astype(F32) + gate * total)
    unit_ref[...] = unit
    dy = (gate * unit).astype(BF16)
    for peer in range(send_ref.shape[0]):
        send_ref[peer, :BLK] = dy
        send_ref[peer, BLK:] = ref_ref[peer]


def miss(got, part_ref, x_own, t_own, gate, mask):
    groups, rows, width = got.shape
    return pl.pallas_call(
        miss_kernel,
        out_shape=[
            jax.ShapeDtypeStruct((rows, width), F32),
            jax.ShapeDtypeStruct((groups, 2 * rows, width), BF16),
        ],
        compiler_params=params(),
        cost_estimate=cost(20 * rows * width, 8 * groups * rows * width),
    )(got, part_ref, x_own, t_own, gate, mask)


def back_kernel(
    got_ref, unit_ref, x_ref, t_ref, gate_ref, mask_ref, own_ref, other_ref, bo_ref, bt_ref, so_ref, st_ref,
    do_ref, dt_ref, dlow_ref, send_ref, turned_scr, straight_scr,
):
    step = pl.program_id(0)
    width = got_ref.shape[2]
    dy = got_ref[:, :BLK].reshape(CAP * BLK, width)
    d_own = (product(dy, own_ref[...]) * so_ref[...]).astype(BF16)
    d_other = (product(dy, other_ref[...]) * st_ref[...]).astype(BF16)
    do_ref[...] = d_own
    dt_ref[...] = d_other
    turned = rows_by_rows(bo_ref[...], d_own) + rows_by_rows(bt_ref[...], d_other)
    straight = rows_by_rows(d_own, bo_ref[...]) + rows_by_rows(d_other, bt_ref[...])

    @pl.when(step == 0)
    def _():
        turned_scr[...] = turned
        straight_scr[...] = straight

    @pl.when(step > 0)
    def _():
        turned_scr[...] += turned
        straight_scr[...] += straight

    @pl.when(step == pl.num_programs(0) - 1)
    def _():
        rank = turned_scr.shape[0]
        dlow_ref[...] = straight_scr[...].astype(BF16)
        mask = mask_ref[...]
        base = x_ref[...].astype(F32) - t_ref[...].astype(F32)
        miss_ref = mask * (base + gate_ref[...] * jnp.sum(got_ref[:, BLK:].astype(F32), axis=0))
        miss_pol = 0.5 * unit_ref[...]
        parts = jnp.sum((miss_pol - miss_ref) * (miss_pol + miss_ref), axis=1, keepdims=True)
        excess = jnp.broadcast_to(jnp.sum(parts, axis=0, keepdims=True), (NOTE, CAP * BLK))
        high = excess.astype(BF16)
        rest = excess - high.astype(F32)
        middle = rest.astype(BF16)
        lowest = rest - middle.astype(F32)
        line = lax.broadcasted_iota(jnp.int32, excess.shape, 0)
        note = jnp.where(line == 0, high.astype(F32), jnp.where(line == 1, middle.astype(F32), lowest)).astype(BF16)
        total = turned_scr[...].astype(BF16)
        for peer in range(send_ref.shape[0]):
            send_ref[peer, :rank] = total
            send_ref[peer, rank:] = note


def backward(got, unit, x_own, t_own, gate, mask, own, other, b_own, b_other, s_own, s_other):
    groups, _, width = got.shape
    half = own.shape[1]
    rank = b_own.shape[0]
    rows = CAP * BLK
    step = 256
    weight = pl.BlockSpec((width, step), lambda i: (0, i))
    factor = pl.BlockSpec((rank, step), lambda i: (0, i))
    cut = pl.BlockSpec((rows, step), lambda i: (0, i))
    block = whole((BLK, width))
    return pl.pallas_call(
        back_kernel,
        grid=(half // step,),
        out_shape=[
            jax.ShapeDtypeStruct((rows, half), BF16),
            jax.ShapeDtypeStruct((rows, half), BF16),
            jax.ShapeDtypeStruct((rows, rank), BF16),
            jax.ShapeDtypeStruct((groups, rank + NOTE, rows), BF16),
        ],
        in_specs=[
            whole(got.shape), block, block, block, whole((1, width)), whole((BLK, 1)),
            weight, weight, factor, factor, cut, cut,
        ],
        out_specs=[cut, cut, whole((rows, rank)), whole((groups, rank + NOTE, rows))],
        scratch_shapes=[pltpu.VMEM((rank, rows), F32), pltpu.VMEM((rows, rank), F32)],
        compiler_params=params(),
        cost_estimate=cost(4 * rows * width * half, 4 * width * half + 12 * rows * half),
    )(got, unit, x_own, t_own, gate, mask, own, other, b_own, b_other, s_own, s_other)


def factor_kernel(split_ref, do_ref, dt_ref, own_ref, other_ref):
    own_ref[...] = product(split_ref[...], do_ref[...])
    other_ref[...] = product(split_ref[...], dt_ref[...])


def factor_terms(split, d_own, d_other):
    lines, rows = split.shape
    half = d_own.shape[1]
    return pl.pallas_call(
        factor_kernel,
        out_shape=[jax.ShapeDtypeStruct((lines, half), F32)] * 2,
        compiler_params=params(),
        cost_estimate=cost(4 * lines * rows * half, 8 * lines * half),
    )(split, d_own, d_other)


def pile_kernel(
    ints_ref, scales_ref, got_ref, modded_ref, own_ref, other_ref, keep_ref, give_ref, facts_ref
):
    wins = ints_ref[0]
    core = ints_ref[1]
    groups, lines, rows = got_ref.shape
    rank = lines - NOTE
    half = own_ref.shape[1]
    gap_first = jnp.zeros((1, rows), F32)
    gap_second = jnp.zeros((1, rows), F32)
    for slot in range(groups):
        note = got_ref[slot, rank:].astype(F32)
        excess = note[0:1] + note[1:2] + note[2:3]
        gap_first += jnp.where(slot < wins, excess, 0.0)
        gap_second += jnp.where(slot < wins, 0.0, excess)
    scale_first = scales_ref[0]
    scale_second = scales_ref[1]
    inside = -BETA * (gap_first * scale_first - gap_second * scale_second)
    losses = jnp.maximum(-inside, 0.0) + jnp.log1p(jnp.exp(-jnp.abs(inside)))
    weight = BETA * LOSS_SCALE * jax.nn.sigmoid(-inside)
    first = weight * scale_first
    second = -weight * scale_second
    line = lax.broadcasted_iota(jnp.int32, facts_ref.shape, 0)
    facts_ref[...] = jnp.where(line == 0, losses, jnp.where(line == 1, first, second))
    slot = lax.broadcasted_iota(jnp.int32, (1, rows), 1) // BLK
    total = jnp.sum(got_ref[:, :rank].astype(F32), axis=0)
    dlow = (total * jnp.where(slot < wins, first, second)).astype(BF16)
    one = first[:, :1]
    two = second[:, :1]
    near = modded_ref[:, pl.ds(pl.multiple_of(core * half, 128), half)]
    far = modded_ref[:, pl.ds(pl.multiple_of((1 - core) * half, 128), half)]
    keep_ref[:rank] = one * own_ref[:rank] + two * own_ref[rank:]
    keep_ref[rank:] = product(dlow, near)
    give_ref[:rank] = (one * other_ref[:rank] + two * other_ref[rank:]).astype(BF16)
    give_ref[rank:] = product(dlow, far).astype(BF16)


def piles(ints, scales, got, modded, b_own, b_other):
    lines, half = b_own.shape
    rows = got.shape[2]
    return pl.pallas_call(
        pile_kernel,
        out_shape=[
            jax.ShapeDtypeStruct((lines, half), F32),
            jax.ShapeDtypeStruct((lines, half), BF16),
            jax.ShapeDtypeStruct((8, rows), F32),
        ],
        in_specs=[pl.BlockSpec(memory_space=SMEM)] * 2 + [pl.BlockSpec(memory_space=pltpu.VMEM)] * 4,
        compiler_params=params(),
        cost_estimate=cost(2 * lines * half * rows, 16 * lines * half),
    )(ints, scales, got, modded, b_own, b_other)


def dm_kernel(after_ref, do_ref, dt_ref, dlow_ref, own_ref, other_ref, a_ref, out_ref):
    total = rows_by_rows(do_ref[...], own_ref[...]) + rows_by_rows(dt_ref[...], other_ref[...])
    out_ref[...] = (total + product(dlow_ref[...], a_ref[...])).astype(BF16)


def dm_terms(after, d_own, d_other, dlow, own, other, a_turned):
    rows, half = d_own.shape
    width = own.shape[0]
    rank = dlow.shape[1]
    step = 512
    cut = pl.BlockSpec((step, half), lambda i: (i, 0))
    return pl.pallas_call(
        dm_kernel,
        grid=(width // step,),
        out_shape=jax.ShapeDtypeStruct((rows, width), BF16),
        in_specs=[
            pl.BlockSpec(memory_space=pl.ANY),
            whole((rows, half)),
            whole((rows, half)),
            whole((rows, rank)),
            cut,
            cut,
            pl.BlockSpec((rank, step), lambda i: (0, i)),
        ],
        out_specs=pl.BlockSpec((rows, step), lambda i: (0, i)),
        compiler_params=params(),
        cost_estimate=cost(4 * rows * width * half, 4 * width * half + 2 * rows * width),
    )(after, d_own, d_other, dlow, own, other, a_turned)


def token_kernel(one_ref, two_ref, three_ref, four_ref, x_ref, scale_ref, unit_ref, coef_ref, out_ref):
    total = one_ref[...].astype(F32) + two_ref[...].astype(F32)
    total = total + three_ref[...].astype(F32) + four_ref[...].astype(F32)
    normed, inverse = normalise(x_ref[...])
    dn = total * scale_ref[...]
    mean_one = jnp.mean(dn, axis=-1, keepdims=True)
    mean_two = jnp.mean(dn * normed, axis=-1, keepdims=True)
    grad = coef_ref[...] * (unit_ref[...] + inverse * (dn - mean_one - normed * mean_two))
    out_ref[...] = grad.astype(BF16)


def token_gradient(pieces, x_own, scale, unit, coef):
    rows, width = x_own.shape
    return pl.pallas_call(
        token_kernel,
        out_shape=jax.ShapeDtypeStruct((rows, width), BF16),
        compiler_params=params(),
        cost_estimate=cost(20 * rows * width, 20 * rows * width),
    )(*pieces, x_own, scale, unit, coef)


def per_device(
    tokens,
    targets,
    modulation,
    live_block_count,
    preferred_blocks,
    last_block_rows,
    up_rows,
    down_rows,
    factor_in,
    factor_out,
):
    width = tokens.shape[1]
    n_z, n_x, n_c, n_t = (lax.axis_size(a) for a in ("z", "x", "c", "t"))
    n_dp = n_z * n_x * n_c
    core = lax.axis_index("c")
    group = lax.axis_index("t")
    thin, hidden = up_rows.shape
    half = hidden // n_c
    pair = n_c * thin
    rank = factor_in.shape[1]

    both = jnp.concatenate([up_rows, down_rows], axis=0)
    keep = lax.dynamic_slice_in_dim(both, core * half, half, axis=1)
    got = lax.ppermute(lax.dynamic_slice_in_dim(both, (1 - core) * half, half, axis=1), "c", SWAP)
    first = jnp.where(core == 0, keep, got)
    second = jnp.where(core == 0, got, keep)
    up_pair = jnp.concatenate([first[:thin], second[:thin]], axis=0)
    down_pair = jnp.concatenate([first[thin:], second[thin:]], axis=0)
    line_one = lax.all_gather(jnp.concatenate([up_pair, down_pair[:EARLY]], 0), "z", axis=0, tiled=True)
    down_late, line_one = lax.optimization_barrier((down_pair[EARLY:], line_one))
    line_two = lax.all_gather(down_late, "z", axis=0, tiled=True)
    near_one = spread(line_one, "x", n_x).reshape(n_x, n_z, pair + EARLY, half).transpose(1, 0, 2, 3)
    near_two = spread(line_two, "x", n_x).reshape(n_x, n_z, pair - EARLY, half).transpose(1, 0, 2, 3)
    up_own = near_one[:, :, :pair].reshape(width, half)
    up_other = lax.ppermute(up_own, "c", SWAP)
    down_own = jnp.concatenate([near_one[:, :, pair:], near_two], axis=2).reshape(width, half)
    down_other = lax.ppermute(down_own, "c", SWAP)

    count = live_block_count[0]
    wins = preferred_blocks[0]
    slots = jnp.arange(CAP, dtype=jnp.int32)
    flags = (slots >= wins).astype(jnp.int32)
    last = jnp.where(flags == 0, wins - 1, count - 1)
    tail = jnp.where(flags == 0, last_block_rows[0, 0], last_block_rows[0, 1])
    live = jnp.where(slots < count, jnp.where(slots == last, tail, BLK), 0)
    rows_first = jnp.sum(jnp.where(flags == 0, live, 0)).astype(F32)
    rows_second = jnp.sum(jnp.where(flags == 1, live, 0)).astype(F32)
    scales = 1.0 / (width * jnp.stack([rows_first, rows_second]))

    own_first = group < wins
    x_own = lax.dynamic_slice_in_dim(tokens, group * BLK, BLK, axis=0)
    t_own = lax.dynamic_slice_in_dim(targets, group * BLK, BLK, axis=0)
    vec_own = jnp.where(own_first, modulation[0], modulation[1]).astype(F32)
    live_own = lax.dynamic_slice_in_dim(live, group, 1)
    mask = (jnp.arange(BLK, dtype=jnp.int32)[:, None] < live_own[None, :]).astype(F32)
    gate = vec_own[2:3]
    scale_own = 1.0 + vec_own[1:2]

    a_turned = factor_in.T
    factor_own = lax.dynamic_slice_in_dim(factor_out, core * half, half, axis=1)
    factor_other = lax.dynamic_slice_in_dim(factor_out, (1 - core) * half, half, axis=1)
    modded, low, low_split = prepare(preferred_blocks, tokens, modulation.reshape(6, width), a_turned)

    pol_own, ref_own, slope_own = activate(modded, low, up_own, factor_own)
    pol_other, ref_other, slope_other = activate(modded, low, up_other, factor_other)
    part_pol = lower(pol_own, pol_other, down_own, down_other).reshape(CAP, BLK, width)
    got_pol = lax.all_to_all(part_pol, "t", 0, 0, tiled=True)
    part_ref = lower(ref_own, ref_other, down_own, down_other).reshape(CAP, BLK, width)

    unit, send = miss(got_pol, part_ref, x_own, t_own, gate, mask)
    got_dy = lax.all_to_all(send, "t", 0, 0, tiled=True)
    d_own, d_other, dlow_part, send = backward(
        got_dy, unit, x_own, t_own, gate, mask, down_own, down_other, factor_own, factor_other, slope_own, slope_other
    )
    got_low = lax.all_to_all(send, "t", 0, 0, tiled=True)
    b_own, b_other = factor_terms(low_split, d_own, d_other)
    keep, give, facts = piles(
        jnp.stack([wins, core]).astype(jnp.int32), scales, got_low, modded, b_own, b_other
    )
    losses = facts[0, :1]
    coef_own = jnp.where(own_first, facts[1:2, :1], facts[2:3, :1])
    pile = (keep + lax.ppermute(give, "c", SWAP).astype(F32)).astype(BF16)

    chips = n_z * n_x
    pieces = lax.all_to_all(pile.reshape(chips, 2 * rank // chips, half), CHIPS, 0, 0, tiled=True)
    total = (jnp.sum(pieces.astype(F32), axis=0) / n_dp).astype(BF16)
    mine = spread(total, CHIPS, chips).reshape(2 * rank, half)
    theirs = lax.ppermute(mine, "c", SWAP)
    ends = jnp.concatenate([mine, theirs], 1)
    flipped = jnp.concatenate([theirs, mine], 1)
    ends = jnp.where(core == 0, ends, flipped).astype(F32)
    sum_b = ends[:rank]
    sum_a = ends[rank:].T

    dm_part = dm_terms(pile, d_own, d_other, dlow_part, up_own, up_other, a_turned).reshape(CAP, BLK, width)
    turns = [[(i, (i + step) % n_t) for i in range(n_t)] for step in range(n_t)]
    chunks = [lax.dynamic_index_in_dim(dm_part, (group + step) % n_t, 0, False) for step in range(n_t)]
    chunks = [chunks[0]] + [lax.ppermute(chunks[step], "t", turns[step]) for step in range(1, n_t)]
    grad_block = token_gradient(chunks, x_own, scale_own, unit, coef_own)
    blocks = [grad_block] + [lax.ppermute(grad_block, "t", turns[step]) for step in range(1, n_t)]
    blocks = jnp.stack(blocks)
    grad_tokens = jnp.concatenate(
        [lax.dynamic_index_in_dim(blocks, (group - slot) % n_t, 0, False) for slot in range(n_t)], 0
    )
    return losses, grad_tokens, sum_a, sum_b


def solution(mesh):
    n_dp, n_t = mesh.devices.shape
    fine = Mesh(mesh.devices.reshape(n_dp // 8, 4, 2, n_t), ("z", "x", "c", "t"))
    return jax.shard_map(
        per_device,
        mesh=fine,
        in_specs=(
            P(DP, None),
            P(DP, None),
            P(DP, None, None),
            P(DP),
            P(DP),
            P(DP, None),
            P(DP, "t"),
            P(DP, "t"),
            P(),
            P(None, "t"),
        ),
        out_specs=(P(DP), P(DP, None), P(), P(None, "t")),
        check_vma=False,
    )
```

```python
import jax
import jax.numpy as jnp
from jax import lax
from jax.experimental import pallas as pl
from jax.experimental.pallas import tpu as pltpu
from jax.sharding import Mesh
from jax.sharding import PartitionSpec as P

BLK = 64
CAP = 4
EPS = 1e-06
BETA = 20.0
LOSS_SCALE = 4096.0
ROOT = 0.7978845608028654
CUBE = 0.044715
BF16 = jnp.bfloat16
F32 = jnp.float32
DP = ("z", "x", "c")
CHIPS = ("z", "x")
SWAP = [(0, 1), (1, 0)]
LATE = 8
NOTE = 16
VMEM_LIMIT = 56 * 1024 * 1024
SMEM = pltpu.SMEM


def gelu(pre):
    th = jnp.tanh(ROOT * (pre + CUBE * pre * pre * pre))
    return 0.5 * pre * (1.0 + th)


def gelu_and_slope(pre):
    square = pre * pre
    th = jnp.tanh(ROOT * (pre + CUBE * pre * square))
    half = 0.5 * (1.0 + th)
    slope = half + 0.5 * pre * (1.0 - th * th) * (ROOT * (1.0 + 3.0 * CUBE * square))
    return pre * half, slope


def rows_by_rows(left, right):
    return lax.dot_general(left, right, (((1,), (1,)), ((), ())), preferred_element_type=F32)


def product(left, right):
    return jnp.dot(left, right, preferred_element_type=F32)


def spread(value, axes, n):
    return lax.all_to_all(jnp.broadcast_to(value[None], (n, *value.shape)), axes, 0, 0, tiled=True)


def normalise(rows):
    wide = rows.astype(F32)
    center = wide - jnp.mean(wide, axis=-1, keepdims=True)
    inverse = lax.rsqrt(jnp.mean(center * center, axis=-1, keepdims=True) + EPS)
    return center * inverse, inverse


def params():
    return pltpu.CompilerParams(vmem_limit_bytes=VMEM_LIMIT)


def cost(flops, moved, tanh=0):
    return pl.CostEstimate(flops=flops, bytes_accessed=moved, transcendentals=tanh)


def whole(shape):
    return pl.BlockSpec(shape, lambda *_: (0,) * len(shape))


def input_kernel(wins_ref, x_ref, mod_ref, a_ref, modded_ref, low_ref, split_ref):
    wins = wins_ref[0]
    for slot in range(CAP):
        rows = slice(slot * BLK, (slot + 1) * BLK)
        normed, _ = normalise(x_ref[rows])
        first = slot < wins
        shift = jnp.where(first, mod_ref[0:1].astype(F32), mod_ref[3:4].astype(F32))
        scale = 1.0 + jnp.where(first, mod_ref[1:2].astype(F32), mod_ref[4:5].astype(F32))
        modded_ref[rows] = (normed * scale + shift).astype(BF16)
    modded = modded_ref[...]
    low_ref[...] = rows_by_rows(modded, a_ref[...]).astype(BF16)
    turned = rows_by_rows(a_ref[...], modded)
    second = lax.broadcasted_iota(jnp.int32, turned.shape, 1) // BLK >= wins
    rank = turned.shape[0]
    split_ref[:rank] = jnp.where(second, 0.0, turned).astype(BF16)
    split_ref[rank:] = jnp.where(second, turned, 0.0).astype(BF16)


def prepare(wins, tokens, mod, a_turned):
    rows, width = tokens.shape
    rank = a_turned.shape[0]
    return pl.pallas_call(
        input_kernel,
        out_shape=[
            jax.ShapeDtypeStruct((rows, width), BF16),
            jax.ShapeDtypeStruct((rows, rank), BF16),
            jax.ShapeDtypeStruct((2 * rank, rows), BF16),
        ],
        in_specs=[pl.BlockSpec(memory_space=SMEM)] + [pl.BlockSpec(memory_space=pltpu.VMEM)] * 3,
        compiler_params=params(),
        cost_estimate=cost(4 * rows * width * rank, 4 * rows * width),
    )(wins, tokens, mod, a_turned)


def after_kernel(*refs):
    refs[-1][...] = refs[0][...]


def after(value, others):
    return pl.pallas_call(
        after_kernel,
        out_shape=jax.ShapeDtypeStruct(value.shape, value.dtype),
        in_specs=[pl.BlockSpec(memory_space=pltpu.VMEM)] + [pl.BlockSpec(memory_space=pl.ANY)] * len(others),
        compiler_params=params(),
        cost_estimate=cost(0, 4 * value.size),
    )(value, *others)


def up_kernel(modded_ref, low_ref, up_ref, b_ref, pol_ref, ref_ref, slope_ref):
    pre_ref = product(modded_ref[...], up_ref[...])
    pre_pol = pre_ref + product(low_ref[...], b_ref[...])
    act, slope = gelu_and_slope(pre_pol)
    pol_ref[...] = act.astype(BF16)
    slope_ref[...] = slope
    ref_ref[...] = gelu(pre_ref).astype(BF16)


def activate(modded, low, up, factor):
    rows, width = modded.shape
    rank, half = factor.shape
    step = 256
    cut = pl.BlockSpec((rows, step), lambda i: (0, i))
    return pl.pallas_call(
        up_kernel,
        grid=(half // step,),
        out_shape=[
            jax.ShapeDtypeStruct((rows, half), BF16),
            jax.ShapeDtypeStruct((rows, half), BF16),
            jax.ShapeDtypeStruct((rows, half), F32),
        ],
        in_specs=[
            whole((rows, width)),
            whole((rows, rank)),
            pl.BlockSpec((width, step), lambda i: (0, i)),
            pl.BlockSpec((rank, step), lambda i: (0, i)),
        ],
        out_specs=[cut, cut, cut],
        compiler_params=params(),
        cost_estimate=cost(2 * rows * width * half, 2 * width * half + 10 * rows * half, 2 * rows * half),
    )(modded, low, up, factor)


def down_kernel(left_ref, right_ref, own_ref, other_ref, out_ref):
    total = rows_by_rows(left_ref[...], own_ref[...]) + rows_by_rows(right_ref[...], other_ref[...])
    out_ref[...] = total.astype(BF16)


def lower(left, right, own, other):
    rows, half = left.shape
    width = own.shape[0]
    step = 512
    cut = pl.BlockSpec((step, half), lambda i: (i, 0))
    return pl.pallas_call(
        down_kernel,
        grid=(width // step,),
        out_shape=jax.ShapeDtypeStruct((rows, width), BF16),
        in_specs=[whole((rows, half)), whole((rows, half)), cut, cut],
        out_specs=pl.BlockSpec((rows, step), lambda i: (0, i)),
        compiler_params=params(),
        cost_estimate=cost(4 * rows * width * half, 4 * width * half + 2 * rows * width),
    )(left, right, own, other)


def miss_kernel(got_ref, ref_ref, x_ref, t_ref, gate_ref, mask_ref, unit_ref, send_ref):
    total = jnp.sum(got_ref[...].astype(F32), axis=0)
    gate = gate_ref[...]
    unit = 2.0 * mask_ref[...] * (x_ref[...].astype(F32) - t_ref[...].astype(F32) + gate * total)
    unit_ref[...] = unit
    dy = (gate * unit).astype(BF16)
    for peer in range(send_ref.shape[0]):
        send_ref[peer, :BLK] = dy
        send_ref[peer, BLK:] = ref_ref[peer]


def miss(got, part_ref, x_own, t_own, gate, mask):
    groups, rows, width = got.shape
    return pl.pallas_call(
        miss_kernel,
        out_shape=[
            jax.ShapeDtypeStruct((rows, width), F32),
            jax.ShapeDtypeStruct((groups, 2 * rows, width), BF16),
        ],
        compiler_params=params(),
        cost_estimate=cost(20 * rows * width, 8 * groups * rows * width),
    )(got, part_ref, x_own, t_own, gate, mask)


def back_kernel(
    got_ref, unit_ref, x_ref, t_ref, gate_ref, mask_ref, own_ref, other_ref, bo_ref, bt_ref, so_ref, st_ref,
    do_ref, dt_ref, dlow_ref, send_ref, turned_scr, straight_scr,
):
    step = pl.program_id(0)
    width = got_ref.shape[2]
    dy = got_ref[:, :BLK].reshape(CAP * BLK, width)
    d_own = (product(dy, own_ref[...]) * so_ref[...]).astype(BF16)
    d_other = (product(dy, other_ref[...]) * st_ref[...]).astype(BF16)
    do_ref[...] = d_own
    dt_ref[...] = d_other
    turned = rows_by_rows(bo_ref[...], d_own) + rows_by_rows(bt_ref[...], d_other)
    straight = rows_by_rows(d_own, bo_ref[...]) + rows_by_rows(d_other, bt_ref[...])

    @pl.when(step == 0)
    def _():
        turned_scr[...] = turned
        straight_scr[...] = straight

    @pl.when(step > 0)
    def _():
        turned_scr[...] += turned
        straight_scr[...] += straight

    @pl.when(step == pl.num_programs(0) - 1)
    def _():
        rank = turned_scr.shape[0]
        dlow_ref[...] = straight_scr[...].astype(BF16)
        mask = mask_ref[...]
        base = x_ref[...].astype(F32) - t_ref[...].astype(F32)
        miss_ref = mask * (base + gate_ref[...] * jnp.sum(got_ref[:, BLK:].astype(F32), axis=0))
        miss_pol = 0.5 * unit_ref[...]
        parts = jnp.sum((miss_pol - miss_ref) * (miss_pol + miss_ref), axis=1, keepdims=True)
        excess = jnp.broadcast_to(jnp.sum(parts, axis=0, keepdims=True), (NOTE, CAP * BLK))
        high = excess.astype(BF16)
        rest = excess - high.astype(F32)
        middle = rest.astype(BF16)
        lowest = rest - middle.astype(F32)
        line = lax.broadcasted_iota(jnp.int32, excess.shape, 0)
        note = jnp.where(line == 0, high.astype(F32), jnp.where(line == 1, middle.astype(F32), lowest)).astype(BF16)
        total = turned_scr[...].astype(BF16)
        for peer in range(send_ref.shape[0]):
            send_ref[peer, :rank] = total
            send_ref[peer, rank:] = note


def backward(got, unit, x_own, t_own, gate, mask, own, other, b_own, b_other, s_own, s_other):
    groups, _, width = got.shape
    half = own.shape[1]
    rank = b_own.shape[0]
    rows = CAP * BLK
    step = 256
    weight = pl.BlockSpec((width, step), lambda i: (0, i))
    factor = pl.BlockSpec((rank, step), lambda i: (0, i))
    cut = pl.BlockSpec((rows, step), lambda i: (0, i))
    block = whole((BLK, width))
    return pl.pallas_call(
        back_kernel,
        grid=(half // step,),
        out_shape=[
            jax.ShapeDtypeStruct((rows, half), BF16),
            jax.ShapeDtypeStruct((rows, half), BF16),
            jax.ShapeDtypeStruct((rows, rank), BF16),
            jax.ShapeDtypeStruct((groups, rank + NOTE, rows), BF16),
        ],
        in_specs=[
            whole(got.shape), block, block, block, whole((1, width)), whole((BLK, 1)),
            weight, weight, factor, factor, cut, cut,
        ],
        out_specs=[cut, cut, whole((rows, rank)), whole((groups, rank + NOTE, rows))],
        scratch_shapes=[pltpu.VMEM((rank, rows), F32), pltpu.VMEM((rows, rank), F32)],
        compiler_params=params(),
        cost_estimate=cost(4 * rows * width * half, 4 * width * half + 12 * rows * half),
    )(got, unit, x_own, t_own, gate, mask, own, other, b_own, b_other, s_own, s_other)


def factor_kernel(split_ref, do_ref, dt_ref, own_ref, other_ref):
    own_ref[...] = product(split_ref[...], do_ref[...])
    other_ref[...] = product(split_ref[...], dt_ref[...])


def factor_terms(split, d_own, d_other):
    lines, rows = split.shape
    half = d_own.shape[1]
    return pl.pallas_call(
        factor_kernel,
        out_shape=[jax.ShapeDtypeStruct((lines, half), F32)] * 2,
        compiler_params=params(),
        cost_estimate=cost(4 * lines * rows * half, 8 * lines * half),
    )(split, d_own, d_other)


def pile_kernel(
    ints_ref, scales_ref, got_ref, modded_ref, own_ref, other_ref, keep_ref, give_ref, facts_ref
):
    wins = ints_ref[0]
    core = ints_ref[1]
    groups, lines, rows = got_ref.shape
    rank = lines - NOTE
    half = own_ref.shape[1]
    gap_first = jnp.zeros((1, rows), F32)
    gap_second = jnp.zeros((1, rows), F32)
    for slot in range(groups):
        note = got_ref[slot, rank:].astype(F32)
        excess = note[0:1] + note[1:2] + note[2:3]
        gap_first += jnp.where(slot < wins, excess, 0.0)
        gap_second += jnp.where(slot < wins, 0.0, excess)
    scale_first = scales_ref[0]
    scale_second = scales_ref[1]
    inside = -BETA * (gap_first * scale_first - gap_second * scale_second)
    losses = jnp.maximum(-inside, 0.0) + jnp.log1p(jnp.exp(-jnp.abs(inside)))
    weight = BETA * LOSS_SCALE * jax.nn.sigmoid(-inside)
    first = weight * scale_first
    second = -weight * scale_second
    line = lax.broadcasted_iota(jnp.int32, facts_ref.shape, 0)
    facts_ref[...] = jnp.where(line == 0, losses, jnp.where(line == 1, first, second))
    slot = lax.broadcasted_iota(jnp.int32, (1, rows), 1) // BLK
    total = jnp.sum(got_ref[:, :rank].astype(F32), axis=0)
    dlow = (total * jnp.where(slot < wins, first, second)).astype(BF16)
    one = first[:, :1]
    two = second[:, :1]
    near = modded_ref[:, pl.ds(pl.multiple_of(core * half, 128), half)]
    far = modded_ref[:, pl.ds(pl.multiple_of((1 - core) * half, 128), half)]
    keep_ref[:rank] = one * own_ref[:rank] + two * own_ref[rank:]
    keep_ref[rank:] = product(dlow, near)
    give_ref[:rank] = (one * other_ref[:rank] + two * other_ref[rank:]).astype(BF16)
    give_ref[rank:] = product(dlow, far).astype(BF16)


def piles(ints, scales, got, modded, b_own, b_other):
    lines, half = b_own.shape
    rows = got.shape[2]
    return pl.pallas_call(
        pile_kernel,
        out_shape=[
            jax.ShapeDtypeStruct((lines, half), F32),
            jax.ShapeDtypeStruct((lines, half), BF16),
            jax.ShapeDtypeStruct((8, rows), F32),
        ],
        in_specs=[pl.BlockSpec(memory_space=SMEM)] * 2 + [pl.BlockSpec(memory_space=pltpu.VMEM)] * 4,
        compiler_params=params(),
        cost_estimate=cost(2 * lines * half * rows, 16 * lines * half),
    )(ints, scales, got, modded, b_own, b_other)


def dm_kernel(after_ref, do_ref, dt_ref, dlow_ref, own_ref, other_ref, a_ref, out_ref):
    total = rows_by_rows(do_ref[...], own_ref[...]) + rows_by_rows(dt_ref[...], other_ref[...])
    out_ref[...] = (total + product(dlow_ref[...], a_ref[...])).astype(BF16)


def dm_terms(after, d_own, d_other, dlow, own, other, a_turned):
    rows, half = d_own.shape
    width = own.shape[0]
    rank = dlow.shape[1]
    step = 512
    cut = pl.BlockSpec((step, half), lambda i: (i, 0))
    return pl.pallas_call(
        dm_kernel,
        grid=(width // step,),
        out_shape=jax.ShapeDtypeStruct((rows, width), BF16),
        in_specs=[
            pl.BlockSpec(memory_space=pl.ANY),
            whole((rows, half)),
            whole((rows, half)),
            whole((rows, rank)),
            cut,
            cut,
            pl.BlockSpec((rank, step), lambda i: (0, i)),
        ],
        out_specs=pl.BlockSpec((rows, step), lambda i: (0, i)),
        compiler_params=params(),
        cost_estimate=cost(4 * rows * width * half, 4 * width * half + 2 * rows * width),
    )(after, d_own, d_other, dlow, own, other, a_turned)


def token_kernel(one_ref, two_ref, three_ref, four_ref, x_ref, scale_ref, unit_ref, coef_ref, out_ref):
    total = one_ref[...].astype(F32) + two_ref[...].astype(F32)
    total = total + three_ref[...].astype(F32) + four_ref[...].astype(F32)
    normed, inverse = normalise(x_ref[...])
    dn = total * scale_ref[...]
    mean_one = jnp.mean(dn, axis=-1, keepdims=True)
    mean_two = jnp.mean(dn * normed, axis=-1, keepdims=True)
    grad = coef_ref[...] * (unit_ref[...] + inverse * (dn - mean_one - normed * mean_two))
    out_ref[...] = grad.astype(BF16)


def token_gradient(pieces, x_own, scale, unit, coef):
    rows, width = x_own.shape
    return pl.pallas_call(
        token_kernel,
        out_shape=jax.ShapeDtypeStruct((rows, width), BF16),
        compiler_params=params(),
        cost_estimate=cost(20 * rows * width, 20 * rows * width),
    )(*pieces, x_own, scale, unit, coef)


def per_device(
    tokens,
    targets,
    modulation,
    live_block_count,
    preferred_blocks,
    last_block_rows,
    up_rows,
    down_rows,
    factor_in,
    factor_out,
):
    width = tokens.shape[1]
    n_z, n_x, n_c, n_t = (lax.axis_size(a) for a in ("z", "x", "c", "t"))
    n_dp = n_z * n_x * n_c
    core = lax.axis_index("c")
    group = lax.axis_index("t")
    thin, hidden = up_rows.shape
    half = hidden // n_c
    pair = n_c * thin
    rank = factor_in.shape[1]

    both = jnp.concatenate([up_rows, down_rows], axis=0)
    keep = lax.dynamic_slice_in_dim(both, core * half, half, axis=1)
    got = lax.ppermute(lax.dynamic_slice_in_dim(both, (1 - core) * half, half, axis=1), "c", SWAP)
    first = jnp.where(core == 0, keep, got)
    second = jnp.where(core == 0, got, keep)
    up_pair = jnp.concatenate([first[:thin], second[:thin]], axis=0)
    down_pair = jnp.concatenate([first[thin:], second[thin:]], axis=0)
    count = live_block_count[0]
    wins = preferred_blocks[0]
    slots = jnp.arange(CAP, dtype=jnp.int32)
    flags = (slots >= wins).astype(jnp.int32)
    last = jnp.where(flags == 0, wins - 1, count - 1)
    tail = jnp.where(flags == 0, last_block_rows[0, 0], last_block_rows[0, 1])
    live = jnp.where(slots < count, jnp.where(slots == last, tail, BLK), 0)
    rows_first = jnp.sum(jnp.where(flags == 0, live, 0)).astype(F32)
    rows_second = jnp.sum(jnp.where(flags == 1, live, 0)).astype(F32)
    scales = 1.0 / (width * jnp.stack([rows_first, rows_second]))

    own_first = group < wins
    x_own = lax.dynamic_slice_in_dim(tokens, group * BLK, BLK, axis=0)
    t_own = lax.dynamic_slice_in_dim(targets, group * BLK, BLK, axis=0)
    vec_own = jnp.where(own_first, modulation[0], modulation[1]).astype(F32)
    live_own = lax.dynamic_slice_in_dim(live, group, 1)
    mask = (jnp.arange(BLK, dtype=jnp.int32)[:, None] < live_own[None, :]).astype(F32)
    gate = vec_own[2:3]
    scale_own = 1.0 + vec_own[1:2]

    a_turned = factor_in.T
    factor_own = lax.dynamic_slice_in_dim(factor_out, core * half, half, axis=1)
    factor_other = lax.dynamic_slice_in_dim(factor_out, (1 - core) * half, half, axis=1)
    modded, low, low_split = prepare(preferred_blocks, tokens, modulation.reshape(6, width), a_turned)

    early = pair - LATE
    line = lax.all_gather(jnp.concatenate([up_pair, down_pair[:early]], 0), "z", axis=0, tiled=True)
    line = line.reshape(n_z, pair + early, half)
    line = jnp.concatenate([line[:, :pair].reshape(n_z * pair, half), line[:, pair:].reshape(n_z * early, half)], 0)
    near = spread(line, "x", n_x)
    late = spread(down_pair[early:], "x", n_x).reshape(n_x * LATE, half)
    late = after(late, [modded, low, low_split, factor_own, factor_other, x_own, t_own, gate, scale_own, mask])
    late = lax.all_gather(late, "z", axis=0, tiled=True).reshape(n_z, n_x, LATE, half)

    def arrange(block, late):
        up = block[:, : n_z * pair].reshape(n_x, n_z, pair, half).transpose(1, 0, 2, 3).reshape(width, half)
        down = block[:, n_z * pair :].reshape(n_x, n_z, early, half).transpose(1, 0, 2, 3)
        return up, jnp.concatenate([down, late], axis=2).reshape(width, half)

    up_own, down_own = arrange(near, late)
    up_other, down_other = arrange(lax.ppermute(near, "c", SWAP), lax.ppermute(late, "c", SWAP))

    pol_own, ref_own, slope_own = activate(modded, low, up_own, factor_own)
    pol_other, ref_other, slope_other = activate(modded, low, up_other, factor_other)
    part_pol = lower(pol_own, pol_other, down_own, down_other).reshape(CAP, BLK, width)
    got_pol = lax.all_to_all(part_pol, "t", 0, 0, tiled=True)
    part_ref = lower(ref_own, ref_other, down_own, down_other).reshape(CAP, BLK, width)

    unit, send = miss(got_pol, part_ref, x_own, t_own, gate, mask)
    got_dy = lax.all_to_all(send, "t", 0, 0, tiled=True)
    d_own, d_other, dlow_part, send = backward(
        got_dy, unit, x_own, t_own, gate, mask, down_own, down_other, factor_own, factor_other, slope_own, slope_other
    )
    got_low = lax.all_to_all(send, "t", 0, 0, tiled=True)
    b_own, b_other = factor_terms(low_split, d_own, d_other)
    keep, give, facts = piles(
        jnp.stack([wins, core]).astype(jnp.int32), scales, got_low, modded, b_own, b_other
    )
    losses = facts[0, :1]
    coef_own = jnp.where(own_first, facts[1:2, :1], facts[2:3, :1])
    pile = (keep + lax.ppermute(give, "c", SWAP).astype(F32)).astype(BF16)

    chips = n_z * n_x
    pieces = lax.all_to_all(pile.reshape(chips, 2 * rank // chips, half), CHIPS, 0, 0, tiled=True)
    total = (jnp.sum(pieces.astype(F32), axis=0) / n_dp).astype(BF16)
    mine = spread(total, CHIPS, chips).reshape(2 * rank, half)
    theirs = lax.ppermute(mine, "c", SWAP)
    ends = jnp.concatenate([mine, theirs], 1)
    flipped = jnp.concatenate([theirs, mine], 1)
    ends = jnp.where(core == 0, ends, flipped).astype(F32)
    sum_b = ends[:rank]
    sum_a = ends[rank:].T

    dm_part = dm_terms(pile, d_own, d_other, dlow_part, up_own, up_other, a_turned).reshape(CAP, BLK, width)
    turns = [[(i, (i + step) % n_t) for i in range(n_t)] for step in range(n_t)]
    chunks = [lax.dynamic_index_in_dim(dm_part, (group + step) % n_t, 0, False) for step in range(n_t)]
    chunks = [chunks[0]] + [lax.ppermute(chunks[step], "t", turns[step]) for step in range(1, n_t)]
    grad_block = token_gradient(chunks, x_own, scale_own, unit, coef_own)
    blocks = [grad_block] + [lax.ppermute(grad_block, "t", turns[step]) for step in range(1, n_t)]
    blocks = jnp.stack(blocks)
    grad_tokens = jnp.concatenate(
        [lax.dynamic_index_in_dim(blocks, (group - slot) % n_t, 0, False) for slot in range(n_t)], 0
    )
    return losses, grad_tokens, sum_a, sum_b


def solution(mesh):
    n_dp, n_t = mesh.devices.shape
    fine = Mesh(mesh.devices.reshape(n_dp // 8, 4, 2, n_t), ("z", "x", "c", "t"))
    return jax.shard_map(
        per_device,
        mesh=fine,
        in_specs=(
            P(DP, None),
            P(DP, None),
            P(DP, None, None),
            P(DP),
            P(DP),
            P(DP, None),
            P(DP, "t"),
            P(DP, "t"),
            P(),
            P(None, "t"),
        ),
        out_specs=(P(DP), P(DP, None), P(), P(None, "t")),
        check_vma=False,
    )
```

```python
import jax
import jax.numpy as jnp
from jax import lax
from jax.experimental import pallas as pl
from jax.experimental.pallas import tpu as pltpu
from jax.sharding import Mesh
from jax.sharding import PartitionSpec as P

BLK = 64
CAP = 4
EPS = 1e-06
BETA = 20.0
LOSS_SCALE = 4096.0
ROOT = 0.7978845608028654
CUBE = 0.044715
BF16 = jnp.bfloat16
F32 = jnp.float32
DP = ("z", "x", "c")
CHIPS = ("z", "x")
SWAP = [(0, 1), (1, 0)]
NOTE = 16
VMEM_LIMIT = 40 * 1024 * 1024
SMEM = pltpu.SMEM


def gelu(pre):
    th = jnp.tanh(ROOT * (pre + CUBE * pre * pre * pre))
    return 0.5 * pre * (1.0 + th)


def gelu_and_slope(pre):
    square = pre * pre
    th = jnp.tanh(ROOT * (pre + CUBE * pre * square))
    half = 0.5 * (1.0 + th)
    slope = half + 0.5 * pre * (1.0 - th * th) * (ROOT * (1.0 + 3.0 * CUBE * square))
    return pre * half, slope


def rows_by_rows(left, right):
    return lax.dot_general(left, right, (((1,), (1,)), ((), ())), preferred_element_type=F32)


def product(left, right):
    return jnp.dot(left, right, preferred_element_type=F32)


def spread(value, axes, n):
    return lax.all_to_all(jnp.broadcast_to(value[None], (n, *value.shape)), axes, 0, 0, tiled=True)


def normalise(rows):
    wide = rows.astype(F32)
    center = wide - jnp.mean(wide, axis=-1, keepdims=True)
    inverse = lax.rsqrt(jnp.mean(center * center, axis=-1, keepdims=True) + EPS)
    return center * inverse, inverse


def params():
    return pltpu.CompilerParams(vmem_limit_bytes=VMEM_LIMIT)


def cost(flops, moved, tanh=0):
    return pl.CostEstimate(flops=flops, bytes_accessed=moved, transcendentals=tanh)


def whole(shape):
    return pl.BlockSpec(shape, lambda *_: (0,) * len(shape))


def input_kernel(wins_ref, x_ref, mod_ref, a_ref, modded_ref, low_ref, split_ref):
    wins = wins_ref[0]
    for slot in range(CAP):
        rows = slice(slot * BLK, (slot + 1) * BLK)
        normed, _ = normalise(x_ref[rows])
        first = slot < wins
        shift = jnp.where(first, mod_ref[0:1].astype(F32), mod_ref[3:4].astype(F32))
        scale = 1.0 + jnp.where(first, mod_ref[1:2].astype(F32), mod_ref[4:5].astype(F32))
        modded_ref[rows] = (normed * scale + shift).astype(BF16)
    modded = modded_ref[...]
    low_ref[...] = rows_by_rows(modded, a_ref[...]).astype(BF16)
    turned = rows_by_rows(a_ref[...], modded)
    second = lax.broadcasted_iota(jnp.int32, turned.shape, 1) // BLK >= wins
    rank = turned.shape[0]
    split_ref[:rank] = jnp.where(second, 0.0, turned).astype(BF16)
    split_ref[rank:] = jnp.where(second, turned, 0.0).astype(BF16)


def prepare(wins, tokens, mod, a_turned):
    rows, width = tokens.shape
    rank = a_turned.shape[0]
    return pl.pallas_call(
        input_kernel,
        out_shape=[
            jax.ShapeDtypeStruct((rows, width), BF16),
            jax.ShapeDtypeStruct((rows, rank), BF16),
            jax.ShapeDtypeStruct((2 * rank, rows), BF16),
        ],
        in_specs=[pl.BlockSpec(memory_space=SMEM)] + [pl.BlockSpec(memory_space=pltpu.VMEM)] * 3,
        compiler_params=params(),
        cost_estimate=cost(4 * rows * width * rank, 4 * rows * width),
    )(wins, tokens, mod, a_turned)


def after_kernel(*refs):
    del refs


def after(value, others):
    return pl.pallas_call(
        after_kernel,
        out_shape=jax.ShapeDtypeStruct(value.shape, value.dtype),
        in_specs=[pl.BlockSpec(memory_space=pl.ANY)] * (1 + len(others)),
        out_specs=pl.BlockSpec(memory_space=pl.ANY),
        input_output_aliases={0: 0},
    )(value, *others)


def up_kernel(modded_ref, low_ref, up_ref, b_ref, pol_ref, ref_ref, slope_ref):
    pre_ref = product(modded_ref[...], up_ref[...])
    pre_pol = pre_ref + product(low_ref[...], b_ref[...])
    act, slope = gelu_and_slope(pre_pol)
    pol_ref[...] = act.astype(BF16)
    slope_ref[...] = slope
    ref_ref[...] = gelu(pre_ref).astype(BF16)


def activate(modded, low, weights, factor):
    rows, width = modded.shape
    rank, half = factor.shape
    step = 256
    cut = pl.BlockSpec((rows, step), lambda i: (0, i))
    return pl.pallas_call(
        up_kernel,
        grid=(half // step,),
        out_shape=[
            jax.ShapeDtypeStruct((rows, half), BF16),
            jax.ShapeDtypeStruct((rows, half), BF16),
            jax.ShapeDtypeStruct((rows, half), F32),
        ],
        in_specs=[
            whole((rows, width)),
            whole((rows, rank)),
            pl.BlockSpec((width, step), lambda i: (0, i)),
            pl.BlockSpec((rank, step), lambda i: (0, i)),
        ],
        out_specs=[cut, cut, cut],
        compiler_params=params(),
        cost_estimate=cost(2 * rows * width * half, 2 * width * half + 10 * rows * half, 2 * rows * half),
    )(modded, low, weights, factor)


def down_kernel(left_ref, right_ref, own_ref, other_ref, out_ref):
    total = rows_by_rows(left_ref[...], own_ref[...]) + rows_by_rows(right_ref[...], other_ref[...])
    out_ref[...] = total.astype(BF16)


def lower(left, right, own, other):
    rows, half = left.shape
    width = own.shape[0]
    step = 512
    cut = pl.BlockSpec((step, half), lambda i: (i, 1))
    return pl.pallas_call(
        down_kernel,
        grid=(width // step,),
        out_shape=jax.ShapeDtypeStruct((rows, width), BF16),
        in_specs=[whole((rows, half)), whole((rows, half)), cut, cut],
        out_specs=pl.BlockSpec((rows, step), lambda i: (0, i)),
        compiler_params=params(),
        cost_estimate=cost(4 * rows * width * half, 4 * width * half + 2 * rows * width),
    )(left, right, own, other)


def miss_kernel(got_ref, ref_ref, x_ref, t_ref, gate_ref, mask_ref, unit_ref, send_ref):
    total = jnp.sum(got_ref[...].astype(F32), axis=0)
    gate = gate_ref[...]
    unit = 2.0 * mask_ref[...] * (x_ref[...].astype(F32) - t_ref[...].astype(F32) + gate * total)
    unit_ref[...] = unit
    dy = (gate * unit).astype(BF16)
    for peer in range(send_ref.shape[0]):
        send_ref[peer, :BLK] = dy
        send_ref[peer, BLK:] = ref_ref[peer]


def miss(got, part_ref, x_own, t_own, gate, mask):
    groups, rows, width = got.shape
    return pl.pallas_call(
        miss_kernel,
        out_shape=[
            jax.ShapeDtypeStruct((rows, width), F32),
            jax.ShapeDtypeStruct((groups, 2 * rows, width), BF16),
        ],
        compiler_params=params(),
        cost_estimate=cost(20 * rows * width, 8 * groups * rows * width),
    )(got, part_ref, x_own, t_own, gate, mask)


def back_kernel(
    got_ref, unit_ref, x_ref, t_ref, gate_ref, mask_ref, own_ref, other_ref, bo_ref, bt_ref, so_ref, st_ref,
    do_ref, dt_ref, dlow_ref, send_ref, turned_scr, straight_scr,
):
    step = pl.program_id(0)
    width = got_ref.shape[2]
    dy = got_ref[:, :BLK].reshape(CAP * BLK, width)
    d_own = (product(dy, own_ref[...]) * so_ref[...]).astype(BF16)
    d_other = (product(dy, other_ref[...]) * st_ref[...]).astype(BF16)
    do_ref[...] = d_own
    dt_ref[...] = d_other
    turned = rows_by_rows(bo_ref[...], d_own) + rows_by_rows(bt_ref[...], d_other)
    straight = rows_by_rows(d_own, bo_ref[...]) + rows_by_rows(d_other, bt_ref[...])

    @pl.when(step == 0)
    def _():
        turned_scr[...] = turned
        straight_scr[...] = straight

    @pl.when(step > 0)
    def _():
        turned_scr[...] += turned
        straight_scr[...] += straight

    @pl.when(step == pl.num_programs(0) - 1)
    def _():
        rank = turned_scr.shape[0]
        dlow_ref[...] = straight_scr[...].astype(BF16)
        mask = mask_ref[...]
        base = x_ref[...].astype(F32) - t_ref[...].astype(F32)
        miss_ref = mask * (base + gate_ref[...] * jnp.sum(got_ref[:, BLK:].astype(F32), axis=0))
        miss_pol = 0.5 * unit_ref[...]
        parts = jnp.sum((miss_pol - miss_ref) * (miss_pol + miss_ref), axis=1, keepdims=True)
        excess = jnp.broadcast_to(jnp.sum(parts, axis=0, keepdims=True), (NOTE, CAP * BLK))
        high = excess.astype(BF16)
        rest = excess - high.astype(F32)
        middle = rest.astype(BF16)
        lowest = rest - middle.astype(F32)
        line = lax.broadcasted_iota(jnp.int32, excess.shape, 0)
        note = jnp.where(line == 0, high.astype(F32), jnp.where(line == 1, middle.astype(F32), lowest)).astype(BF16)
        total = turned_scr[...].astype(BF16)
        for peer in range(send_ref.shape[0]):
            send_ref[peer, :rank] = total
            send_ref[peer, rank:] = note


def backward(got, unit, x_own, t_own, gate, mask, own, other, b_own, b_other, s_own, s_other):
    groups, _, width = got.shape
    half = s_own.shape[1]
    rank = b_own.shape[0]
    rows = CAP * BLK
    step = 256
    weight = pl.BlockSpec((width, step), lambda i: (0, half // step + i))
    factor = pl.BlockSpec((rank, step), lambda i: (0, i))
    cut = pl.BlockSpec((rows, step), lambda i: (0, i))
    block = whole((BLK, width))
    return pl.pallas_call(
        back_kernel,
        grid=(half // step,),
        out_shape=[
            jax.ShapeDtypeStruct((rows, half), BF16),
            jax.ShapeDtypeStruct((rows, half), BF16),
            jax.ShapeDtypeStruct((rows, rank), BF16),
            jax.ShapeDtypeStruct((groups, rank + NOTE, rows), BF16),
        ],
        in_specs=[
            whole(got.shape), block, block, block, whole((1, width)), whole((BLK, 1)),
            weight, weight, factor, factor, cut, cut,
        ],
        out_specs=[cut, cut, whole((rows, rank)), whole((groups, rank + NOTE, rows))],
        scratch_shapes=[pltpu.VMEM((rank, rows), F32), pltpu.VMEM((rows, rank), F32)],
        compiler_params=params(),
        cost_estimate=cost(4 * rows * width * half, 4 * width * half + 12 * rows * half),
    )(got, unit, x_own, t_own, gate, mask, own, other, b_own, b_other, s_own, s_other)


def factor_kernel(split_ref, do_ref, dt_ref, own_ref, other_ref):
    own_ref[...] = product(split_ref[...], do_ref[...])
    other_ref[...] = product(split_ref[...], dt_ref[...])


def factor_terms(split, d_own, d_other):
    lines, rows = split.shape
    half = d_own.shape[1]
    return pl.pallas_call(
        factor_kernel,
        out_shape=[jax.ShapeDtypeStruct((lines, half), F32)] * 2,
        compiler_params=params(),
        cost_estimate=cost(4 * lines * rows * half, 8 * lines * half),
    )(split, d_own, d_other)


def pile_kernel(
    ints_ref, scales_ref, got_ref, modded_ref, own_ref, other_ref, keep_ref, give_ref, facts_ref
):
    wins = ints_ref[0]
    core = ints_ref[1]
    groups, lines, rows = got_ref.shape
    rank = lines - NOTE
    half = own_ref.shape[1]
    gap_first = jnp.zeros((1, rows), F32)
    gap_second = jnp.zeros((1, rows), F32)
    for slot in range(groups):
        note = got_ref[slot, rank:].astype(F32)
        excess = note[0:1] + note[1:2] + note[2:3]
        gap_first += jnp.where(slot < wins, excess, 0.0)
        gap_second += jnp.where(slot < wins, 0.0, excess)
    scale_first = scales_ref[0]
    scale_second = scales_ref[1]
    inside = -BETA * (gap_first * scale_first - gap_second * scale_second)
    losses = jnp.maximum(-inside, 0.0) + jnp.log1p(jnp.exp(-jnp.abs(inside)))
    weight = BETA * LOSS_SCALE * jax.nn.sigmoid(-inside)
    first = weight * scale_first
    second = -weight * scale_second
    line = lax.broadcasted_iota(jnp.int32, facts_ref.shape, 0)
    facts_ref[...] = jnp.where(line == 0, losses, jnp.where(line == 1, first, second))
    slot = lax.broadcasted_iota(jnp.int32, (1, rows), 1) // BLK
    total = jnp.sum(got_ref[:, :rank].astype(F32), axis=0)
    dlow = (total * jnp.where(slot < wins, first, second)).astype(BF16)
    one = first[:, :1]
    two = second[:, :1]
    near = modded_ref[:, pl.ds(pl.multiple_of(core * half, 128), half)]
    far = modded_ref[:, pl.ds(pl.multiple_of((1 - core) * half, 128), half)]
    keep_ref[:rank] = one * own_ref[:rank] + two * own_ref[rank:]
    keep_ref[rank:] = product(dlow, near)
    give_ref[:rank] = (one * other_ref[:rank] + two * other_ref[rank:]).astype(BF16)
    give_ref[rank:] = product(dlow, far).astype(BF16)


def piles(ints, scales, got, modded, b_own, b_other):
    lines, half = b_own.shape
    rows = got.shape[2]
    return pl.pallas_call(
        pile_kernel,
        out_shape=[
            jax.ShapeDtypeStruct((lines, half), F32),
            jax.ShapeDtypeStruct((lines, half), BF16),
            jax.ShapeDtypeStruct((8, rows), F32),
        ],
        in_specs=[pl.BlockSpec(memory_space=SMEM)] * 2 + [pl.BlockSpec(memory_space=pltpu.VMEM)] * 4,
        compiler_params=params(),
        cost_estimate=cost(2 * lines * half * rows, 16 * lines * half),
    )(ints, scales, got, modded, b_own, b_other)


def dm_kernel(after_ref, do_ref, dt_ref, dlow_ref, own_ref, other_ref, a_ref, out_ref):
    total = rows_by_rows(do_ref[...], own_ref[...]) + rows_by_rows(dt_ref[...], other_ref[...])
    out_ref[...] = (total + product(dlow_ref[...], a_ref[...])).astype(BF16)


def dm_terms(after, d_own, d_other, dlow, own, other, a_turned):
    rows, half = d_own.shape
    width = own.shape[0]
    rank = dlow.shape[1]
    step = 512
    cut = pl.BlockSpec((step, half), lambda i: (i, 0))
    return pl.pallas_call(
        dm_kernel,
        grid=(width // step,),
        out_shape=jax.ShapeDtypeStruct((rows, width), BF16),
        in_specs=[
            pl.BlockSpec(memory_space=pl.ANY),
            whole((rows, half)),
            whole((rows, half)),
            whole((rows, rank)),
            cut,
            cut,
            pl.BlockSpec((rank, step), lambda i: (0, i)),
        ],
        out_specs=pl.BlockSpec((rows, step), lambda i: (0, i)),
        compiler_params=params(),
        cost_estimate=cost(4 * rows * width * half, 4 * width * half + 2 * rows * width),
    )(after, d_own, d_other, dlow, own, other, a_turned)


def token_kernel(one_ref, two_ref, three_ref, four_ref, x_ref, scale_ref, unit_ref, coef_ref, out_ref):
    total = one_ref[...].astype(F32) + two_ref[...].astype(F32)
    total = total + three_ref[...].astype(F32) + four_ref[...].astype(F32)
    normed, inverse = normalise(x_ref[...])
    dn = total * scale_ref[...]
    mean_one = jnp.mean(dn, axis=-1, keepdims=True)
    mean_two = jnp.mean(dn * normed, axis=-1, keepdims=True)
    grad = coef_ref[...] * (unit_ref[...] + inverse * (dn - mean_one - normed * mean_two))
    out_ref[...] = grad.astype(BF16)


def token_gradient(pieces, x_own, scale, unit, coef):
    rows, width = x_own.shape
    return pl.pallas_call(
        token_kernel,
        out_shape=jax.ShapeDtypeStruct((rows, width), BF16),
        compiler_params=params(),
        cost_estimate=cost(20 * rows * width, 20 * rows * width),
    )(*pieces, x_own, scale, unit, coef)


def per_device(
    tokens,
    targets,
    modulation,
    live_block_count,
    preferred_blocks,
    last_block_rows,
    up_rows,
    down_rows,
    factor_in,
    factor_out,
):
    width = tokens.shape[1]
    n_z, n_x, n_c, n_t = (lax.axis_size(a) for a in ("z", "x", "c", "t"))
    n_dp = n_z * n_x * n_c
    core = lax.axis_index("c")
    group = lax.axis_index("t")
    thin, hidden = up_rows.shape
    half = hidden // n_c
    rank = factor_in.shape[1]

    sent = jnp.stack([up_rows.reshape(thin, n_c, half), down_rows.reshape(thin, n_c, half)], axis=2)
    sent = sent.reshape(thin, n_c, 2 * half).transpose(1, 0, 2)
    sent = jnp.broadcast_to(sent[None], (n_x, n_c, thin, 2 * half)).reshape(n_x * n_c, thin, 2 * half)
    near = lax.all_to_all(sent, ("x", "c"), 0, 0, tiled=True).reshape(n_x * n_c * thin, 2 * half)
    own = lax.all_gather(near, "z", axis=0, tiled=True)

    count = live_block_count[0]
    wins = preferred_blocks[0]
    slots = jnp.arange(CAP, dtype=jnp.int32)
    flags = (slots >= wins).astype(jnp.int32)
    last = jnp.where(flags == 0, wins - 1, count - 1)
    tail = jnp.where(flags == 0, last_block_rows[0, 0], last_block_rows[0, 1])
    live = jnp.where(slots < count, jnp.where(slots == last, tail, BLK), 0)
    rows_first = jnp.sum(jnp.where(flags == 0, live, 0)).astype(F32)
    rows_second = jnp.sum(jnp.where(flags == 1, live, 0)).astype(F32)
    scales = 1.0 / (width * jnp.stack([rows_first, rows_second]))

    own_first = group < wins
    x_own = lax.dynamic_slice_in_dim(tokens, group * BLK, BLK, axis=0)
    t_own = lax.dynamic_slice_in_dim(targets, group * BLK, BLK, axis=0)
    vec_own = jnp.where(own_first, modulation[0], modulation[1]).astype(F32)
    live_own = lax.dynamic_slice_in_dim(live, group, 1)
    mask = (jnp.arange(BLK, dtype=jnp.int32)[:, None] < live_own[None, :]).astype(F32)
    gate = vec_own[2:3]
    scale_own = 1.0 + vec_own[1:2]

    a_turned = factor_in.T
    factor_own = lax.dynamic_slice_in_dim(factor_out, core * half, half, axis=1)
    factor_other = lax.dynamic_slice_in_dim(factor_out, (1 - core) * half, half, axis=1)
    modded, low, low_split = prepare(preferred_blocks, tokens, modulation.reshape(6, width), a_turned)

    own = after(own, [modded, low, low_split, factor_own, factor_other, x_own, t_own, gate, scale_own, mask])
    other = lax.ppermute(own, "c", SWAP)

    pol_own, ref_own, slope_own = activate(modded, low, own, factor_own)
    pol_other, ref_other, slope_other = activate(modded, low, other, factor_other)
    part_pol = lower(pol_own, pol_other, own, other).reshape(CAP, BLK, width)
    got_pol = lax.all_to_all(part_pol, "t", 0, 0, tiled=True)
    part_ref = lower(ref_own, ref_other, own, other).reshape(CAP, BLK, width)

    unit, send = miss(got_pol, part_ref, x_own, t_own, gate, mask)
    got_dy = lax.all_to_all(send, "t", 0, 0, tiled=True)
    d_own, d_other, dlow_part, send = backward(
        got_dy, unit, x_own, t_own, gate, mask, own, other, factor_own, factor_other, slope_own, slope_other
    )
    got_low = lax.all_to_all(send, "t", 0, 0, tiled=True)
    b_own, b_other = factor_terms(low_split, d_own, d_other)
    keep, give, facts = piles(
        jnp.stack([wins, core]).astype(jnp.int32), scales, got_low, modded, b_own, b_other
    )
    losses = facts[0, :1]
    coef_own = jnp.where(own_first, facts[1:2, :1], facts[2:3, :1])
    pile = (keep + lax.ppermute(give, "c", SWAP).astype(F32)).astype(BF16)

    chips = n_z * n_x
    pieces = lax.all_to_all(pile.reshape(chips, 2 * rank // chips, half), CHIPS, 0, 0, tiled=True)
    total = (jnp.sum(pieces.astype(F32), axis=0) / n_dp).astype(BF16)
    mine = spread(total, CHIPS, chips).reshape(2 * rank, half)
    theirs = lax.ppermute(mine, "c", SWAP)
    ends = jnp.concatenate([mine, theirs], 1)
    flipped = jnp.concatenate([theirs, mine], 1)
    ends = jnp.where(core == 0, ends, flipped).astype(F32)
    sum_b = ends[:rank]
    sum_a = ends[rank:].T

    dm_part = dm_terms(pile, d_own, d_other, dlow_part, own, other, a_turned).reshape(CAP, BLK, width)
    turns = [[(i, (i + step) % n_t) for i in range(n_t)] for step in range(n_t)]
    chunks = [lax.dynamic_index_in_dim(dm_part, (group + step) % n_t, 0, False) for step in range(n_t)]
    chunks = [chunks[0]] + [lax.ppermute(chunks[step], "t", turns[step]) for step in range(1, n_t)]
    grad_block = token_gradient(chunks, x_own, scale_own, unit, coef_own)
    blocks = [grad_block] + [lax.ppermute(grad_block, "t", turns[step]) for step in range(1, n_t)]
    blocks = jnp.stack(blocks)
    grad_tokens = jnp.concatenate(
        [lax.dynamic_index_in_dim(blocks, (group - slot) % n_t, 0, False) for slot in range(n_t)], 0
    )
    return losses, grad_tokens, sum_a, sum_b


def solution(mesh):
    n_dp, n_t = mesh.devices.shape
    fine = Mesh(mesh.devices.reshape(n_dp // 8, 4, 2, n_t), ("z", "x", "c", "t"))
    return jax.shard_map(
        per_device,
        mesh=fine,
        in_specs=(
            P(DP, None),
            P(DP, None),
            P(DP, None, None),
            P(DP),
            P(DP),
            P(DP, None),
            P(DP, "t"),
            P(DP, "t"),
            P(),
            P(None, "t"),
        ),
        out_specs=(P(DP), P(DP, None), P(), P(None, "t")),
        check_vma=False,
    )
```

```python
import jax
import jax.numpy as jnp
from jax import lax
from jax.experimental import pallas as pl
from jax.experimental.pallas import tpu as pltpu
from jax.sharding import Mesh
from jax.sharding import PartitionSpec as P

BLK = 64
CAP = 4
EPS = 1e-06
BETA = 20.0
LOSS_SCALE = 4096.0
ROOT = 0.7978845608028654
CUBE = 0.044715
BF16 = jnp.bfloat16
F32 = jnp.float32
DP = ("z", "x", "c")
SWAP = [(0, 1), (1, 0)]
NOTE = 16
VMEM_LIMIT = 24 * 1024 * 1024
SMEM = pltpu.SMEM


def gelu(pre):
    th = jnp.tanh(ROOT * (pre + CUBE * pre * pre * pre))
    return 0.5 * pre * (1.0 + th)


def gelu_and_slope(pre):
    square = pre * pre
    th = jnp.tanh(ROOT * (pre + CUBE * pre * square))
    half = 0.5 * (1.0 + th)
    slope = half + 0.5 * pre * (1.0 - th * th) * (ROOT * (1.0 + 3.0 * CUBE * square))
    return pre * half, slope


def rows_by_rows(left, right):
    return lax.dot_general(left, right, (((1,), (1,)), ((), ())), preferred_element_type=F32)


def product(left, right):
    return jnp.dot(left, right, preferred_element_type=F32)


def spread(value, axes, n):
    return lax.all_to_all(jnp.broadcast_to(value[None], (n, *value.shape)), axes, 0, 0, tiled=True)


def normalise(rows):
    wide = rows.astype(F32)
    center = wide - jnp.mean(wide, axis=-1, keepdims=True)
    inverse = lax.rsqrt(jnp.mean(center * center, axis=-1, keepdims=True) + EPS)
    return center * inverse, inverse


def params():
    return pltpu.CompilerParams(vmem_limit_bytes=VMEM_LIMIT)


def cost(flops, moved, tanh=0):
    return pl.CostEstimate(flops=flops, bytes_accessed=moved, transcendentals=tanh)


def whole(shape):
    return pl.BlockSpec(shape, lambda *_: (0,) * len(shape))


def input_kernel(wins_ref, x_ref, mod_ref, a_ref, modded_ref, low_ref, split_ref):
    wins = wins_ref[0]
    for slot in range(CAP):
        rows = slice(slot * BLK, (slot + 1) * BLK)
        normed, _ = normalise(x_ref[rows])
        first = slot < wins
        shift = jnp.where(first, mod_ref[0:1].astype(F32), mod_ref[3:4].astype(F32))
        scale = 1.0 + jnp.where(first, mod_ref[1:2].astype(F32), mod_ref[4:5].astype(F32))
        modded_ref[rows] = (normed * scale + shift).astype(BF16)
    modded = modded_ref[...]
    low_ref[...] = rows_by_rows(modded, a_ref[...]).astype(BF16)
    turned = rows_by_rows(a_ref[...], modded)
    second = lax.broadcasted_iota(jnp.int32, turned.shape, 1) // BLK >= wins
    rank = turned.shape[0]
    split_ref[:rank] = jnp.where(second, 0.0, turned).astype(BF16)
    split_ref[rank:] = jnp.where(second, turned, 0.0).astype(BF16)


def prepare(wins, tokens, mod, a_turned):
    rows, width = tokens.shape
    rank = a_turned.shape[0]
    return pl.pallas_call(
        input_kernel,
        out_shape=[
            jax.ShapeDtypeStruct((rows, width), BF16),
            jax.ShapeDtypeStruct((rows, rank), BF16),
            jax.ShapeDtypeStruct((2 * rank, rows), BF16),
        ],
        in_specs=[pl.BlockSpec(memory_space=SMEM)] + [pl.BlockSpec(memory_space=pltpu.VMEM)] * 3,
        compiler_params=params(),
        cost_estimate=cost(4 * rows * width * rank, 4 * rows * width),
    )(wins, tokens, mod, a_turned)


def after_kernel(*refs):
    del refs


def after(value, others):
    return pl.pallas_call(
        after_kernel,
        out_shape=jax.ShapeDtypeStruct(value.shape, value.dtype),
        in_specs=[pl.BlockSpec(memory_space=pl.ANY)] * (1 + len(others)),
        out_specs=pl.BlockSpec(memory_space=pl.ANY),
        input_output_aliases={0: 0},
    )(value, *others)


def up_kernel(modded_ref, low_ref, up_ref, b_ref, pol_ref, ref_ref, slope_ref):
    pre_ref = product(modded_ref[...], up_ref[...])
    pre_pol = pre_ref + product(low_ref[...], b_ref[...])
    act, slope = gelu_and_slope(pre_pol)
    pol_ref[...] = act.astype(BF16)
    slope_ref[...] = slope
    ref_ref[...] = gelu(pre_ref).astype(BF16)


def activate(modded, low, weights, factor):
    rows, width = modded.shape
    rank, half = factor.shape
    step = 256
    cut = pl.BlockSpec((rows, step), lambda i: (0, i))
    return pl.pallas_call(
        up_kernel,
        grid=(half // step,),
        out_shape=[
            jax.ShapeDtypeStruct((rows, half), BF16),
            jax.ShapeDtypeStruct((rows, half), BF16),
            jax.ShapeDtypeStruct((rows, half), F32),
        ],
        in_specs=[
            whole((rows, width)),
            whole((rows, rank)),
            pl.BlockSpec((width, step), lambda i: (0, i)),
            pl.BlockSpec((rank, step), lambda i: (0, i)),
        ],
        out_specs=[cut, cut, cut],
        compiler_params=params(),
        cost_estimate=cost(2 * rows * width * half, 2 * width * half + 10 * rows * half, 2 * rows * half),
    )(modded, low, weights, factor)


def down_kernel(left_ref, right_ref, own_ref, other_ref, out_ref):
    total = rows_by_rows(left_ref[...], own_ref[...]) + rows_by_rows(right_ref[...], other_ref[...])
    out_ref[...] = total.astype(BF16)


def lower(left, right, own, other):
    rows, half = left.shape
    width = own.shape[0]
    step = 512
    cut = pl.BlockSpec((step, half), lambda i: (i, 1))
    return pl.pallas_call(
        down_kernel,
        grid=(width // step,),
        out_shape=jax.ShapeDtypeStruct((rows, width), BF16),
        in_specs=[whole((rows, half)), whole((rows, half)), cut, cut],
        out_specs=pl.BlockSpec((rows, step), lambda i: (0, i)),
        compiler_params=params(),
        cost_estimate=cost(4 * rows * width * half, 4 * width * half + 2 * rows * width),
    )(left, right, own, other)


def miss_kernel(got_ref, ref_ref, x_ref, t_ref, gate_ref, mask_ref, unit_ref, send_ref):
    total = jnp.sum(got_ref[...].astype(F32), axis=0)
    gate = gate_ref[...]
    unit = 2.0 * mask_ref[...] * (x_ref[...].astype(F32) - t_ref[...].astype(F32) + gate * total)
    unit_ref[...] = unit
    dy = (gate * unit).astype(BF16)
    for peer in range(send_ref.shape[0]):
        send_ref[peer, :BLK] = dy
        send_ref[peer, BLK:] = ref_ref[peer]


def miss(got, part_ref, x_own, t_own, gate, mask):
    groups, rows, width = got.shape
    return pl.pallas_call(
        miss_kernel,
        out_shape=[
            jax.ShapeDtypeStruct((rows, width), F32),
            jax.ShapeDtypeStruct((groups, 2 * rows, width), BF16),
        ],
        compiler_params=params(),
        cost_estimate=cost(20 * rows * width, 8 * groups * rows * width),
    )(got, part_ref, x_own, t_own, gate, mask)


def back_kernel(
    got_ref, unit_ref, x_ref, t_ref, gate_ref, mask_ref, own_ref, other_ref, bo_ref, bt_ref, so_ref, st_ref,
    do_ref, dt_ref, dlow_ref, send_ref, turned_scr, straight_scr,
):
    step = pl.program_id(0)
    width = got_ref.shape[2]
    dy = got_ref[:, :BLK].reshape(CAP * BLK, width)
    d_own = (product(dy, own_ref[...]) * so_ref[...]).astype(BF16)
    d_other = (product(dy, other_ref[...]) * st_ref[...]).astype(BF16)
    do_ref[...] = d_own
    dt_ref[...] = d_other
    turned = rows_by_rows(bo_ref[...], d_own) + rows_by_rows(bt_ref[...], d_other)
    straight = rows_by_rows(d_own, bo_ref[...]) + rows_by_rows(d_other, bt_ref[...])

    @pl.when(step == 0)
    def _():
        turned_scr[...] = turned
        straight_scr[...] = straight

    @pl.when(step > 0)
    def _():
        turned_scr[...] += turned
        straight_scr[...] += straight

    @pl.when(step == pl.num_programs(0) - 1)
    def _():
        rank = turned_scr.shape[0]
        dlow_ref[...] = straight_scr[...].astype(BF16)
        mask = mask_ref[...]
        base = x_ref[...].astype(F32) - t_ref[...].astype(F32)
        miss_ref = mask * (base + gate_ref[...] * jnp.sum(got_ref[:, BLK:].astype(F32), axis=0))
        miss_pol = 0.5 * unit_ref[...]
        parts = jnp.sum((miss_pol - miss_ref) * (miss_pol + miss_ref), axis=1, keepdims=True)
        excess = jnp.broadcast_to(jnp.sum(parts, axis=0, keepdims=True), (NOTE, CAP * BLK))
        high = excess.astype(BF16)
        rest = excess - high.astype(F32)
        middle = rest.astype(BF16)
        lowest = rest - middle.astype(F32)
        line = lax.broadcasted_iota(jnp.int32, excess.shape, 0)
        note = jnp.where(line == 0, high.astype(F32), jnp.where(line == 1, middle.astype(F32), lowest)).astype(BF16)
        total = turned_scr[...].astype(BF16)
        for peer in range(send_ref.shape[0]):
            send_ref[peer, :rank] = total
            send_ref[peer, rank:] = note


def backward(got, unit, x_own, t_own, gate, mask, own, other, b_own, b_other, s_own, s_other):
    groups, _, width = got.shape
    half = s_own.shape[1]
    rank = b_own.shape[0]
    rows = CAP * BLK
    step = 256
    weight = pl.BlockSpec((width, step), lambda i: (0, half // step + i))
    factor = pl.BlockSpec((rank, step), lambda i: (0, i))
    cut = pl.BlockSpec((rows, step), lambda i: (0, i))
    block = whole((BLK, width))
    return pl.pallas_call(
        back_kernel,
        grid=(half // step,),
        out_shape=[
            jax.ShapeDtypeStruct((rows, half), BF16),
            jax.ShapeDtypeStruct((rows, half), BF16),
            jax.ShapeDtypeStruct((rows, rank), BF16),
            jax.ShapeDtypeStruct((groups, rank + NOTE, rows), BF16),
        ],
        in_specs=[
            whole(got.shape), block, block, block, whole((1, width)), whole((BLK, 1)),
            weight, weight, factor, factor, cut, cut,
        ],
        out_specs=[cut, cut, whole((rows, rank)), whole((groups, rank + NOTE, rows))],
        scratch_shapes=[pltpu.VMEM((rank, rows), F32), pltpu.VMEM((rows, rank), F32)],
        compiler_params=params(),
        cost_estimate=cost(4 * rows * width * half, 4 * width * half + 12 * rows * half),
    )(got, unit, x_own, t_own, gate, mask, own, other, b_own, b_other, s_own, s_other)


def factor_kernel(split_ref, do_ref, dt_ref, own_ref, other_ref):
    own_ref[...] = product(split_ref[...], do_ref[...])
    other_ref[...] = product(split_ref[...], dt_ref[...])


def factor_terms(split, d_own, d_other):
    lines, rows = split.shape
    half = d_own.shape[1]
    return pl.pallas_call(
        factor_kernel,
        out_shape=[jax.ShapeDtypeStruct((lines, half), F32)] * 2,
        compiler_params=params(),
        cost_estimate=cost(4 * lines * rows * half, 8 * lines * half),
    )(split, d_own, d_other)


def pile_kernel(
    ints_ref, scales_ref, got_ref, modded_ref, own_ref, other_ref, pile_ref, facts_ref
):
    wins = ints_ref[0]
    core = ints_ref[1]
    groups, lines, rows = got_ref.shape
    rank = lines - NOTE
    half = own_ref.shape[1]
    gap_first = jnp.zeros((1, rows), F32)
    gap_second = jnp.zeros((1, rows), F32)
    for slot in range(groups):
        note = got_ref[slot, rank:].astype(F32)
        excess = note[0:1] + note[1:2] + note[2:3]
        gap_first += jnp.where(slot < wins, excess, 0.0)
        gap_second += jnp.where(slot < wins, 0.0, excess)
    scale_first = scales_ref[0]
    scale_second = scales_ref[1]
    inside = -BETA * (gap_first * scale_first - gap_second * scale_second)
    losses = jnp.maximum(-inside, 0.0) + jnp.log1p(jnp.exp(-jnp.abs(inside)))
    weight = BETA * LOSS_SCALE * jax.nn.sigmoid(-inside)
    first = weight * scale_first
    second = -weight * scale_second
    line = lax.broadcasted_iota(jnp.int32, facts_ref.shape, 0)
    facts_ref[...] = jnp.where(line == 0, losses, jnp.where(line == 1, first, second))
    slot = lax.broadcasted_iota(jnp.int32, (1, rows), 1) // BLK
    total = jnp.sum(got_ref[:, :rank].astype(F32), axis=0)
    dlow = (total * jnp.where(slot < wins, first, second)).astype(BF16)
    one = first[:, :1]
    two = second[:, :1]
    near = pl.ds(pl.multiple_of(core * half, 128), half)
    far = pl.ds(pl.multiple_of((1 - core) * half, 128), half)
    pile_ref[:rank, near] = (one * own_ref[:rank] + two * own_ref[rank:]).astype(BF16)
    pile_ref[:rank, far] = (one * other_ref[:rank] + two * other_ref[rank:]).astype(BF16)
    pile_ref[rank:] = product(dlow, modded_ref[...]).astype(BF16)


def piles(ints, scales, got, modded, b_own, b_other):
    lines, half = b_own.shape
    rows, width = modded.shape
    return pl.pallas_call(
        pile_kernel,
        out_shape=[
            jax.ShapeDtypeStruct((lines, width), BF16),
            jax.ShapeDtypeStruct((8, rows), F32),
        ],
        in_specs=[pl.BlockSpec(memory_space=SMEM)] * 2 + [pl.BlockSpec(memory_space=pltpu.VMEM)] * 4,
        compiler_params=params(),
        cost_estimate=cost(lines * width * rows, 16 * lines * half),
    )(ints, scales, got, modded, b_own, b_other)


def dm_kernel(after_ref, do_ref, dt_ref, dlow_ref, own_ref, other_ref, a_ref, out_ref):
    total = rows_by_rows(do_ref[...], own_ref[...]) + rows_by_rows(dt_ref[...], other_ref[...])
    out_ref[...] = (total + product(dlow_ref[...], a_ref[...])).astype(BF16)


def dm_terms(after, d_own, d_other, dlow, own, other, a_turned):
    rows, half = d_own.shape
    width = own.shape[0]
    rank = dlow.shape[1]
    step = 512
    cut = pl.BlockSpec((step, half), lambda i: (i, 0))
    return pl.pallas_call(
        dm_kernel,
        grid=(width // step,),
        out_shape=jax.ShapeDtypeStruct((rows, width), BF16),
        in_specs=[
            pl.BlockSpec(memory_space=pl.ANY),
            whole((rows, half)),
            whole((rows, half)),
            whole((rows, rank)),
            cut,
            cut,
            pl.BlockSpec((rank, step), lambda i: (0, i)),
        ],
        out_specs=pl.BlockSpec((rows, step), lambda i: (0, i)),
        compiler_params=params(),
        cost_estimate=cost(4 * rows * width * half, 4 * width * half + 2 * rows * width),
    )(after, d_own, d_other, dlow, own, other, a_turned)


def token_kernel(one_ref, two_ref, three_ref, four_ref, x_ref, scale_ref, unit_ref, coef_ref, out_ref):
    total = one_ref[...].astype(F32) + two_ref[...].astype(F32)
    total = total + three_ref[...].astype(F32) + four_ref[...].astype(F32)
    normed, inverse = normalise(x_ref[...])
    dn = total * scale_ref[...]
    mean_one = jnp.mean(dn, axis=-1, keepdims=True)
    mean_two = jnp.mean(dn * normed, axis=-1, keepdims=True)
    grad = coef_ref[...] * (unit_ref[...] + inverse * (dn - mean_one - normed * mean_two))
    out_ref[...] = grad.astype(BF16)


def token_gradient(pieces, x_own, scale, unit, coef):
    rows, width = x_own.shape
    return pl.pallas_call(
        token_kernel,
        out_shape=jax.ShapeDtypeStruct((rows, width), BF16),
        compiler_params=params(),
        cost_estimate=cost(20 * rows * width, 20 * rows * width),
    )(*pieces, x_own, scale, unit, coef)


def per_device(
    tokens,
    targets,
    modulation,
    live_block_count,
    preferred_blocks,
    last_block_rows,
    up_rows,
    down_rows,
    factor_in,
    factor_out,
):
    width = tokens.shape[1]
    n_z, n_x, n_c, n_t = (lax.axis_size(a) for a in ("z", "x", "c", "t"))
    n_dp = n_z * n_x * n_c
    core = lax.axis_index("c")
    group = lax.axis_index("t")
    thin, hidden = up_rows.shape
    half = hidden // n_c
    rank = factor_in.shape[1]

    sent = jnp.stack([up_rows.reshape(thin, n_c, half), down_rows.reshape(thin, n_c, half)], axis=2)
    sent = sent.reshape(thin, n_c, 2 * half).transpose(1, 0, 2)
    sent = jnp.broadcast_to(sent[None], (n_x, n_c, thin, 2 * half)).reshape(n_x * n_c, thin, 2 * half)
    near = lax.all_to_all(sent, ("x", "c"), 0, 0, tiled=True).reshape(n_x * n_c * thin, 2 * half)
    own = lax.all_gather(near, "z", axis=0, tiled=True)

    count = live_block_count[0]
    wins = preferred_blocks[0]
    slots = jnp.arange(CAP, dtype=jnp.int32)
    flags = (slots >= wins).astype(jnp.int32)
    last = jnp.where(flags == 0, wins - 1, count - 1)
    tail = jnp.where(flags == 0, last_block_rows[0, 0], last_block_rows[0, 1])
    live = jnp.where(slots < count, jnp.where(slots == last, tail, BLK), 0)
    rows_first = jnp.sum(jnp.where(flags == 0, live, 0)).astype(F32)
    rows_second = jnp.sum(jnp.where(flags == 1, live, 0)).astype(F32)
    scales = 1.0 / (width * jnp.stack([rows_first, rows_second]))

    own_first = group < wins
    x_own = lax.dynamic_slice_in_dim(tokens, group * BLK, BLK, axis=0)
    t_own = lax.dynamic_slice_in_dim(targets, group * BLK, BLK, axis=0)
    vec_own = jnp.where(own_first, modulation[0], modulation[1]).astype(F32)
    live_own = lax.dynamic_slice_in_dim(live, group, 1)
    mask = (jnp.arange(BLK, dtype=jnp.int32)[:, None] < live_own[None, :]).astype(F32)
    gate = vec_own[2:3]
    scale_own = 1.0 + vec_own[1:2]

    a_turned = factor_in.T
    factor_own = lax.dynamic_slice_in_dim(factor_out, core * half, half, axis=1)
    factor_other = lax.dynamic_slice_in_dim(factor_out, (1 - core) * half, half, axis=1)
    modded, low, low_split = prepare(preferred_blocks, tokens, modulation.reshape(6, width), a_turned)

    own = after(own, [modded, low, low_split, factor_own, factor_other, x_own, t_own, gate, scale_own, mask])
    other = lax.ppermute(own, "c", SWAP)

    pol_own, ref_own, slope_own = activate(modded, low, own, factor_own)
    pol_other, ref_other, slope_other = activate(modded, low, other, factor_other)
    part_pol = lower(pol_own, pol_other, own, other).reshape(CAP, BLK, width)
    got_pol = lax.all_to_all(part_pol, "t", 0, 0, tiled=True)
    part_ref = lower(ref_own, ref_other, own, other).reshape(CAP, BLK, width)

    unit, send = miss(got_pol, part_ref, x_own, t_own, gate, mask)
    got_dy = lax.all_to_all(send, "t", 0, 0, tiled=True)
    d_own, d_other, dlow_part, send = backward(
        got_dy, unit, x_own, t_own, gate, mask, own, other, factor_own, factor_other, slope_own, slope_other
    )
    got_low = lax.all_to_all(send, "t", 0, 0, tiled=True)
    b_own, b_other = factor_terms(low_split, d_own, d_other)
    pile, facts = piles(
        jnp.stack([wins, core]).astype(jnp.int32), scales, got_low, modded, b_own, b_other
    )
    losses = facts[0, :1]
    coef_own = jnp.where(own_first, facts[1:2, :1], facts[2:3, :1])

    across = n_x * n_c
    lines = 2 * rank // across
    pieces = lax.all_to_all(pile.reshape(across, lines, width), ("x", "c"), 0, 0, tiled=True)
    pieces = jnp.sum(pieces.astype(F32), axis=0).astype(BF16)
    pieces = lax.all_to_all(pieces.reshape(n_z, lines // n_z, width), "z", 0, 0, tiled=True)
    total = (jnp.sum(pieces.astype(F32), axis=0) / n_dp).astype(BF16)
    total = spread(total, "z", n_z).reshape(lines, width)
    total = spread(total, ("x", "c"), across).reshape(2 * rank, width).astype(F32)
    sum_b = total[:rank]
    sum_a = total[rank:].T

    dm_part = dm_terms(pile, d_own, d_other, dlow_part, own, other, a_turned).reshape(CAP, BLK, width)
    turns = [[(i, (i + step) % n_t) for i in range(n_t)] for step in range(n_t)]
    chunks = [lax.dynamic_index_in_dim(dm_part, (group + step) % n_t, 0, False) for step in range(n_t)]
    chunks = [chunks[0]] + [lax.ppermute(chunks[step], "t", turns[step]) for step in range(1, n_t)]
    grad_block = token_gradient(chunks, x_own, scale_own, unit, coef_own)
    blocks = [grad_block] + [lax.ppermute(grad_block, "t", turns[step]) for step in range(1, n_t)]
    blocks = jnp.stack(blocks)
    grad_tokens = jnp.concatenate(
        [lax.dynamic_index_in_dim(blocks, (group - slot) % n_t, 0, False) for slot in range(n_t)], 0
    )
    return losses, grad_tokens, sum_a, sum_b


def solution(mesh):
    n_dp, n_t = mesh.devices.shape
    fine = Mesh(mesh.devices.reshape(n_dp // 8, 4, 2, n_t), ("z", "x", "c", "t"))
    return jax.shard_map(
        per_device,
        mesh=fine,
        in_specs=(
            P(DP, None),
            P(DP, None),
            P(DP, None, None),
            P(DP),
            P(DP),
            P(DP, None),
            P(DP, "t"),
            P(DP, "t"),
            P(),
            P(None, "t"),
        ),
        out_specs=(P(DP), P(DP, None), P(), P(None, "t")),
        check_vma=False,
    )
```

```python
import jax
import jax.numpy as jnp
from jax import lax
from jax.experimental import pallas as pl
from jax.experimental.pallas import tpu as pltpu
from jax.sharding import Mesh
from jax.sharding import PartitionSpec as P

BLK = 64
CAP = 4
EPS = 1e-06
BETA = 20.0
LOSS_SCALE = 4096.0
ROOT = 0.7978845608028654
CUBE = 0.044715
BF16 = jnp.bfloat16
F32 = jnp.float32
DP = ("z", "x", "c")
CHIPS = ("z", "x")
SWAP = [(0, 1), (1, 0)]
NOTE = 16
VMEM_LIMIT = 40 * 1024 * 1024
SMEM = pltpu.SMEM


def gelu(pre):
    th = jnp.tanh(ROOT * (pre + CUBE * pre * pre * pre))
    return 0.5 * pre * (1.0 + th)


def gelu_and_slope(pre):
    square = pre * pre
    th = jnp.tanh(ROOT * (pre + CUBE * pre * square))
    half = 0.5 * (1.0 + th)
    slope = half + 0.5 * pre * (1.0 - th * th) * (ROOT * (1.0 + 3.0 * CUBE * square))
    return pre * half, slope


def rows_by_rows(left, right):
    return lax.dot_general(left, right, (((1,), (1,)), ((), ())), preferred_element_type=F32)


def product(left, right):
    return jnp.dot(left, right, preferred_element_type=F32)


def spread(value, axes, n):
    return lax.all_to_all(jnp.broadcast_to(value[None], (n, *value.shape)), axes, 0, 0, tiled=True)


def normalise(rows):
    wide = rows.astype(F32)
    center = wide - jnp.mean(wide, axis=-1, keepdims=True)
    inverse = lax.rsqrt(jnp.mean(center * center, axis=-1, keepdims=True) + EPS)
    return center * inverse, inverse


def params():
    return pltpu.CompilerParams(vmem_limit_bytes=VMEM_LIMIT)


def cost(flops, moved, tanh=0):
    return pl.CostEstimate(flops=flops, bytes_accessed=moved, transcendentals=tanh)


def whole(shape):
    return pl.BlockSpec(shape, lambda *_: (0,) * len(shape))


def input_kernel(wins_ref, x_ref, mod_ref, a_ref, modded_ref, low_ref, split_ref):
    wins = wins_ref[0]
    for slot in range(CAP):
        rows = slice(slot * BLK, (slot + 1) * BLK)
        normed, _ = normalise(x_ref[rows])
        first = slot < wins
        shift = jnp.where(first, mod_ref[0:1].astype(F32), mod_ref[3:4].astype(F32))
        scale = 1.0 + jnp.where(first, mod_ref[1:2].astype(F32), mod_ref[4:5].astype(F32))
        modded_ref[rows] = (normed * scale + shift).astype(BF16)
    modded = modded_ref[...]
    low_ref[...] = rows_by_rows(modded, a_ref[...]).astype(BF16)
    turned = rows_by_rows(a_ref[...], modded)
    second = lax.broadcasted_iota(jnp.int32, turned.shape, 1) // BLK >= wins
    rank = turned.shape[0]
    split_ref[:rank] = jnp.where(second, 0.0, turned).astype(BF16)
    split_ref[rank:] = jnp.where(second, turned, 0.0).astype(BF16)


def prepare(wins, tokens, mod, a_turned):
    rows, width = tokens.shape
    rank = a_turned.shape[0]
    return pl.pallas_call(
        input_kernel,
        out_shape=[
            jax.ShapeDtypeStruct((rows, width), BF16),
            jax.ShapeDtypeStruct((rows, rank), BF16),
            jax.ShapeDtypeStruct((2 * rank, rows), BF16),
        ],
        in_specs=[pl.BlockSpec(memory_space=SMEM)] + [pl.BlockSpec(memory_space=pltpu.VMEM)] * 3,
        compiler_params=params(),
        cost_estimate=cost(4 * rows * width * rank, 4 * rows * width),
    )(wins, tokens, mod, a_turned)


def after_kernel(*refs):
    del refs


def after(value, others):
    return pl.pallas_call(
        after_kernel,
        out_shape=jax.ShapeDtypeStruct(value.shape, value.dtype),
        in_specs=[pl.BlockSpec(memory_space=pl.ANY)] * (1 + len(others)),
        out_specs=pl.BlockSpec(memory_space=pl.ANY),
        input_output_aliases={0: 0},
    )(value, *others)


def up_kernel(modded_ref, low_ref, up_ref, b_ref, pol_ref, ref_ref, slope_ref):
    pre_ref = product(modded_ref[...], up_ref[...])
    pre_pol = pre_ref + product(low_ref[...], b_ref[...])
    act, slope = gelu_and_slope(pre_pol)
    pol_ref[...] = act.astype(BF16)
    slope_ref[...] = slope
    ref_ref[...] = gelu(pre_ref).astype(BF16)


def activate(modded, low, weights, factor):
    rows, width = modded.shape
    rank, half = factor.shape
    step = 256
    cut = pl.BlockSpec((rows, step), lambda i: (0, i))
    return pl.pallas_call(
        up_kernel,
        grid=(half // step,),
        out_shape=[
            jax.ShapeDtypeStruct((rows, half), BF16),
            jax.ShapeDtypeStruct((rows, half), BF16),
            jax.ShapeDtypeStruct((rows, half), F32),
        ],
        in_specs=[
            whole((rows, width)),
            whole((rows, rank)),
            pl.BlockSpec((width, step), lambda i: (0, i)),
            pl.BlockSpec((rank, step), lambda i: (0, i)),
        ],
        out_specs=[cut, cut, cut],
        compiler_params=params(),
        cost_estimate=cost(2 * rows * width * half, 2 * width * half + 10 * rows * half, 2 * rows * half),
    )(modded, low, weights, factor)


def down_kernel(left_ref, right_ref, own_ref, other_ref, out_ref):
    total = rows_by_rows(left_ref[...], own_ref[...]) + rows_by_rows(right_ref[...], other_ref[...])
    out_ref[...] = total.astype(BF16)


def lower(left, right, own, other):
    rows, half = left.shape
    width = own.shape[0]
    step = 512
    cut = pl.BlockSpec((step, half), lambda i: (i, 1))
    return pl.pallas_call(
        down_kernel,
        grid=(width // step,),
        out_shape=jax.ShapeDtypeStruct((rows, width), BF16),
        in_specs=[whole((rows, half)), whole((rows, half)), cut, cut],
        out_specs=pl.BlockSpec((rows, step), lambda i: (0, i)),
        compiler_params=params(),
        cost_estimate=cost(4 * rows * width * half, 4 * width * half + 2 * rows * width),
    )(left, right, own, other)


def miss_kernel(got_ref, x_ref, t_ref, gate_ref, mask_ref, unit_ref, dy_ref):
    total = jnp.sum(got_ref[...].astype(F32), axis=0)
    gate = gate_ref[...]
    unit = 2.0 * mask_ref[...] * (x_ref[...].astype(F32) - t_ref[...].astype(F32) + gate * total)
    unit_ref[...] = unit
    dy_ref[...] = (gate * unit).astype(BF16)


def miss(got, x_own, t_own, gate, mask):
    groups, rows, width = got.shape
    return pl.pallas_call(
        miss_kernel,
        out_shape=[
            jax.ShapeDtypeStruct((rows, width), F32),
            jax.ShapeDtypeStruct((rows, width), BF16),
        ],
        compiler_params=params(),
        cost_estimate=cost(20 * rows * width, 4 * groups * rows * width),
    )(got, x_own, t_own, gate, mask)


def back_kernel(
    dy_ref, got_ref, unit_ref, x_ref, t_ref, gate_ref, mask_ref, own_ref, other_ref, bo_ref, bt_ref, so_ref, st_ref,
    do_ref, dt_ref, dlow_ref, send_ref, turned_scr, straight_scr,
):
    step = pl.program_id(0)
    dy = dy_ref[...]
    d_own = (product(dy, own_ref[...]) * so_ref[...]).astype(BF16)
    d_other = (product(dy, other_ref[...]) * st_ref[...]).astype(BF16)
    do_ref[...] = d_own
    dt_ref[...] = d_other
    turned = rows_by_rows(bo_ref[...], d_own) + rows_by_rows(bt_ref[...], d_other)
    straight = rows_by_rows(d_own, bo_ref[...]) + rows_by_rows(d_other, bt_ref[...])

    @pl.when(step == 0)
    def _():
        turned_scr[...] = turned
        straight_scr[...] = straight

    @pl.when(step > 0)
    def _():
        turned_scr[...] += turned
        straight_scr[...] += straight

    @pl.when(step == pl.num_programs(0) - 1)
    def _():
        rank = turned_scr.shape[0]
        dlow_ref[...] = straight_scr[...].astype(BF16)
        mask = mask_ref[...]
        base = x_ref[...].astype(F32) - t_ref[...].astype(F32)
        miss_ref = mask * (base + gate_ref[...] * jnp.sum(got_ref[...].astype(F32), axis=0))
        miss_pol = 0.5 * unit_ref[...]
        parts = jnp.sum((miss_pol - miss_ref) * (miss_pol + miss_ref), axis=1, keepdims=True)
        excess = jnp.broadcast_to(jnp.sum(parts, axis=0, keepdims=True), (NOTE, CAP * BLK))
        high = excess.astype(BF16)
        rest = excess - high.astype(F32)
        middle = rest.astype(BF16)
        lowest = rest - middle.astype(F32)
        line = lax.broadcasted_iota(jnp.int32, excess.shape, 0)
        note = jnp.where(line == 0, high.astype(F32), jnp.where(line == 1, middle.astype(F32), lowest)).astype(BF16)
        total = turned_scr[...].astype(BF16)
        for peer in range(send_ref.shape[0]):
            send_ref[peer, :rank] = total
            send_ref[peer, rank:] = note


def backward(dy, got, unit, x_own, t_own, gate, mask, own, other, b_own, b_other, s_own, s_other):
    groups, _, width = got.shape
    half = s_own.shape[1]
    rank = b_own.shape[0]
    rows = CAP * BLK
    step = 256
    weight = pl.BlockSpec((width, step), lambda i: (0, half // step + i))
    factor = pl.BlockSpec((rank, step), lambda i: (0, i))
    cut = pl.BlockSpec((rows, step), lambda i: (0, i))
    block = whole((BLK, width))
    return pl.pallas_call(
        back_kernel,
        grid=(half // step,),
        out_shape=[
            jax.ShapeDtypeStruct((rows, half), BF16),
            jax.ShapeDtypeStruct((rows, half), BF16),
            jax.ShapeDtypeStruct((rows, rank), BF16),
            jax.ShapeDtypeStruct((groups, rank + NOTE, rows), BF16),
        ],
        in_specs=[
            whole(dy.shape), whole(got.shape), block, block, block, whole((1, width)), whole((BLK, 1)),
            weight, weight, factor, factor, cut, cut,
        ],
        out_specs=[cut, cut, whole((rows, rank)), whole((groups, rank + NOTE, rows))],
        scratch_shapes=[pltpu.VMEM((rank, rows), F32), pltpu.VMEM((rows, rank), F32)],
        compiler_params=params(),
        cost_estimate=cost(4 * rows * width * half, 4 * width * half + 12 * rows * half),
    )(dy, got, unit, x_own, t_own, gate, mask, own, other, b_own, b_other, s_own, s_other)


def factor_kernel(split_ref, do_ref, dt_ref, own_ref, other_ref):
    own_ref[...] = product(split_ref[...], do_ref[...])
    other_ref[...] = product(split_ref[...], dt_ref[...])


def factor_terms(split, d_own, d_other):
    lines, rows = split.shape
    half = d_own.shape[1]
    return pl.pallas_call(
        factor_kernel,
        out_shape=[jax.ShapeDtypeStruct((lines, half), F32)] * 2,
        compiler_params=params(),
        cost_estimate=cost(4 * lines * rows * half, 8 * lines * half),
    )(split, d_own, d_other)


def pile_kernel(
    ints_ref, scales_ref, got_ref, modded_ref, own_ref, other_ref, keep_ref, give_ref, facts_ref
):
    wins = ints_ref[0]
    core = ints_ref[1]
    groups, lines, rows = got_ref.shape
    rank = lines - NOTE
    half = own_ref.shape[1]
    gap_first = jnp.zeros((1, rows), F32)
    gap_second = jnp.zeros((1, rows), F32)
    for slot in range(groups):
        note = got_ref[slot, rank:].astype(F32)
        excess = note[0:1] + note[1:2] + note[2:3]
        gap_first += jnp.where(slot < wins, excess, 0.0)
        gap_second += jnp.where(slot < wins, 0.0, excess)
    scale_first = scales_ref[0]
    scale_second = scales_ref[1]
    inside = -BETA * (gap_first * scale_first - gap_second * scale_second)
    losses = jnp.maximum(-inside, 0.0) + jnp.log1p(jnp.exp(-jnp.abs(inside)))
    weight = BETA * LOSS_SCALE * jax.nn.sigmoid(-inside)
    first = weight * scale_first
    second = -weight * scale_second
    line = lax.broadcasted_iota(jnp.int32, facts_ref.shape, 0)
    facts_ref[...] = jnp.where(line == 0, losses, jnp.where(line == 1, first, second))
    slot = lax.broadcasted_iota(jnp.int32, (1, rows), 1) // BLK
    total = jnp.sum(got_ref[:, :rank].astype(F32), axis=0)
    dlow = (total * jnp.where(slot < wins, first, second)).astype(BF16)
    one = first[:, :1]
    two = second[:, :1]
    near = modded_ref[:, pl.ds(pl.multiple_of(core * half, 128), half)]
    far = modded_ref[:, pl.ds(pl.multiple_of((1 - core) * half, 128), half)]
    keep_ref[:rank] = one * own_ref[:rank] + two * own_ref[rank:]
    keep_ref[rank:] = product(dlow, near)
    give_ref[:rank] = (one * other_ref[:rank] + two * other_ref[rank:]).astype(BF16)
    give_ref[rank:] = product(dlow, far).astype(BF16)


def piles(ints, scales, got, modded, b_own, b_other):
    lines, half = b_own.shape
    rows = got.shape[2]
    return pl.pallas_call(
        pile_kernel,
        out_shape=[
            jax.ShapeDtypeStruct((lines, half), F32),
            jax.ShapeDtypeStruct((lines, half), BF16),
            jax.ShapeDtypeStruct((8, rows), F32),
        ],
        in_specs=[pl.BlockSpec(memory_space=SMEM)] * 2 + [pl.BlockSpec(memory_space=pltpu.VMEM)] * 4,
        compiler_params=params(),
        cost_estimate=cost(2 * lines * half * rows, 16 * lines * half),
    )(ints, scales, got, modded, b_own, b_other)


def dm_kernel(do_ref, dt_ref, dlow_ref, own_ref, other_ref, a_ref, out_ref):
    total = rows_by_rows(do_ref[...], own_ref[...]) + rows_by_rows(dt_ref[...], other_ref[...])
    out_ref[...] = (total + product(dlow_ref[...], a_ref[...])).astype(BF16)


def dm_terms(d_own, d_other, dlow, own, other, a_turned):
    rows, half = d_own.shape
    width = own.shape[0]
    rank = dlow.shape[1]
    step = 512
    cut = pl.BlockSpec((step, half), lambda i: (i, 0))
    return pl.pallas_call(
        dm_kernel,
        grid=(width // step,),
        out_shape=jax.ShapeDtypeStruct((rows, width), BF16),
        in_specs=[
            whole((rows, half)),
            whole((rows, half)),
            whole((rows, rank)),
            cut,
            cut,
            pl.BlockSpec((rank, step), lambda i: (0, i)),
        ],
        out_specs=pl.BlockSpec((rows, step), lambda i: (0, i)),
        compiler_params=params(),
        cost_estimate=cost(4 * rows * width * half, 4 * width * half + 2 * rows * width),
    )(d_own, d_other, dlow, own, other, a_turned)


def token_kernel(one_ref, two_ref, three_ref, four_ref, x_ref, scale_ref, unit_ref, coef_ref, out_ref):
    total = one_ref[...].astype(F32) + two_ref[...].astype(F32)
    total = total + three_ref[...].astype(F32) + four_ref[...].astype(F32)
    normed, inverse = normalise(x_ref[...])
    dn = total * scale_ref[...]
    mean_one = jnp.mean(dn, axis=-1, keepdims=True)
    mean_two = jnp.mean(dn * normed, axis=-1, keepdims=True)
    grad = coef_ref[...] * (unit_ref[...] + inverse * (dn - mean_one - normed * mean_two))
    out_ref[...] = grad.astype(BF16)


def token_gradient(pieces, x_own, scale, unit, coef):
    rows, width = x_own.shape
    return pl.pallas_call(
        token_kernel,
        out_shape=jax.ShapeDtypeStruct((rows, width), BF16),
        compiler_params=params(),
        cost_estimate=cost(20 * rows * width, 20 * rows * width),
    )(*pieces, x_own, scale, unit, coef)


def per_device(
    tokens,
    targets,
    modulation,
    live_block_count,
    preferred_blocks,
    last_block_rows,
    up_rows,
    down_rows,
    factor_in,
    factor_out,
):
    width = tokens.shape[1]
    n_z, n_x, n_c, n_t = (lax.axis_size(a) for a in ("z", "x", "c", "t"))
    n_dp = n_z * n_x * n_c
    core = lax.axis_index("c")
    group = lax.axis_index("t")
    thin, hidden = up_rows.shape
    half = hidden // n_c
    rank = factor_in.shape[1]

    sent = jnp.stack([up_rows.reshape(thin, n_c, half), down_rows.reshape(thin, n_c, half)], axis=2)
    sent = sent.reshape(thin, n_c, 2 * half).transpose(1, 0, 2)
    sent = jnp.broadcast_to(sent[None], (n_x, n_c, thin, 2 * half)).reshape(n_x * n_c, thin, 2 * half)
    near = lax.all_to_all(sent, ("x", "c"), 0, 0, tiled=True).reshape(n_x * n_c * thin, 2 * half)
    own = lax.all_gather(near, "z", axis=0, tiled=True)

    count = live_block_count[0]
    wins = preferred_blocks[0]
    slots = jnp.arange(CAP, dtype=jnp.int32)
    flags = (slots >= wins).astype(jnp.int32)
    last = jnp.where(flags == 0, wins - 1, count - 1)
    tail = jnp.where(flags == 0, last_block_rows[0, 0], last_block_rows[0, 1])
    live = jnp.where(slots < count, jnp.where(slots == last, tail, BLK), 0)
    rows_first = jnp.sum(jnp.where(flags == 0, live, 0)).astype(F32)
    rows_second = jnp.sum(jnp.where(flags == 1, live, 0)).astype(F32)
    scales = 1.0 / (width * jnp.stack([rows_first, rows_second]))

    own_first = group < wins
    x_own = lax.dynamic_slice_in_dim(tokens, group * BLK, BLK, axis=0)
    t_own = lax.dynamic_slice_in_dim(targets, group * BLK, BLK, axis=0)
    vec_own = jnp.where(own_first, modulation[0], modulation[1]).astype(F32)
    live_own = lax.dynamic_slice_in_dim(live, group, 1)
    mask = (jnp.arange(BLK, dtype=jnp.int32)[:, None] < live_own[None, :]).astype(F32)
    gate = vec_own[2:3]
    scale_own = 1.0 + vec_own[1:2]

    a_turned = factor_in.T
    factor_own = lax.dynamic_slice_in_dim(factor_out, core * half, half, axis=1)
    factor_other = lax.dynamic_slice_in_dim(factor_out, (1 - core) * half, half, axis=1)
    modded, low, low_split = prepare(preferred_blocks, tokens, modulation.reshape(6, width), a_turned)

    own = after(own, [modded, low, low_split, factor_own, factor_other, x_own, t_own, gate, scale_own, mask])
    other = lax.ppermute(own, "c", SWAP)

    pol_own, ref_own, slope_own = activate(modded, low, own, factor_own)
    pol_other, ref_other, slope_other = activate(modded, low, other, factor_other)
    part_pol = lower(pol_own, pol_other, own, other).reshape(CAP, BLK, width)
    got_pol = lax.all_to_all(part_pol, "t", 0, 0, tiled=True)
    part_ref = lower(ref_own, ref_other, own, other).reshape(CAP, BLK, width)

    unit, dy = miss(got_pol, x_own, t_own, gate, mask)
    dy = lax.all_gather(dy, "t", axis=0, tiled=True)
    got_ref = lax.all_to_all(part_ref, "t", 0, 0, tiled=True)
    d_own, d_other, dlow_part, send = backward(
        dy, got_ref, unit, x_own, t_own, gate, mask, own, other, factor_own, factor_other, slope_own, slope_other
    )
    got_low = lax.all_to_all(send, "t", 0, 0, tiled=True)
    b_own, b_other = factor_terms(low_split, d_own, d_other)
    dm_part = dm_terms(d_own, d_other, dlow_part, own, other, a_turned)
    keep, give, facts = piles(
        jnp.stack([wins, core]).astype(jnp.int32), scales, got_low, modded, b_own, b_other
    )
    losses = facts[0, :1]
    coef_own = jnp.where(own_first, facts[1:2, :1], facts[2:3, :1])
    pile = (keep + lax.ppermute(give, "c", SWAP).astype(F32)).astype(BF16)

    chips = n_z * n_x
    pieces = lax.all_to_all(pile.reshape(chips, 2 * rank // chips, half), CHIPS, 0, 0, tiled=True)
    total = (jnp.sum(pieces.astype(F32), axis=0) / n_dp).astype(BF16)
    mine = spread(total, CHIPS, chips).reshape(2 * rank, half)
    theirs = lax.ppermute(mine, "c", SWAP)
    ends = jnp.concatenate([mine, theirs], 1)
    flipped = jnp.concatenate([theirs, mine], 1)
    ends = jnp.where(core == 0, ends, flipped).astype(F32)
    sum_b = ends[:rank]
    sum_a = ends[rank:].T

    dm_part = after(dm_part, [pile]).reshape(CAP, BLK, width)
    turns = [[(i, (i + step) % n_t) for i in range(n_t)] for step in range(n_t)]
    chunks = [lax.dynamic_index_in_dim(dm_part, (group + step) % n_t, 0, False) for step in range(n_t)]
    chunks = [chunks[0]] + [lax.ppermute(chunks[step], "t", turns[step]) for step in range(1, n_t)]
    grad_block = token_gradient(chunks, x_own, scale_own, unit, coef_own)
    grad_tokens = lax.all_gather(grad_block, "t", axis=0, tiled=True)
    return losses, grad_tokens, sum_a, sum_b


def solution(mesh):
    n_dp, n_t = mesh.devices.shape
    fine = Mesh(mesh.devices.reshape(n_dp // 8, 4, 2, n_t), ("z", "x", "c", "t"))
    return jax.shard_map(
        per_device,
        mesh=fine,
        in_specs=(
            P(DP, None),
            P(DP, None),
            P(DP, None, None),
            P(DP),
            P(DP),
            P(DP, None),
            P(DP, "t"),
            P(DP, "t"),
            P(),
            P(None, "t"),
        ),
        out_specs=(P(DP), P(DP, None), P(), P(None, "t")),
        check_vma=False,
    )
```

```python
import jax
import jax.numpy as jnp
from jax import lax
from jax.experimental import pallas as pl
from jax.experimental.pallas import tpu as pltpu
from jax.sharding import Mesh
from jax.sharding import PartitionSpec as P

BLK = 64
CAP = 4
EPS = 1e-06
BETA = 20.0
LOSS_SCALE = 4096.0
ROOT = 0.7978845608028654
CUBE = 0.044715
BF16 = jnp.bfloat16
F32 = jnp.float32
DP = ("z", "x", "c")
CHIPS = ("z", "x")
SWAP = [(0, 1), (1, 0)]
NOTE = 16
VMEM_LIMIT = 40 * 1024 * 1024
SMEM = pltpu.SMEM


def gelu(pre):
    th = jnp.tanh(ROOT * (pre + CUBE * pre * pre * pre))
    return 0.5 * pre * (1.0 + th)


def gelu_and_slope(pre):
    square = pre * pre
    th = jnp.tanh(ROOT * (pre + CUBE * pre * square))
    half = 0.5 * (1.0 + th)
    slope = half + 0.5 * pre * (1.0 - th * th) * (ROOT * (1.0 + 3.0 * CUBE * square))
    return pre * half, slope


def rows_by_rows(left, right):
    return lax.dot_general(left, right, (((1,), (1,)), ((), ())), preferred_element_type=F32)


def product(left, right):
    return jnp.dot(left, right, preferred_element_type=F32)


def spread(value, axes, n):
    return lax.all_to_all(jnp.broadcast_to(value[None], (n, *value.shape)), axes, 0, 0, tiled=True)


def around(block, n):
    here = lax.axis_index("z")
    up = [(i, (i + 1) % n) for i in range(n)]
    down = [(i, (i - 1) % n) for i in range(n)]
    found = lax.dynamic_update_index_in_dim(jnp.zeros((n, *block.shape), block.dtype), block, here, 0)
    left = right = block
    for step in range(1, n // 2 + 1):
        left = lax.ppermute(left, "z", up)
        found = lax.dynamic_update_index_in_dim(found, left, (here - step) % n, 0)
        if step < n // 2:
            right = lax.ppermute(right, "z", down)
            found = lax.dynamic_update_index_in_dim(found, right, (here + step) % n, 0)
    return found


def normalise(rows):
    wide = rows.astype(F32)
    center = wide - jnp.mean(wide, axis=-1, keepdims=True)
    inverse = lax.rsqrt(jnp.mean(center * center, axis=-1, keepdims=True) + EPS)
    return center * inverse, inverse


def params():
    return pltpu.CompilerParams(vmem_limit_bytes=VMEM_LIMIT)


def cost(flops, moved, tanh=0):
    return pl.CostEstimate(flops=flops, bytes_accessed=moved, transcendentals=tanh)


def whole(shape):
    return pl.BlockSpec(shape, lambda *_: (0,) * len(shape))


def input_kernel(wins_ref, x_ref, mod_ref, a_ref, modded_ref, low_ref, split_ref):
    wins = wins_ref[0]
    for slot in range(CAP):
        rows = slice(slot * BLK, (slot + 1) * BLK)
        normed, _ = normalise(x_ref[rows])
        first = slot < wins
        shift = jnp.where(first, mod_ref[0:1].astype(F32), mod_ref[3:4].astype(F32))
        scale = 1.0 + jnp.where(first, mod_ref[1:2].astype(F32), mod_ref[4:5].astype(F32))
        modded_ref[rows] = (normed * scale + shift).astype(BF16)
    modded = modded_ref[...]
    low_ref[...] = rows_by_rows(modded, a_ref[...]).astype(BF16)
    turned = rows_by_rows(a_ref[...], modded)
    second = lax.broadcasted_iota(jnp.int32, turned.shape, 1) // BLK >= wins
    rank = turned.shape[0]
    split_ref[:rank] = jnp.where(second, 0.0, turned).astype(BF16)
    split_ref[rank:] = jnp.where(second, turned, 0.0).astype(BF16)


def prepare(wins, tokens, mod, a_turned):
    rows, width = tokens.shape
    rank = a_turned.shape[0]
    return pl.pallas_call(
        input_kernel,
        out_shape=[
            jax.ShapeDtypeStruct((rows, width), BF16),
            jax.ShapeDtypeStruct((rows, rank), BF16),
            jax.ShapeDtypeStruct((2 * rank, rows), BF16),
        ],
        in_specs=[pl.BlockSpec(memory_space=SMEM)] + [pl.BlockSpec(memory_space=pltpu.VMEM)] * 3,
        compiler_params=params(),
        cost_estimate=cost(4 * rows * width * rank, 4 * rows * width),
    )(wins, tokens, mod, a_turned)


def after_kernel(*refs):
    del refs


def after(value, others):
    return pl.pallas_call(
        after_kernel,
        out_shape=jax.ShapeDtypeStruct(value.shape, value.dtype),
        in_specs=[pl.BlockSpec(memory_space=pl.ANY)] * (1 + len(others)),
        out_specs=pl.BlockSpec(memory_space=pl.ANY),
        input_output_aliases={0: 0},
    )(value, *others)


def up_kernel(modded_ref, low_ref, up_ref, b_ref, pol_ref, ref_ref, slope_ref):
    pre_ref = product(modded_ref[...], up_ref[...])
    pre_pol = pre_ref + product(low_ref[...], b_ref[...])
    act, slope = gelu_and_slope(pre_pol)
    pol_ref[...] = act.astype(BF16)
    slope_ref[...] = slope
    ref_ref[...] = gelu(pre_ref).astype(BF16)


def activate(modded, low, weights, factor):
    rows, width = modded.shape
    rank, half = factor.shape
    step = 256
    cut = pl.BlockSpec((rows, step), lambda i: (0, i))
    return pl.pallas_call(
        up_kernel,
        grid=(half // step,),
        out_shape=[
            jax.ShapeDtypeStruct((rows, half), BF16),
            jax.ShapeDtypeStruct((rows, half), BF16),
            jax.ShapeDtypeStruct((rows, half), F32),
        ],
        in_specs=[
            whole((rows, width)),
            whole((rows, rank)),
            pl.BlockSpec((width, step), lambda i: (0, i)),
            pl.BlockSpec((rank, step), lambda i: (0, i)),
        ],
        out_specs=[cut, cut, cut],
        compiler_params=params(),
        cost_estimate=cost(2 * rows * width * half, 2 * width * half + 10 * rows * half, 2 * rows * half),
    )(modded, low, weights, factor)


def down_kernel(left_ref, right_ref, own_ref, other_ref, out_ref):
    total = rows_by_rows(left_ref[...], own_ref[...]) + rows_by_rows(right_ref[...], other_ref[...])
    out_ref[...] = total.astype(BF16)


def lower(left, right, own, other):
    rows, half = left.shape
    width = own.shape[0]
    step = 512
    cut = pl.BlockSpec((step, half), lambda i: (i, 1))
    return pl.pallas_call(
        down_kernel,
        grid=(width // step,),
        out_shape=jax.ShapeDtypeStruct((rows, width), BF16),
        in_specs=[whole((rows, half)), whole((rows, half)), cut, cut],
        out_specs=pl.BlockSpec((rows, step), lambda i: (0, i)),
        compiler_params=params(),
        cost_estimate=cost(4 * rows * width * half, 4 * width * half + 2 * rows * width),
    )(left, right, own, other)


def miss_kernel(got_ref, ref_ref, x_ref, t_ref, gate_ref, mask_ref, unit_ref, send_ref):
    total = jnp.sum(got_ref[...].astype(F32), axis=0)
    gate = gate_ref[...]
    unit = 2.0 * mask_ref[...] * (x_ref[...].astype(F32) - t_ref[...].astype(F32) + gate * total)
    unit_ref[...] = unit
    dy = (gate * unit).astype(BF16)
    for peer in range(send_ref.shape[0]):
        send_ref[peer, :BLK] = dy
        send_ref[peer, BLK:] = ref_ref[peer]


def miss(got, part_ref, x_own, t_own, gate, mask):
    groups, rows, width = got.shape
    return pl.pallas_call(
        miss_kernel,
        out_shape=[
            jax.ShapeDtypeStruct((rows, width), F32),
            jax.ShapeDtypeStruct((groups, 2 * rows, width), BF16),
        ],
        compiler_params=params(),
        cost_estimate=cost(20 * rows * width, 8 * groups * rows * width),
    )(got, part_ref, x_own, t_own, gate, mask)


def back_kernel(
    got_ref, unit_ref, x_ref, t_ref, gate_ref, mask_ref, own_ref, other_ref, bo_ref, bt_ref, so_ref, st_ref,
    do_ref, dt_ref, dlow_ref, send_ref, turned_scr, straight_scr,
):
    step = pl.program_id(0)
    width = got_ref.shape[2]
    dy = got_ref[:, :BLK].reshape(CAP * BLK, width)
    d_own = (product(dy, own_ref[...]) * so_ref[...]).astype(BF16)
    d_other = (product(dy, other_ref[...]) * st_ref[...]).astype(BF16)
    do_ref[...] = d_own
    dt_ref[...] = d_other
    turned = rows_by_rows(bo_ref[...], d_own) + rows_by_rows(bt_ref[...], d_other)
    straight = rows_by_rows(d_own, bo_ref[...]) + rows_by_rows(d_other, bt_ref[...])

    @pl.when(step == 0)
    def _():
        turned_scr[...] = turned
        straight_scr[...] = straight

    @pl.when(step > 0)
    def _():
        turned_scr[...] += turned
        straight_scr[...] += straight

    @pl.when(step == pl.num_programs(0) - 1)
    def _():
        rank = turned_scr.shape[0]
        dlow_ref[...] = straight_scr[...].astype(BF16)
        mask = mask_ref[...]
        base = x_ref[...].astype(F32) - t_ref[...].astype(F32)
        miss_ref = mask * (base + gate_ref[...] * jnp.sum(got_ref[:, BLK:].astype(F32), axis=0))
        miss_pol = 0.5 * unit_ref[...]
        parts = jnp.sum((miss_pol - miss_ref) * (miss_pol + miss_ref), axis=1, keepdims=True)
        excess = jnp.broadcast_to(jnp.sum(parts, axis=0, keepdims=True), (NOTE, CAP * BLK))
        high = excess.astype(BF16)
        rest = excess - high.astype(F32)
        middle = rest.astype(BF16)
        lowest = rest - middle.astype(F32)
        line = lax.broadcasted_iota(jnp.int32, excess.shape, 0)
        note = jnp.where(line == 0, high.astype(F32), jnp.where(line == 1, middle.astype(F32), lowest)).astype(BF16)
        total = turned_scr[...].astype(BF16)
        for peer in range(send_ref.shape[0]):
            send_ref[peer, :rank] = total
            send_ref[peer, rank:] = note


def backward(got, unit, x_own, t_own, gate, mask, own, other, b_own, b_other, s_own, s_other):
    groups, _, width = got.shape
    half = s_own.shape[1]
    rank = b_own.shape[0]
    rows = CAP * BLK
    step = 256
    weight = pl.BlockSpec((width, step), lambda i: (0, half // step + i))
    factor = pl.BlockSpec((rank, step), lambda i: (0, i))
    cut = pl.BlockSpec((rows, step), lambda i: (0, i))
    block = whole((BLK, width))
    return pl.pallas_call(
        back_kernel,
        grid=(half // step,),
        out_shape=[
            jax.ShapeDtypeStruct((rows, half), BF16),
            jax.ShapeDtypeStruct((rows, half), BF16),
            jax.ShapeDtypeStruct((rows, rank), BF16),
            jax.ShapeDtypeStruct((groups, rank + NOTE, rows), BF16),
        ],
        in_specs=[
            whole(got.shape), block, block, block, whole((1, width)), whole((BLK, 1)),
            weight, weight, factor, factor, cut, cut,
        ],
        out_specs=[cut, cut, whole((rows, rank)), whole((groups, rank + NOTE, rows))],
        scratch_shapes=[pltpu.VMEM((rank, rows), F32), pltpu.VMEM((rows, rank), F32)],
        compiler_params=params(),
        cost_estimate=cost(4 * rows * width * half, 4 * width * half + 12 * rows * half),
    )(got, unit, x_own, t_own, gate, mask, own, other, b_own, b_other, s_own, s_other)


def factor_kernel(split_ref, do_ref, dt_ref, own_ref, other_ref):
    own_ref[...] = product(split_ref[...], do_ref[...])
    other_ref[...] = product(split_ref[...], dt_ref[...])


def factor_terms(split, d_own, d_other):
    lines, rows = split.shape
    half = d_own.shape[1]
    return pl.pallas_call(
        factor_kernel,
        out_shape=[jax.ShapeDtypeStruct((lines, half), F32)] * 2,
        compiler_params=params(),
        cost_estimate=cost(4 * lines * rows * half, 8 * lines * half),
    )(split, d_own, d_other)


def pile_kernel(
    ints_ref, scales_ref, got_ref, modded_ref, own_ref, other_ref, keep_ref, give_ref, facts_ref
):
    wins = ints_ref[0]
    core = ints_ref[1]
    groups, lines, rows = got_ref.shape
    rank = lines - NOTE
    half = own_ref.shape[1]
    gap_first = jnp.zeros((1, rows), F32)
    gap_second = jnp.zeros((1, rows), F32)
    for slot in range(groups):
        note = got_ref[slot, rank:].astype(F32)
        excess = note[0:1] + note[1:2] + note[2:3]
        gap_first += jnp.where(slot < wins, excess, 0.0)
        gap_second += jnp.where(slot < wins, 0.0, excess)
    scale_first = scales_ref[0]
    scale_second = scales_ref[1]
    inside = -BETA * (gap_first * scale_first - gap_second * scale_second)
    losses = jnp.maximum(-inside, 0.0) + jnp.log1p(jnp.exp(-jnp.abs(inside)))
    weight = BETA * LOSS_SCALE * jax.nn.sigmoid(-inside)
    first = weight * scale_first
    second = -weight * scale_second
    line = lax.broadcasted_iota(jnp.int32, facts_ref.shape, 0)
    facts_ref[...] = jnp.where(line == 0, losses, jnp.where(line == 1, first, second))
    slot = lax.broadcasted_iota(jnp.int32, (1, rows), 1) // BLK
    total = jnp.sum(got_ref[:, :rank].astype(F32), axis=0)
    dlow = (total * jnp.where(slot < wins, first, second)).astype(BF16)
    one = first[:, :1]
    two = second[:, :1]
    near = modded_ref[:, pl.ds(pl.multiple_of(core * half, 128), half)]
    far = modded_ref[:, pl.ds(pl.multiple_of((1 - core) * half, 128), half)]
    keep_ref[:rank] = one * own_ref[:rank] + two * own_ref[rank:]
    keep_ref[rank:] = product(dlow, near)
    give_ref[:rank] = (one * other_ref[:rank] + two * other_ref[rank:]).astype(BF16)
    give_ref[rank:] = product(dlow, far).astype(BF16)


def piles(ints, scales, got, modded, b_own, b_other):
    lines, half = b_own.shape
    rows = got.shape[2]
    return pl.pallas_call(
        pile_kernel,
        out_shape=[
            jax.ShapeDtypeStruct((lines, half), F32),
            jax.ShapeDtypeStruct((lines, half), BF16),
            jax.ShapeDtypeStruct((8, rows), F32),
        ],
        in_specs=[pl.BlockSpec(memory_space=SMEM)] * 2 + [pl.BlockSpec(memory_space=pltpu.VMEM)] * 4,
        compiler_params=params(),
        cost_estimate=cost(2 * lines * half * rows, 16 * lines * half),
    )(ints, scales, got, modded, b_own, b_other)


def dm_kernel(after_ref, do_ref, dt_ref, dlow_ref, own_ref, other_ref, a_ref, out_ref):
    total = rows_by_rows(do_ref[...], own_ref[...]) + rows_by_rows(dt_ref[...], other_ref[...])
    out_ref[...] = (total + product(dlow_ref[...], a_ref[...])).astype(BF16)


def dm_terms(after, d_own, d_other, dlow, own, other, a_turned):
    rows, half = d_own.shape
    width = own.shape[0]
    rank = dlow.shape[1]
    step = 512
    cut = pl.BlockSpec((step, half), lambda i: (i, 0))
    return pl.pallas_call(
        dm_kernel,
        grid=(width // step,),
        out_shape=jax.ShapeDtypeStruct((rows, width), BF16),
        in_specs=[
            pl.BlockSpec(memory_space=pl.ANY),
            whole((rows, half)),
            whole((rows, half)),
            whole((rows, rank)),
            cut,
            cut,
            pl.BlockSpec((rank, step), lambda i: (0, i)),
        ],
        out_specs=pl.BlockSpec((rows, step), lambda i: (0, i)),
        compiler_params=params(),
        cost_estimate=cost(4 * rows * width * half, 4 * width * half + 2 * rows * width),
    )(after, d_own, d_other, dlow, own, other, a_turned)


def token_kernel(one_ref, two_ref, three_ref, four_ref, x_ref, scale_ref, unit_ref, coef_ref, out_ref):
    total = one_ref[...].astype(F32) + two_ref[...].astype(F32)
    total = total + three_ref[...].astype(F32) + four_ref[...].astype(F32)
    normed, inverse = normalise(x_ref[...])
    dn = total * scale_ref[...]
    mean_one = jnp.mean(dn, axis=-1, keepdims=True)
    mean_two = jnp.mean(dn * normed, axis=-1, keepdims=True)
    grad = coef_ref[...] * (unit_ref[...] + inverse * (dn - mean_one - normed * mean_two))
    out_ref[...] = grad.astype(BF16)


def token_gradient(pieces, x_own, scale, unit, coef):
    rows, width = x_own.shape
    return pl.pallas_call(
        token_kernel,
        out_shape=jax.ShapeDtypeStruct((rows, width), BF16),
        compiler_params=params(),
        cost_estimate=cost(20 * rows * width, 20 * rows * width),
    )(*pieces, x_own, scale, unit, coef)


def per_device(
    tokens,
    targets,
    modulation,
    live_block_count,
    preferred_blocks,
    last_block_rows,
    up_rows,
    down_rows,
    factor_in,
    factor_out,
):
    width = tokens.shape[1]
    n_z, n_x, n_c, n_t = (lax.axis_size(a) for a in ("z", "x", "c", "t"))
    n_dp = n_z * n_x * n_c
    core = lax.axis_index("c")
    group = lax.axis_index("t")
    thin, hidden = up_rows.shape
    half = hidden // n_c
    rank = factor_in.shape[1]

    sent = jnp.stack([up_rows.reshape(thin, n_c, half), down_rows.reshape(thin, n_c, half)], axis=2)
    sent = sent.reshape(thin, n_c, 2 * half).transpose(1, 0, 2)
    sent = jnp.broadcast_to(sent[None], (n_x, n_c, thin, 2 * half)).reshape(n_x * n_c, thin, 2 * half)
    near = lax.all_to_all(sent, ("x", "c"), 0, 0, tiled=True).reshape(n_x * n_c * thin, 2 * half)

    count = live_block_count[0]
    wins = preferred_blocks[0]
    slots = jnp.arange(CAP, dtype=jnp.int32)
    flags = (slots >= wins).astype(jnp.int32)
    last = jnp.where(flags == 0, wins - 1, count - 1)
    tail = jnp.where(flags == 0, last_block_rows[0, 0], last_block_rows[0, 1])
    live = jnp.where(slots < count, jnp.where(slots == last, tail, BLK), 0)
    rows_first = jnp.sum(jnp.where(flags == 0, live, 0)).astype(F32)
    rows_second = jnp.sum(jnp.where(flags == 1, live, 0)).astype(F32)
    scales = 1.0 / (width * jnp.stack([rows_first, rows_second]))

    own_first = group < wins
    x_own = lax.dynamic_slice_in_dim(tokens, group * BLK, BLK, axis=0)
    t_own = lax.dynamic_slice_in_dim(targets, group * BLK, BLK, axis=0)
    vec_own = jnp.where(own_first, modulation[0], modulation[1]).astype(F32)
    live_own = lax.dynamic_slice_in_dim(live, group, 1)
    mask = (jnp.arange(BLK, dtype=jnp.int32)[:, None] < live_own[None, :]).astype(F32)
    gate = vec_own[2:3]
    scale_own = 1.0 + vec_own[1:2]

    a_turned = factor_in.T
    factor_own = lax.dynamic_slice_in_dim(factor_out, core * half, half, axis=1)
    factor_other = lax.dynamic_slice_in_dim(factor_out, (1 - core) * half, half, axis=1)
    modded, low, low_split = prepare(preferred_blocks, tokens, modulation.reshape(6, width), a_turned)

    near = after(near, [modded, low, low_split, factor_own, factor_other, x_own, t_own, gate, scale_own, mask])
    own = around(near, n_z).reshape(width, 2 * half)
    other = lax.ppermute(own, "c", SWAP)

    pol_own, ref_own, slope_own = activate(modded, low, own, factor_own)
    pol_other, ref_other, slope_other = activate(modded, low, other, factor_other)
    part_pol = lower(pol_own, pol_other, own, other).reshape(CAP, BLK, width)
    got_pol = lax.all_to_all(part_pol, "t", 0, 0, tiled=True)
    part_ref = lower(ref_own, ref_other, own, other).reshape(CAP, BLK, width)

    unit, send = miss(got_pol, part_ref, x_own, t_own, gate, mask)
    got_dy = lax.all_to_all(send, "t", 0, 0, tiled=True)
    d_own, d_other, dlow_part, send = backward(
        got_dy, unit, x_own, t_own, gate, mask, own, other, factor_own, factor_other, slope_own, slope_other
    )
    got_low = lax.all_to_all(send, "t", 0, 0, tiled=True)
    b_own, b_other = factor_terms(low_split, d_own, d_other)
    keep, give, facts = piles(
        jnp.stack([wins, core]).astype(jnp.int32), scales, got_low, modded, b_own, b_other
    )
    losses = facts[0, :1]
    coef_own = jnp.where(own_first, facts[1:2, :1], facts[2:3, :1])
    pile = (keep + lax.ppermute(give, "c", SWAP).astype(F32)).astype(BF16)

    chips = n_z * n_x
    pieces = lax.all_to_all(pile.reshape(chips, 2 * rank // chips, half), CHIPS, 0, 0, tiled=True)
    total = (jnp.sum(pieces.astype(F32), axis=0) / n_dp).astype(BF16)
    mine = spread(total, CHIPS, chips).reshape(2 * rank, half)
    theirs = lax.ppermute(mine, "c", SWAP)
    ends = jnp.concatenate([mine, theirs], 1)
    flipped = jnp.concatenate([theirs, mine], 1)
    ends = jnp.where(core == 0, ends, flipped).astype(F32)
    sum_b = ends[:rank]
    sum_a = ends[rank:].T

    dm_part = dm_terms(pile, d_own, d_other, dlow_part, own, other, a_turned).reshape(CAP, BLK, width)
    turns = [[(i, (i + step) % n_t) for i in range(n_t)] for step in range(n_t)]
    chunks = [lax.dynamic_index_in_dim(dm_part, (group + step) % n_t, 0, False) for step in range(n_t)]
    chunks = [chunks[0]] + [lax.ppermute(chunks[step], "t", turns[step]) for step in range(1, n_t)]
    grad_block = token_gradient(chunks, x_own, scale_own, unit, coef_own)
    blocks = [grad_block] + [lax.ppermute(grad_block, "t", turns[step]) for step in range(1, n_t)]
    blocks = jnp.stack(blocks)
    grad_tokens = jnp.concatenate(
        [lax.dynamic_index_in_dim(blocks, (group - slot) % n_t, 0, False) for slot in range(n_t)], 0
    )
    return losses, grad_tokens, sum_a, sum_b


def solution(mesh):
    n_dp, n_t = mesh.devices.shape
    fine = Mesh(mesh.devices.reshape(n_dp // 8, 4, 2, n_t), ("z", "x", "c", "t"))
    return jax.shard_map(
        per_device,
        mesh=fine,
        in_specs=(
            P(DP, None),
            P(DP, None),
            P(DP, None, None),
            P(DP),
            P(DP),
            P(DP, None),
            P(DP, "t"),
            P(DP, "t"),
            P(),
            P(None, "t"),
        ),
        out_specs=(P(DP), P(DP, None), P(), P(None, "t")),
        check_vma=False,
    )
```

```python
import functools

import jax
import jax.numpy as jnp
from jax import lax
from jax.experimental import pallas as pl
from jax.experimental.pallas import tpu as pltpu
from jax.sharding import Mesh
from jax.sharding import PartitionSpec as P

BLK = 64
CAP = 4
EPS = 1e-06
BETA = 20.0
LOSS_SCALE = 4096.0
ROOT = 0.7978845608028654
CUBE = 0.044715
BF16 = jnp.bfloat16
F32 = jnp.float32
DP = ("z", "x", "c")
CHIPS = ("z", "x")
SWAP = [(0, 1), (1, 0)]
NOTE = 16
VMEM_LIMIT = 40 * 1024 * 1024
SMEM = pltpu.SMEM


def gelu(pre):
    th = jnp.tanh(ROOT * (pre + CUBE * pre * pre * pre))
    return 0.5 * pre * (1.0 + th)


def gelu_and_slope(pre):
    square = pre * pre
    th = jnp.tanh(ROOT * (pre + CUBE * pre * square))
    half = 0.5 * (1.0 + th)
    slope = half + 0.5 * pre * (1.0 - th * th) * (ROOT * (1.0 + 3.0 * CUBE * square))
    return pre * half, slope


def rows_by_rows(left, right):
    return lax.dot_general(left, right, (((1,), (1,)), ((), ())), preferred_element_type=F32)


def product(left, right):
    return jnp.dot(left, right, preferred_element_type=F32)


def spread(value, axes, n):
    return lax.all_to_all(jnp.broadcast_to(value[None], (n, *value.shape)), axes, 0, 0, tiled=True)


def around(block, n):
    here = lax.axis_index("z")
    up = [(i, (i + 1) % n) for i in range(n)]
    down = [(i, (i - 1) % n) for i in range(n)]
    found = lax.dynamic_update_index_in_dim(jnp.zeros((n, *block.shape), block.dtype), block, here, 0)
    left = right = block
    for step in range(1, n // 2 + 1):
        left = lax.ppermute(left, "z", up)
        found = lax.dynamic_update_index_in_dim(found, left, (here - step) % n, 0)
        if step < n // 2:
            right = lax.ppermute(right, "z", down)
            found = lax.dynamic_update_index_in_dim(found, right, (here + step) % n, 0)
    return found


def normalise(rows):
    wide = rows.astype(F32)
    center = wide - jnp.mean(wide, axis=-1, keepdims=True)
    inverse = lax.rsqrt(jnp.mean(center * center, axis=-1, keepdims=True) + EPS)
    return center * inverse, inverse


def params():
    return pltpu.CompilerParams(vmem_limit_bytes=VMEM_LIMIT)


def cost(flops, moved, tanh=0):
    return pl.CostEstimate(flops=flops, bytes_accessed=moved, transcendentals=tanh)


def whole(shape):
    return pl.BlockSpec(shape, lambda *_: (0,) * len(shape))


def input_kernel(wins_ref, x_ref, mod_ref, a_ref, modded_ref, low_ref, split_ref):
    wins = wins_ref[0]
    for slot in range(CAP):
        rows = slice(slot * BLK, (slot + 1) * BLK)
        normed, _ = normalise(x_ref[rows])
        first = slot < wins
        shift = jnp.where(first, mod_ref[0:1].astype(F32), mod_ref[3:4].astype(F32))
        scale = 1.0 + jnp.where(first, mod_ref[1:2].astype(F32), mod_ref[4:5].astype(F32))
        modded_ref[rows] = (normed * scale + shift).astype(BF16)
    modded = modded_ref[...]
    low_ref[...] = rows_by_rows(modded, a_ref[...]).astype(BF16)
    turned = rows_by_rows(a_ref[...], modded)
    second = lax.broadcasted_iota(jnp.int32, turned.shape, 1) // BLK >= wins
    rank = turned.shape[0]
    split_ref[:rank] = jnp.where(second, 0.0, turned).astype(BF16)
    split_ref[rank:] = jnp.where(second, turned, 0.0).astype(BF16)


def prepare(wins, tokens, mod, a_turned):
    rows, width = tokens.shape
    rank = a_turned.shape[0]
    return pl.pallas_call(
        input_kernel,
        out_shape=[
            jax.ShapeDtypeStruct((rows, width), BF16),
            jax.ShapeDtypeStruct((rows, rank), BF16),
            jax.ShapeDtypeStruct((2 * rank, rows), BF16),
        ],
        in_specs=[pl.BlockSpec(memory_space=SMEM)] + [pl.BlockSpec(memory_space=pltpu.VMEM)] * 3,
        compiler_params=params(),
        cost_estimate=cost(4 * rows * width * rank, 4 * rows * width),
    )(wins, tokens, mod, a_turned)


def own_slot(ints_ref):
    wins, count, slot = ints_ref[0], ints_ref[1], ints_ref[4]
    first = slot < wins
    last = jnp.where(first, wins - 1, count - 1)
    tail = jnp.where(first, ints_ref[2], ints_ref[3])
    return first, jnp.where(slot < count, jnp.where(slot == last, tail, BLK), 0)


def pick(first, ref, line):
    return jnp.where(first, ref[line : line + 1].astype(F32), ref[line + 3 : line + 4].astype(F32))


def after_kernel(*refs):
    del refs


def after(value, others):
    return pl.pallas_call(
        after_kernel,
        out_shape=jax.ShapeDtypeStruct(value.shape, value.dtype),
        in_specs=[pl.BlockSpec(memory_space=pl.ANY)] * (1 + len(others)),
        out_specs=pl.BlockSpec(memory_space=pl.ANY),
        input_output_aliases={0: 0},
    )(value, *others)


def half_of(core, step, half, size):
    return pl.ds(pl.multiple_of(core * half + step * size, 128), size)


def up_kernel(far, ints_ref, modded_ref, low_ref, up_ref, b_ref, pol_ref, ref_ref, slope_ref):
    core = 1 - ints_ref[5] if far else ints_ref[5]
    size = up_ref.shape[1]
    cut = half_of(core, pl.program_id(0), size * pl.num_programs(0), size)
    pre_ref = product(modded_ref[...], up_ref[...])
    pre_pol = pre_ref + product(low_ref[...], b_ref[:, cut])
    act, slope = gelu_and_slope(pre_pol)
    pol_ref[...] = act.astype(BF16)
    slope_ref[...] = slope.astype(BF16)
    ref_ref[...] = gelu(pre_ref).astype(BF16)


def activate(far, ints, modded, low, weights, factor):
    rows, width = modded.shape
    rank = factor.shape[0]
    half = factor.shape[1] // 2
    step = 256
    cut = pl.BlockSpec((rows, step), lambda i: (0, i))
    return pl.pallas_call(
        functools.partial(up_kernel, far),
        grid=(half // step,),
        out_shape=[
            jax.ShapeDtypeStruct((rows, half), BF16),
            jax.ShapeDtypeStruct((rows, half), BF16),
            jax.ShapeDtypeStruct((rows, half), BF16),
        ],
        in_specs=[
            pl.BlockSpec(memory_space=SMEM),
            whole((rows, width)),
            whole((rows, rank)),
            pl.BlockSpec((width, step), lambda i: (0, i)),
            whole(factor.shape),
        ],
        out_specs=[cut, cut, cut],
        compiler_params=params(),
        cost_estimate=cost(2 * rows * width * half, 2 * width * half + 10 * rows * half, 2 * rows * half),
    )(ints, modded, low, weights, factor)


def down_kernel(left_ref, right_ref, own_ref, other_ref, out_ref):
    total = rows_by_rows(left_ref[...], own_ref[...]) + rows_by_rows(right_ref[...], other_ref[...])
    out_ref[...] = total.astype(BF16)


def lower(left, right, own, other):
    rows, half = left.shape
    width = own.shape[0]
    step = 512
    cut = pl.BlockSpec((step, half), lambda i: (i, 1))
    return pl.pallas_call(
        down_kernel,
        grid=(width // step,),
        out_shape=jax.ShapeDtypeStruct((rows, width), BF16),
        in_specs=[whole((rows, half)), whole((rows, half)), cut, cut],
        out_specs=pl.BlockSpec((rows, step), lambda i: (0, i)),
        compiler_params=params(),
        cost_estimate=cost(4 * rows * width * half, 4 * width * half + 2 * rows * width),
    )(left, right, own, other)


def miss_kernel(ints_ref, got_ref, ref_ref, x_ref, t_ref, mod_ref, unit_ref, send_ref):
    first, live = own_slot(ints_ref)
    total = jnp.sum(got_ref[...].astype(F32), axis=0)
    gate = pick(first, mod_ref, 2)
    unit = 2.0 * (x_ref[...].astype(F32) - t_ref[...].astype(F32) + gate * total)
    unit = jnp.where(lax.broadcasted_iota(jnp.int32, unit.shape, 0) < live, unit, 0.0)
    unit_ref[...] = unit
    dy = (gate * unit).astype(BF16)
    for peer in range(send_ref.shape[0]):
        send_ref[peer, :BLK] = dy
        send_ref[peer, BLK:] = ref_ref[peer]


def miss(ints, got, part_ref, x_own, t_own, mod):
    groups, rows, width = got.shape
    return pl.pallas_call(
        miss_kernel,
        out_shape=[
            jax.ShapeDtypeStruct((rows, width), F32),
            jax.ShapeDtypeStruct((groups, 2 * rows, width), BF16),
        ],
        in_specs=[pl.BlockSpec(memory_space=SMEM)] + [pl.BlockSpec(memory_space=pltpu.VMEM)] * 5,
        compiler_params=params(),
        cost_estimate=cost(20 * rows * width, 8 * groups * rows * width),
    )(ints, got, part_ref, x_own, t_own, mod)


def back_kernel(
    ints_ref, got_ref, unit_ref, x_ref, t_ref, mod_ref, own_ref, other_ref, b_ref, so_ref, st_ref,
    do_ref, dt_ref, dlow_ref, send_ref, turned_scr, straight_scr,
):
    step = pl.program_id(0)
    core = ints_ref[5]
    width = got_ref.shape[2]
    size = so_ref.shape[1]
    half = size * pl.num_programs(0)
    b_own = b_ref[:, half_of(core, step, half, size)]
    b_other = b_ref[:, half_of(1 - core, step, half, size)]
    dy = got_ref[:, :BLK].reshape(CAP * BLK, width)
    d_own = (product(dy, own_ref[...]) * so_ref[...].astype(F32)).astype(BF16)
    d_other = (product(dy, other_ref[...]) * st_ref[...].astype(F32)).astype(BF16)
    do_ref[...] = d_own
    dt_ref[...] = d_other
    turned = rows_by_rows(b_own, d_own) + rows_by_rows(b_other, d_other)
    straight = rows_by_rows(d_own, b_own) + rows_by_rows(d_other, b_other)

    @pl.when(step == 0)
    def _():
        turned_scr[...] = turned
        straight_scr[...] = straight

    @pl.when(step > 0)
    def _():
        turned_scr[...] += turned
        straight_scr[...] += straight

    @pl.when(step == pl.num_programs(0) - 1)
    def _():
        rank = turned_scr.shape[0]
        dlow_ref[...] = straight_scr[...].astype(BF16)
        first, live = own_slot(ints_ref)
        base = x_ref[...].astype(F32) - t_ref[...].astype(F32)
        miss_ref = base + pick(first, mod_ref, 2) * jnp.sum(got_ref[:, BLK:].astype(F32), axis=0)
        miss_ref = jnp.where(lax.broadcasted_iota(jnp.int32, miss_ref.shape, 0) < live, miss_ref, 0.0)
        miss_pol = 0.5 * unit_ref[...]
        parts = jnp.sum((miss_pol - miss_ref) * (miss_pol + miss_ref), axis=1, keepdims=True)
        excess = jnp.broadcast_to(jnp.sum(parts, axis=0, keepdims=True), (NOTE, CAP * BLK))
        high = excess.astype(BF16)
        rest = excess - high.astype(F32)
        middle = rest.astype(BF16)
        lowest = rest - middle.astype(F32)
        line = lax.broadcasted_iota(jnp.int32, excess.shape, 0)
        note = jnp.where(line == 0, high.astype(F32), jnp.where(line == 1, middle.astype(F32), lowest)).astype(BF16)
        total = turned_scr[...].astype(BF16)
        for peer in range(send_ref.shape[0]):
            send_ref[peer, :rank] = total
            send_ref[peer, rank:] = note


def backward(ints, got, unit, x_own, t_own, mod, own, other, factor, s_own, s_other):
    groups, _, width = got.shape
    half = s_own.shape[1]
    rank = factor.shape[0]
    rows = CAP * BLK
    step = 256
    weight = pl.BlockSpec((width, step), lambda i: (0, half // step + i))
    cut = pl.BlockSpec((rows, step), lambda i: (0, i))
    block = whole((BLK, width))
    return pl.pallas_call(
        back_kernel,
        grid=(half // step,),
        out_shape=[
            jax.ShapeDtypeStruct((rows, half), BF16),
            jax.ShapeDtypeStruct((rows, half), BF16),
            jax.ShapeDtypeStruct((rows, rank), BF16),
            jax.ShapeDtypeStruct((groups, rank + NOTE, rows), BF16),
        ],
        in_specs=[
            pl.BlockSpec(memory_space=SMEM), whole(got.shape), block, block, block, whole(mod.shape),
            weight, weight, whole(factor.shape), cut, cut,
        ],
        out_specs=[cut, cut, whole((rows, rank)), whole((groups, rank + NOTE, rows))],
        scratch_shapes=[pltpu.VMEM((rank, rows), F32), pltpu.VMEM((rows, rank), F32)],
        compiler_params=params(),
        cost_estimate=cost(4 * rows * width * half, 4 * width * half + 12 * rows * half),
    )(ints, got, unit, x_own, t_own, mod, own, other, factor, s_own, s_other)


def factor_kernel(split_ref, do_ref, dt_ref, own_ref, other_ref):
    own_ref[...] = product(split_ref[...], do_ref[...])
    other_ref[...] = product(split_ref[...], dt_ref[...])


def factor_terms(split, d_own, d_other):
    lines, rows = split.shape
    half = d_own.shape[1]
    return pl.pallas_call(
        factor_kernel,
        out_shape=[jax.ShapeDtypeStruct((lines, half), F32)] * 2,
        compiler_params=params(),
        cost_estimate=cost(4 * lines * rows * half, 8 * lines * half),
    )(split, d_own, d_other)


def pile_kernel(
    ints_ref, got_ref, modded_ref, own_ref, other_ref, keep_ref, give_ref, facts_ref
):
    wins = ints_ref[0]
    core = ints_ref[5]
    groups, lines, rows = got_ref.shape
    rank = lines - NOTE
    half = own_ref.shape[1]
    gap_first = jnp.zeros((1, rows), F32)
    gap_second = jnp.zeros((1, rows), F32)
    for slot in range(groups):
        note = got_ref[slot, rank:].astype(F32)
        excess = note[0:1] + note[1:2] + note[2:3]
        gap_first += jnp.where(slot < wins, excess, 0.0)
        gap_second += jnp.where(slot < wins, 0.0, excess)
    width = modded_ref.shape[1]
    rows_first = (wins - 1) * BLK + ints_ref[2]
    rows_second = (ints_ref[1] - wins - 1) * BLK + ints_ref[3]
    scale_first = 1.0 / (width * jnp.full((1, rows), rows_first, jnp.int32).astype(F32))
    scale_second = 1.0 / (width * jnp.full((1, rows), rows_second, jnp.int32).astype(F32))
    inside = -BETA * (gap_first * scale_first - gap_second * scale_second)
    losses = jnp.maximum(-inside, 0.0) + jnp.log1p(jnp.exp(-jnp.abs(inside)))
    weight = BETA * LOSS_SCALE * jax.nn.sigmoid(-inside)
    first = weight * scale_first
    second = -weight * scale_second
    line = lax.broadcasted_iota(jnp.int32, facts_ref.shape, 0)
    facts_ref[...] = jnp.where(line == 0, losses, jnp.where(line == 1, first, second))
    slot = lax.broadcasted_iota(jnp.int32, (1, rows), 1) // BLK
    total = jnp.sum(got_ref[:, :rank].astype(F32), axis=0)
    dlow = (total * jnp.where(slot < wins, first, second)).astype(BF16)
    one = first[:, :1]
    two = second[:, :1]
    near = modded_ref[:, pl.ds(pl.multiple_of(core * half, 128), half)]
    far = modded_ref[:, pl.ds(pl.multiple_of((1 - core) * half, 128), half)]
    keep_ref[:rank] = one * own_ref[:rank] + two * own_ref[rank:]
    keep_ref[rank:] = product(dlow, near)
    give_ref[:rank] = (one * other_ref[:rank] + two * other_ref[rank:]).astype(BF16)
    give_ref[rank:] = product(dlow, far).astype(BF16)


def piles(ints, got, modded, b_own, b_other):
    lines, half = b_own.shape
    rows = got.shape[2]
    return pl.pallas_call(
        pile_kernel,
        out_shape=[
            jax.ShapeDtypeStruct((lines, half), F32),
            jax.ShapeDtypeStruct((lines, half), BF16),
            jax.ShapeDtypeStruct((8, rows), F32),
        ],
        in_specs=[pl.BlockSpec(memory_space=SMEM)] + [pl.BlockSpec(memory_space=pltpu.VMEM)] * 4,
        compiler_params=params(),
        cost_estimate=cost(2 * lines * half * rows, 16 * lines * half),
    )(ints, got, modded, b_own, b_other)


def dm_kernel(after_ref, do_ref, dt_ref, dlow_ref, own_ref, other_ref, a_ref, out_ref):
    total = rows_by_rows(do_ref[...], own_ref[...]) + rows_by_rows(dt_ref[...], other_ref[...])
    out_ref[...] = (total + product(dlow_ref[...], a_ref[...])).astype(BF16)


def dm_terms(after, d_own, d_other, dlow, own, other, a_turned):
    rows, half = d_own.shape
    width = own.shape[0]
    rank = dlow.shape[1]
    step = 512
    cut = pl.BlockSpec((step, half), lambda i: (i, 0))
    return pl.pallas_call(
        dm_kernel,
        grid=(width // step,),
        out_shape=jax.ShapeDtypeStruct((rows, width), BF16),
        in_specs=[
            pl.BlockSpec(memory_space=pl.ANY),
            whole((rows, half)),
            whole((rows, half)),
            whole((rows, rank)),
            cut,
            cut,
            pl.BlockSpec((rank, step), lambda i: (0, i)),
        ],
        out_specs=pl.BlockSpec((rows, step), lambda i: (0, i)),
        compiler_params=params(),
        cost_estimate=cost(4 * rows * width * half, 4 * width * half + 2 * rows * width),
    )(after, d_own, d_other, dlow, own, other, a_turned)


def token_kernel(ints_ref, one_ref, two_ref, three_ref, four_ref, x_ref, mod_ref, unit_ref, facts_ref, out_ref):
    total = one_ref[...].astype(F32) + two_ref[...].astype(F32)
    total = total + three_ref[...].astype(F32) + four_ref[...].astype(F32)
    normed, inverse = normalise(x_ref[...])
    first, _ = own_slot(ints_ref)
    coef = jnp.where(first, facts_ref[1:2, :1], facts_ref[2:3, :1])
    dn = total * (1.0 + pick(first, mod_ref, 1))
    mean_one = jnp.mean(dn, axis=-1, keepdims=True)
    mean_two = jnp.mean(dn * normed, axis=-1, keepdims=True)
    grad = coef * (unit_ref[...] + inverse * (dn - mean_one - normed * mean_two))
    out_ref[...] = grad.astype(BF16)


def token_gradient(ints, pieces, x_own, mod, unit, facts):
    rows, width = x_own.shape
    return pl.pallas_call(
        token_kernel,
        out_shape=jax.ShapeDtypeStruct((rows, width), BF16),
        in_specs=[pl.BlockSpec(memory_space=SMEM)] + [pl.BlockSpec(memory_space=pltpu.VMEM)] * 8,
        compiler_params=params(),
        cost_estimate=cost(20 * rows * width, 20 * rows * width),
    )(ints, *pieces, x_own, mod, unit, facts)


def per_device(
    tokens,
    targets,
    modulation,
    live_block_count,
    preferred_blocks,
    last_block_rows,
    up_rows,
    down_rows,
    factor_in,
    factor_out,
):
    width = tokens.shape[1]
    n_z, n_x, n_c, n_t = (lax.axis_size(a) for a in ("z", "x", "c", "t"))
    n_dp = n_z * n_x * n_c
    core = lax.axis_index("c")
    group = lax.axis_index("t")
    thin, hidden = up_rows.shape
    half = hidden // n_c
    rank = factor_in.shape[1]

    sent = jnp.stack([up_rows.reshape(thin, n_c, half), down_rows.reshape(thin, n_c, half)], axis=2)
    sent = sent.reshape(thin, n_c, 2 * half).transpose(1, 0, 2)
    sent = jnp.broadcast_to(sent[None], (n_x, n_c, thin, 2 * half)).reshape(n_x * n_c, thin, 2 * half)
    near = lax.all_to_all(sent, ("x", "c"), 0, 0, tiled=True).reshape(n_x * n_c * thin, 2 * half)

    ints = [preferred_blocks[0], live_block_count[0], last_block_rows[0, 0], last_block_rows[0, 1], group, core]
    ints = jnp.stack(ints).astype(jnp.int32)
    x_own = lax.dynamic_slice_in_dim(tokens, group * BLK, BLK, axis=0)
    t_own = lax.dynamic_slice_in_dim(targets, group * BLK, BLK, axis=0)
    mod = modulation.reshape(6, width)
    a_turned = factor_in.T
    modded, low, low_split = prepare(ints, tokens, mod, a_turned)

    near = after(near, [modded, low, low_split, x_own, t_own])
    own = around(near, n_z).reshape(width, 2 * half)
    other = lax.ppermute(own, "c", SWAP)

    pol_own, ref_own, slope_own = activate(False, ints, modded, low, own, factor_out)
    pol_other, ref_other, slope_other = activate(True, ints, modded, low, other, factor_out)
    part_pol = lower(pol_own, pol_other, own, other).reshape(CAP, BLK, width)
    got_pol = lax.all_to_all(part_pol, "t", 0, 0, tiled=True)
    part_ref = lower(ref_own, ref_other, own, other).reshape(CAP, BLK, width)

    unit, send = miss(ints, got_pol, part_ref, x_own, t_own, mod)
    got_dy = lax.all_to_all(send, "t", 0, 0, tiled=True)
    d_own, d_other, dlow_part, send = backward(
        ints, got_dy, unit, x_own, t_own, mod, own, other, factor_out, slope_own, slope_other
    )
    got_low = lax.all_to_all(send, "t", 0, 0, tiled=True)
    b_own, b_other = factor_terms(low_split, d_own, d_other)
    keep, give, facts = piles(ints, got_low, modded, b_own, b_other)
    losses = facts[0, :1]
    pile = (keep + lax.ppermute(give, "c", SWAP).astype(F32)).astype(BF16)

    chips = n_z * n_x
    pieces = lax.all_to_all(pile.reshape(chips, 2 * rank // chips, half), CHIPS, 0, 0, tiled=True)
    dm_part = dm_terms(pile, d_own, d_other, dlow_part, own, other, a_turned).reshape(CAP, BLK, width)
    turns = [[(i, (i + step) % n_t) for i in range(n_t)] for step in range(n_t)]
    chunks = [lax.dynamic_index_in_dim(dm_part, (group + step) % n_t, 0, False) for step in range(n_t)]
    chunks = [chunks[0]] + [lax.ppermute(chunks[step], "t", turns[step]) for step in range(1, n_t)]
    total = (jnp.sum(pieces.astype(F32), axis=0) / n_dp).astype(BF16)
    total = after(total, chunks[1:])
    mine = spread(total, CHIPS, chips).reshape(2 * rank, half)
    theirs = lax.ppermute(mine, "c", SWAP)
    ends = jnp.concatenate([mine, theirs], 1)
    flipped = jnp.concatenate([theirs, mine], 1)
    ends = jnp.where(core == 0, ends, flipped).astype(F32)
    sum_b = ends[:rank]
    sum_a = ends[rank:].T

    grad_block = token_gradient(ints, chunks, x_own, mod, unit, facts)
    grad_tokens = lax.all_gather(grad_block, "t", axis=0, tiled=True)
    return losses, grad_tokens, sum_a, sum_b


def solution(mesh):
    n_dp, n_t = mesh.devices.shape
    fine = Mesh(mesh.devices.reshape(n_dp // 8, 4, 2, n_t), ("z", "x", "c", "t"))
    return jax.shard_map(
        per_device,
        mesh=fine,
        in_specs=(
            P(DP, None),
            P(DP, None),
            P(DP, None, None),
            P(DP),
            P(DP),
            P(DP, None),
            P(DP, "t"),
            P(DP, "t"),
            P(),
            P(None, "t"),
        ),
        out_specs=(P(DP), P(DP, None), P(), P(None, "t")),
        check_vma=False,
    )
```

```python
import functools

import jax
import jax.numpy as jnp
from jax import lax
from jax.experimental import pallas as pl
from jax.experimental.pallas import tpu as pltpu
from jax.sharding import Mesh
from jax.sharding import PartitionSpec as P

BLK = 64
CAP = 4
EPS = 1e-06
BETA = 20.0
LOSS_SCALE = 4096.0
ROOT = 0.7978845608028654
CUBE = 0.044715
BF16 = jnp.bfloat16
F32 = jnp.float32
DP = ("z", "x", "c")
CHIPS = ("z", "x")
SWAP = [(0, 1), (1, 0)]
NOTE = 16
VMEM_LIMIT = 40 * 1024 * 1024
SMEM = pltpu.SMEM


def gelu(pre):
    th = jnp.tanh(ROOT * (pre + CUBE * pre * pre * pre))
    return 0.5 * pre * (1.0 + th)


def gelu_and_slope(pre):
    square = pre * pre
    th = jnp.tanh(ROOT * (pre + CUBE * pre * square))
    half = 0.5 * (1.0 + th)
    slope = half + 0.5 * pre * (1.0 - th * th) * (ROOT * (1.0 + 3.0 * CUBE * square))
    return pre * half, slope


def rows_by_rows(left, right):
    return lax.dot_general(left, right, (((1,), (1,)), ((), ())), preferred_element_type=F32)


def product(left, right):
    return jnp.dot(left, right, preferred_element_type=F32)


def spread(value, axes, n):
    return lax.all_to_all(jnp.broadcast_to(value[None], (n, *value.shape)), axes, 0, 0, tiled=True)


def around(block, n):
    here = lax.axis_index("z")
    up = [(i, (i + 1) % n) for i in range(n)]
    down = [(i, (i - 1) % n) for i in range(n)]
    found = lax.dynamic_update_index_in_dim(jnp.zeros((n, *block.shape), block.dtype), block, here, 0)
    left = right = block
    for step in range(1, n // 2 + 1):
        left = lax.ppermute(left, "z", up)
        found = lax.dynamic_update_index_in_dim(found, left, (here - step) % n, 0)
        if step < n // 2:
            right = lax.ppermute(right, "z", down)
            found = lax.dynamic_update_index_in_dim(found, right, (here + step) % n, 0)
    return found


def normalise(rows):
    wide = rows.astype(F32)
    center = wide - jnp.mean(wide, axis=-1, keepdims=True)
    inverse = lax.rsqrt(jnp.mean(center * center, axis=-1, keepdims=True) + EPS)
    return center * inverse, inverse


def params():
    return pltpu.CompilerParams(vmem_limit_bytes=VMEM_LIMIT)


def cost(flops, moved, tanh=0):
    return pl.CostEstimate(flops=flops, bytes_accessed=moved, transcendentals=tanh)


def whole(shape):
    return pl.BlockSpec(shape, lambda *_: (0,) * len(shape))


def input_kernel(wins_ref, x_ref, mod_ref, a_ref, modded_ref, low_ref, split_ref):
    wins = wins_ref[0]
    for slot in range(CAP):
        rows = slice(slot * BLK, (slot + 1) * BLK)
        normed, _ = normalise(x_ref[rows])
        first = slot < wins
        shift = jnp.where(first, mod_ref[0:1].astype(F32), mod_ref[3:4].astype(F32))
        scale = 1.0 + jnp.where(first, mod_ref[1:2].astype(F32), mod_ref[4:5].astype(F32))
        modded_ref[rows] = (normed * scale + shift).astype(BF16)
    modded = modded_ref[...]
    low_ref[...] = rows_by_rows(modded, a_ref[...]).astype(BF16)
    turned = rows_by_rows(a_ref[...], modded)
    second = lax.broadcasted_iota(jnp.int32, turned.shape, 1) // BLK >= wins
    rank = turned.shape[0]
    split_ref[:rank] = jnp.where(second, 0.0, turned).astype(BF16)
    split_ref[rank:] = jnp.where(second, turned, 0.0).astype(BF16)


def prepare(wins, tokens, mod, a_turned):
    rows, width = tokens.shape
    rank = a_turned.shape[0]
    return pl.pallas_call(
        input_kernel,
        out_shape=[
            jax.ShapeDtypeStruct((rows, width), BF16),
            jax.ShapeDtypeStruct((rows, rank), BF16),
            jax.ShapeDtypeStruct((2 * rank, rows), BF16),
        ],
        in_specs=[pl.BlockSpec(memory_space=SMEM)] + [pl.BlockSpec(memory_space=pltpu.VMEM)] * 3,
        compiler_params=params(),
        cost_estimate=cost(4 * rows * width * rank, 4 * rows * width),
    )(wins, tokens, mod, a_turned)


def own_slot(ints_ref):
    wins, count, slot = ints_ref[0], ints_ref[1], ints_ref[4]
    first = slot < wins
    last = jnp.where(first, wins - 1, count - 1)
    tail = jnp.where(first, ints_ref[2], ints_ref[3])
    return first, jnp.where(slot < count, jnp.where(slot == last, tail, BLK), 0)


def pick(first, ref, line):
    return jnp.where(first, ref[line : line + 1].astype(F32), ref[line + 3 : line + 4].astype(F32))


def after_kernel(*refs):
    del refs


def after(value, others):
    return pl.pallas_call(
        after_kernel,
        out_shape=jax.ShapeDtypeStruct(value.shape, value.dtype),
        in_specs=[pl.BlockSpec(memory_space=pl.ANY)] * (1 + len(others)),
        out_specs=pl.BlockSpec(memory_space=pl.ANY),
        input_output_aliases={0: 0},
    )(value, *others)


def half_of(core, step, half, size):
    return pl.ds(pl.multiple_of(core * half + step * size, 128), size)


def up_kernel(far, ints_ref, modded_ref, low_ref, up_ref, b_ref, pol_ref, ref_ref, slope_ref):
    core = 1 - ints_ref[5] if far else ints_ref[5]
    size = up_ref.shape[1]
    cut = half_of(core, pl.program_id(0), size * pl.num_programs(0), size)
    pre_ref = product(modded_ref[...], up_ref[...])
    pre_pol = pre_ref + product(low_ref[...], b_ref[:, cut])
    act, slope = gelu_and_slope(pre_pol)
    pol_ref[...] = act.astype(BF16)
    slope_ref[...] = slope.astype(BF16)
    ref_ref[...] = gelu(pre_ref).astype(BF16)


def activate(far, ints, modded, low, weights, factor):
    rows, width = modded.shape
    rank = factor.shape[0]
    half = factor.shape[1] // 2
    step = 256
    cut = pl.BlockSpec((rows, step), lambda i: (0, i))
    return pl.pallas_call(
        functools.partial(up_kernel, far),
        grid=(half // step,),
        out_shape=[
            jax.ShapeDtypeStruct((rows, half), BF16),
            jax.ShapeDtypeStruct((rows, half), BF16),
            jax.ShapeDtypeStruct((rows, half), BF16),
        ],
        in_specs=[
            pl.BlockSpec(memory_space=SMEM),
            whole((rows, width)),
            whole((rows, rank)),
            pl.BlockSpec((width, step), lambda i: (0, i)),
            whole(factor.shape),
        ],
        out_specs=[cut, cut, cut],
        compiler_params=params(),
        cost_estimate=cost(2 * rows * width * half, 2 * width * half + 10 * rows * half, 2 * rows * half),
    )(ints, modded, low, weights, factor)


def down_kernel(left_ref, right_ref, own_ref, other_ref, out_ref):
    total = rows_by_rows(left_ref[...], own_ref[...]) + rows_by_rows(right_ref[...], other_ref[...])
    out_ref[...] = total.astype(BF16)


def lower(left, right, own, other):
    rows, half = left.shape
    width = own.shape[0]
    step = 512
    cut = pl.BlockSpec((step, half), lambda i: (i, 0))
    return pl.pallas_call(
        down_kernel,
        grid=(width // step,),
        out_shape=jax.ShapeDtypeStruct((rows, width), BF16),
        in_specs=[whole((rows, half)), whole((rows, half)), cut, cut],
        out_specs=pl.BlockSpec((rows, step), lambda i: (0, i)),
        compiler_params=params(),
        cost_estimate=cost(4 * rows * width * half, 4 * width * half + 2 * rows * width),
    )(left, right, own, other)


def miss_kernel(ints_ref, got_ref, ref_ref, x_ref, t_ref, mod_ref, unit_ref, send_ref):
    first, live = own_slot(ints_ref)
    total = jnp.sum(got_ref[...].astype(F32), axis=0)
    gate = pick(first, mod_ref, 2)
    unit = 2.0 * (x_ref[...].astype(F32) - t_ref[...].astype(F32) + gate * total)
    unit = jnp.where(lax.broadcasted_iota(jnp.int32, unit.shape, 0) < live, unit, 0.0)
    unit_ref[...] = unit
    dy = (gate * unit).astype(BF16)
    for peer in range(send_ref.shape[0]):
        send_ref[peer, :BLK] = dy
        send_ref[peer, BLK:] = ref_ref[peer]


def miss(ints, got, part_ref, x_own, t_own, mod):
    groups, rows, width = got.shape
    return pl.pallas_call(
        miss_kernel,
        out_shape=[
            jax.ShapeDtypeStruct((rows, width), F32),
            jax.ShapeDtypeStruct((groups, 2 * rows, width), BF16),
        ],
        in_specs=[pl.BlockSpec(memory_space=SMEM)] + [pl.BlockSpec(memory_space=pltpu.VMEM)] * 5,
        compiler_params=params(),
        cost_estimate=cost(20 * rows * width, 8 * groups * rows * width),
    )(ints, got, part_ref, x_own, t_own, mod)


def back_kernel(
    ints_ref, got_ref, unit_ref, x_ref, t_ref, mod_ref, own_ref, other_ref, b_ref, so_ref, st_ref,
    do_ref, dt_ref, dlow_ref, send_ref, turned_scr, straight_scr,
):
    step = pl.program_id(0)
    core = ints_ref[5]
    width = got_ref.shape[2]
    size = so_ref.shape[1]
    half = size * pl.num_programs(0)
    b_own = b_ref[:, half_of(core, step, half, size)]
    b_other = b_ref[:, half_of(1 - core, step, half, size)]
    dy = got_ref[:, :BLK].reshape(CAP * BLK, width)
    d_own = (product(dy, own_ref[...]) * so_ref[...].astype(F32)).astype(BF16)
    d_other = (product(dy, other_ref[...]) * st_ref[...].astype(F32)).astype(BF16)
    do_ref[...] = d_own
    dt_ref[...] = d_other
    turned = rows_by_rows(b_own, d_own) + rows_by_rows(b_other, d_other)
    straight = rows_by_rows(d_own, b_own) + rows_by_rows(d_other, b_other)

    @pl.when(step == 0)
    def _():
        turned_scr[...] = turned
        straight_scr[...] = straight

    @pl.when(step > 0)
    def _():
        turned_scr[...] += turned
        straight_scr[...] += straight

    @pl.when(step == pl.num_programs(0) - 1)
    def _():
        rank = turned_scr.shape[0]
        dlow_ref[...] = straight_scr[...].astype(BF16)
        first, live = own_slot(ints_ref)
        base = x_ref[...].astype(F32) - t_ref[...].astype(F32)
        miss_ref = base + pick(first, mod_ref, 2) * jnp.sum(got_ref[:, BLK:].astype(F32), axis=0)
        miss_ref = jnp.where(lax.broadcasted_iota(jnp.int32, miss_ref.shape, 0) < live, miss_ref, 0.0)
        miss_pol = 0.5 * unit_ref[...]
        parts = jnp.sum((miss_pol - miss_ref) * (miss_pol + miss_ref), axis=1, keepdims=True)
        excess = jnp.broadcast_to(jnp.sum(parts, axis=0, keepdims=True), (NOTE, CAP * BLK))
        high = excess.astype(BF16)
        rest = excess - high.astype(F32)
        middle = rest.astype(BF16)
        lowest = rest - middle.astype(F32)
        line = lax.broadcasted_iota(jnp.int32, excess.shape, 0)
        note = jnp.where(line == 0, high.astype(F32), jnp.where(line == 1, middle.astype(F32), lowest)).astype(BF16)
        total = turned_scr[...].astype(BF16)
        for peer in range(send_ref.shape[0]):
            send_ref[peer, :rank] = total
            send_ref[peer, rank:] = note


def backward(ints, got, unit, x_own, t_own, mod, own, other, factor, s_own, s_other):
    groups, _, width = got.shape
    half = s_own.shape[1]
    rank = factor.shape[0]
    rows = CAP * BLK
    step = 256
    weight = pl.BlockSpec((width, step), lambda i: (0, i))
    cut = pl.BlockSpec((rows, step), lambda i: (0, i))
    block = whole((BLK, width))
    return pl.pallas_call(
        back_kernel,
        grid=(half // step,),
        out_shape=[
            jax.ShapeDtypeStruct((rows, half), BF16),
            jax.ShapeDtypeStruct((rows, half), BF16),
            jax.ShapeDtypeStruct((rows, rank), BF16),
            jax.ShapeDtypeStruct((groups, rank + NOTE, rows), BF16),
        ],
        in_specs=[
            pl.BlockSpec(memory_space=SMEM), whole(got.shape), block, block, block, whole(mod.shape),
            weight, weight, whole(factor.shape), cut, cut,
        ],
        out_specs=[cut, cut, whole((rows, rank)), whole((groups, rank + NOTE, rows))],
        scratch_shapes=[pltpu.VMEM((rank, rows), F32), pltpu.VMEM((rows, rank), F32)],
        compiler_params=params(),
        cost_estimate=cost(4 * rows * width * half, 4 * width * half + 12 * rows * half),
    )(ints, got, unit, x_own, t_own, mod, own, other, factor, s_own, s_other)


def factor_kernel(split_ref, do_ref, dt_ref, own_ref, other_ref):
    own_ref[...] = product(split_ref[...], do_ref[...])
    other_ref[...] = product(split_ref[...], dt_ref[...])


def factor_terms(split, d_own, d_other):
    lines, rows = split.shape
    half = d_own.shape[1]
    return pl.pallas_call(
        factor_kernel,
        out_shape=[jax.ShapeDtypeStruct((lines, half), F32)] * 2,
        compiler_params=params(),
        cost_estimate=cost(4 * lines * rows * half, 8 * lines * half),
    )(split, d_own, d_other)


def pile_kernel(
    ints_ref, got_ref, modded_ref, own_ref, other_ref, keep_ref, give_ref, facts_ref
):
    wins = ints_ref[0]
    core = ints_ref[5]
    groups, lines, rows = got_ref.shape
    rank = lines - NOTE
    half = own_ref.shape[1]
    gap_first = jnp.zeros((1, rows), F32)
    gap_second = jnp.zeros((1, rows), F32)
    for slot in range(groups):
        note = got_ref[slot, rank:].astype(F32)
        excess = note[0:1] + note[1:2] + note[2:3]
        gap_first += jnp.where(slot < wins, excess, 0.0)
        gap_second += jnp.where(slot < wins, 0.0, excess)
    width = modded_ref.shape[1]
    rows_first = (wins - 1) * BLK + ints_ref[2]
    rows_second = (ints_ref[1] - wins - 1) * BLK + ints_ref[3]
    scale_first = 1.0 / (width * jnp.full((1, rows), rows_first, jnp.int32).astype(F32))
    scale_second = 1.0 / (width * jnp.full((1, rows), rows_second, jnp.int32).astype(F32))
    inside = -BETA * (gap_first * scale_first - gap_second * scale_second)
    losses = jnp.maximum(-inside, 0.0) + jnp.log1p(jnp.exp(-jnp.abs(inside)))
    weight = BETA * LOSS_SCALE * jax.nn.sigmoid(-inside)
    first = weight * scale_first
    second = -weight * scale_second
    line = lax.broadcasted_iota(jnp.int32, facts_ref.shape, 0)
    facts_ref[...] = jnp.where(line == 0, losses, jnp.where(line == 1, first, second))
    slot = lax.broadcasted_iota(jnp.int32, (1, rows), 1) // BLK
    total = jnp.sum(got_ref[:, :rank].astype(F32), axis=0)
    dlow = (total * jnp.where(slot < wins, first, second)).astype(BF16)
    one = first[:, :1]
    two = second[:, :1]
    near = modded_ref[:, pl.ds(pl.multiple_of(core * half, 128), half)]
    far = modded_ref[:, pl.ds(pl.multiple_of((1 - core) * half, 128), half)]
    keep_ref[:rank] = one * own_ref[:rank] + two * own_ref[rank:]
    keep_ref[rank:] = product(dlow, near)
    give_ref[:rank] = (one * other_ref[:rank] + two * other_ref[rank:]).astype(BF16)
    give_ref[rank:] = product(dlow, far).astype(BF16)


def piles(ints, got, modded, b_own, b_other):
    lines, half = b_own.shape
    rows = got.shape[2]
    return pl.pallas_call(
        pile_kernel,
        out_shape=[
            jax.ShapeDtypeStruct((lines, half), F32),
            jax.ShapeDtypeStruct((lines, half), BF16),
            jax.ShapeDtypeStruct((8, rows), F32),
        ],
        in_specs=[pl.BlockSpec(memory_space=SMEM)] + [pl.BlockSpec(memory_space=pltpu.VMEM)] * 4,
        compiler_params=params(),
        cost_estimate=cost(2 * lines * half * rows, 16 * lines * half),
    )(ints, got, modded, b_own, b_other)


def dm_kernel(after_ref, do_ref, dt_ref, dlow_ref, own_ref, other_ref, a_ref, out_ref):
    total = rows_by_rows(do_ref[...], own_ref[...]) + rows_by_rows(dt_ref[...], other_ref[...])
    out_ref[...] = (total + product(dlow_ref[...], a_ref[...])).astype(BF16)


def dm_terms(after, d_own, d_other, dlow, own, other, a_turned):
    rows, half = d_own.shape
    width = own.shape[0]
    rank = dlow.shape[1]
    step = 512
    cut = pl.BlockSpec((step, half), lambda i: (i, 0))
    return pl.pallas_call(
        dm_kernel,
        grid=(width // step,),
        out_shape=jax.ShapeDtypeStruct((rows, width), BF16),
        in_specs=[
            pl.BlockSpec(memory_space=pl.ANY),
            whole((rows, half)),
            whole((rows, half)),
            whole((rows, rank)),
            cut,
            cut,
            pl.BlockSpec((rank, step), lambda i: (0, i)),
        ],
        out_specs=pl.BlockSpec((rows, step), lambda i: (0, i)),
        compiler_params=params(),
        cost_estimate=cost(4 * rows * width * half, 4 * width * half + 2 * rows * width),
    )(after, d_own, d_other, dlow, own, other, a_turned)


def token_kernel(ints_ref, one_ref, two_ref, three_ref, four_ref, x_ref, mod_ref, unit_ref, facts_ref, out_ref):
    total = one_ref[...].astype(F32) + two_ref[...].astype(F32)
    total = total + three_ref[...].astype(F32) + four_ref[...].astype(F32)
    normed, inverse = normalise(x_ref[...])
    first, _ = own_slot(ints_ref)
    coef = jnp.where(first, facts_ref[1:2, :1], facts_ref[2:3, :1])
    dn = total * (1.0 + pick(first, mod_ref, 1))
    mean_one = jnp.mean(dn, axis=-1, keepdims=True)
    mean_two = jnp.mean(dn * normed, axis=-1, keepdims=True)
    grad = coef * (unit_ref[...] + inverse * (dn - mean_one - normed * mean_two))
    out_ref[...] = grad.astype(BF16)


def token_gradient(ints, pieces, x_own, mod, unit, facts):
    rows, width = x_own.shape
    return pl.pallas_call(
        token_kernel,
        out_shape=jax.ShapeDtypeStruct((rows, width), BF16),
        in_specs=[pl.BlockSpec(memory_space=SMEM)] + [pl.BlockSpec(memory_space=pltpu.VMEM)] * 8,
        compiler_params=params(),
        cost_estimate=cost(20 * rows * width, 20 * rows * width),
    )(ints, *pieces, x_own, mod, unit, facts)


def per_device(
    tokens,
    targets,
    modulation,
    live_block_count,
    preferred_blocks,
    last_block_rows,
    up_rows,
    down_rows,
    factor_in,
    factor_out,
):
    width = tokens.shape[1]
    n_z, n_x, n_c, n_t = (lax.axis_size(a) for a in ("z", "x", "c", "t"))
    n_dp = n_z * n_x * n_c
    core = lax.axis_index("c")
    group = lax.axis_index("t")
    thin, hidden = up_rows.shape
    half = hidden // n_c
    rank = factor_in.shape[1]

    sent = jnp.stack([up_rows.reshape(thin, n_c, half), down_rows.reshape(thin, n_c, half)], axis=2)
    sent = sent.reshape(thin, n_c, 2 * half).transpose(1, 0, 2)
    sent = jnp.broadcast_to(sent[None], (n_x, n_c, thin, 2 * half)).reshape(n_x * n_c, thin, 2 * half)
    near = lax.all_to_all(sent, ("x", "c"), 0, 0, tiled=True)
    near_up = near[:, :, :half].reshape(n_x * n_c * thin, half)
    near_down = near[:, :, half:].reshape(n_x * n_c * thin, half)
    down_own = lax.all_gather(near_down, "z", axis=0, tiled=True)

    ints = [preferred_blocks[0], live_block_count[0], last_block_rows[0, 0], last_block_rows[0, 1], group, core]
    ints = jnp.stack(ints).astype(jnp.int32)
    x_own = lax.dynamic_slice_in_dim(tokens, group * BLK, BLK, axis=0)
    t_own = lax.dynamic_slice_in_dim(targets, group * BLK, BLK, axis=0)
    mod = modulation.reshape(6, width)
    a_turned = factor_in.T
    modded, low, low_split = prepare(ints, tokens, mod, a_turned)

    near_up = after(near_up, [modded, low, low_split, x_own, t_own])
    up_own = around(near_up, n_z).reshape(width, half)
    up_other = lax.ppermute(up_own, "c", SWAP)
    down_other = lax.ppermute(down_own, "c", SWAP)

    pol_own, ref_own, slope_own = activate(False, ints, modded, low, up_own, factor_out)
    pol_other, ref_other, slope_other = activate(True, ints, modded, low, up_other, factor_out)
    part_pol = lower(pol_own, pol_other, down_own, down_other).reshape(CAP, BLK, width)
    got_pol = lax.all_to_all(part_pol, "t", 0, 0, tiled=True)
    part_ref = lower(ref_own, ref_other, down_own, down_other).reshape(CAP, BLK, width)

    unit, send = miss(ints, got_pol, part_ref, x_own, t_own, mod)
    got_dy = lax.all_to_all(send, "t", 0, 0, tiled=True)
    d_own, d_other, dlow_part, send = backward(
        ints, got_dy, unit, x_own, t_own, mod, down_own, down_other, factor_out, slope_own, slope_other
    )
    got_low = lax.all_to_all(send, "t", 0, 0, tiled=True)
    b_own, b_other = factor_terms(low_split, d_own, d_other)
    keep, give, facts = piles(ints, got_low, modded, b_own, b_other)
    losses = facts[0, :1]
    pile = (keep + lax.ppermute(give, "c", SWAP).astype(F32)).astype(BF16)

    chips = n_z * n_x
    pieces = lax.all_to_all(pile.reshape(chips, 2 * rank // chips, half), CHIPS, 0, 0, tiled=True)
    dm_part = dm_terms(pile, d_own, d_other, dlow_part, up_own, up_other, a_turned).reshape(CAP, BLK, width)
    turns = [[(i, (i + step) % n_t) for i in range(n_t)] for step in range(n_t)]
    chunks = [lax.dynamic_index_in_dim(dm_part, (group + step) % n_t, 0, False) for step in range(n_t)]
    chunks = [chunks[0]] + [lax.ppermute(chunks[step], "t", turns[step]) for step in range(1, n_t)]
    total = (jnp.sum(pieces.astype(F32), axis=0) / n_dp).astype(BF16)
    total = after(total, chunks[1:])
    mine = spread(total, CHIPS, chips).reshape(2 * rank, half)
    grad_block = token_gradient(ints, chunks, x_own, mod, unit, facts)
    grad_tokens = lax.all_gather(grad_block, "t", axis=0, tiled=True)
    mine = after(mine, [grad_tokens])
    theirs = lax.ppermute(mine, "c", SWAP)
    ends = jnp.concatenate([mine, theirs], 1)
    flipped = jnp.concatenate([theirs, mine], 1)
    ends = jnp.where(core == 0, ends, flipped).astype(F32)
    sum_b = ends[:rank]
    sum_a = ends[rank:].T
    return losses, grad_tokens, sum_a, sum_b


def solution(mesh):
    n_dp, n_t = mesh.devices.shape
    fine = Mesh(mesh.devices.reshape(n_dp // 8, 4, 2, n_t), ("z", "x", "c", "t"))
    return jax.shard_map(
        per_device,
        mesh=fine,
        in_specs=(
            P(DP, None),
            P(DP, None),
            P(DP, None, None),
            P(DP),
            P(DP),
            P(DP, None),
            P(DP, "t"),
            P(DP, "t"),
            P(),
            P(None, "t"),
        ),
        out_specs=(P(DP), P(DP, None), P(), P(None, "t")),
        check_vma=False,
    )
```

```python
import functools

import jax
import jax.numpy as jnp
from jax import lax
from jax.experimental import pallas as pl
from jax.experimental.pallas import tpu as pltpu
from jax.sharding import Mesh
from jax.sharding import PartitionSpec as P

BLK = 64
CAP = 4
EPS = 1e-06
BETA = 20.0
LOSS_SCALE = 4096.0
ROOT = 0.7978845608028654
CUBE = 0.044715
BF16 = jnp.bfloat16
F32 = jnp.float32
DP = ("z", "x", "c")
CHIPS = ("z", "x")
SWAP = [(0, 1), (1, 0)]
NOTE = 16
VMEM_LIMIT = 40 * 1024 * 1024
SMEM = pltpu.SMEM


def gelu(pre):
    th = jnp.tanh(ROOT * (pre + CUBE * pre * pre * pre))
    return 0.5 * pre * (1.0 + th)


def gelu_and_slope(pre):
    square = pre * pre
    th = jnp.tanh(ROOT * (pre + CUBE * pre * square))
    half = 0.5 * (1.0 + th)
    slope = half + 0.5 * pre * (1.0 - th * th) * (ROOT * (1.0 + 3.0 * CUBE * square))
    return pre * half, slope


def rows_by_rows(left, right):
    return lax.dot_general(left, right, (((1,), (1,)), ((), ())), preferred_element_type=F32)


def product(left, right):
    return jnp.dot(left, right, preferred_element_type=F32)


def spread(value, axes, n):
    return lax.all_to_all(jnp.broadcast_to(value[None], (n, *value.shape)), axes, 0, 0, tiled=True)


def normalise(rows):
    wide = rows.astype(F32)
    center = wide - jnp.mean(wide, axis=-1, keepdims=True)
    inverse = lax.rsqrt(jnp.mean(center * center, axis=-1, keepdims=True) + EPS)
    return center * inverse, inverse


def params():
    return pltpu.CompilerParams(vmem_limit_bytes=VMEM_LIMIT)


def cost(flops, moved, tanh=0):
    return pl.CostEstimate(flops=flops, bytes_accessed=moved, transcendentals=tanh)


def whole(shape):
    return pl.BlockSpec(shape, lambda *_: (0,) * len(shape))


def input_kernel(wins_ref, x_ref, mod_ref, a_ref, modded_ref, low_ref, split_ref):
    wins = wins_ref[0]
    for slot in range(CAP):
        rows = slice(slot * BLK, (slot + 1) * BLK)
        normed, _ = normalise(x_ref[rows])
        first = slot < wins
        shift = jnp.where(first, mod_ref[0:1].astype(F32), mod_ref[3:4].astype(F32))
        scale = 1.0 + jnp.where(first, mod_ref[1:2].astype(F32), mod_ref[4:5].astype(F32))
        modded_ref[rows] = (normed * scale + shift).astype(BF16)
    modded = modded_ref[...]
    low_ref[...] = rows_by_rows(modded, a_ref[...]).astype(BF16)
    turned = rows_by_rows(a_ref[...], modded)
    second = lax.broadcasted_iota(jnp.int32, turned.shape, 1) // BLK >= wins
    rank = turned.shape[0]
    split_ref[:rank] = jnp.where(second, 0.0, turned).astype(BF16)
    split_ref[rank:] = jnp.where(second, turned, 0.0).astype(BF16)


def prepare(wins, tokens, mod, a_turned):
    rows, width = tokens.shape
    rank = a_turned.shape[0]
    return pl.pallas_call(
        input_kernel,
        out_shape=[
            jax.ShapeDtypeStruct((rows, width), BF16),
            jax.ShapeDtypeStruct((rows, rank), BF16),
            jax.ShapeDtypeStruct((2 * rank, rows), BF16),
        ],
        in_specs=[pl.BlockSpec(memory_space=SMEM)] + [pl.BlockSpec(memory_space=pltpu.VMEM)] * 3,
        compiler_params=params(),
        cost_estimate=cost(4 * rows * width * rank, 4 * rows * width),
    )(wins, tokens, mod, a_turned)


def own_slot(ints_ref):
    wins, count, slot = ints_ref[0], ints_ref[1], ints_ref[4]
    first = slot < wins
    last = jnp.where(first, wins - 1, count - 1)
    tail = jnp.where(first, ints_ref[2], ints_ref[3])
    return first, jnp.where(slot < count, jnp.where(slot == last, tail, BLK), 0)


def pick(first, ref, line):
    return jnp.where(first, ref[line : line + 1].astype(F32), ref[line + 3 : line + 4].astype(F32))


def after_kernel(*refs):
    del refs


def after(value, others):
    return pl.pallas_call(
        after_kernel,
        out_shape=jax.ShapeDtypeStruct(value.shape, value.dtype),
        in_specs=[pl.BlockSpec(memory_space=pl.ANY)] * (1 + len(others)),
        out_specs=pl.BlockSpec(memory_space=pl.ANY),
        input_output_aliases={0: 0},
    )(value, *others)


def half_of(core, step, half, size):
    return pl.ds(pl.multiple_of(core * half + step * size, 128), size)


def up_kernel(far, ints_ref, modded_ref, low_ref, up_ref, b_ref, pol_ref, ref_ref, slope_ref):
    core = 1 - ints_ref[5] if far else ints_ref[5]
    size = up_ref.shape[1]
    cut = half_of(core, pl.program_id(0), size * pl.num_programs(0), size)
    pre_ref = product(modded_ref[...], up_ref[...])
    pre_pol = pre_ref + product(low_ref[...], b_ref[:, cut])
    act, slope = gelu_and_slope(pre_pol)
    pol_ref[...] = act.astype(BF16)
    slope_ref[...] = slope.astype(BF16)
    ref_ref[...] = gelu(pre_ref).astype(BF16)


def activate(far, ints, modded, low, weights, factor):
    rows, width = modded.shape
    rank = factor.shape[0]
    half = factor.shape[1] // 2
    step = 256
    cut = pl.BlockSpec((rows, step), lambda i: (0, i))
    return pl.pallas_call(
        functools.partial(up_kernel, far),
        grid=(half // step,),
        out_shape=[
            jax.ShapeDtypeStruct((rows, half), BF16),
            jax.ShapeDtypeStruct((rows, half), BF16),
            jax.ShapeDtypeStruct((rows, half), BF16),
        ],
        in_specs=[
            pl.BlockSpec(memory_space=SMEM),
            whole((rows, width)),
            whole((rows, rank)),
            pl.BlockSpec((width, step), lambda i: (0, i)),
            whole(factor.shape),
        ],
        out_specs=[cut, cut, cut],
        compiler_params=params(),
        cost_estimate=cost(2 * rows * width * half, 2 * width * half + 10 * rows * half, 2 * rows * half),
    )(ints, modded, low, weights, factor)


def down_kernel(left_ref, right_ref, own_ref, other_ref, out_ref):
    total = rows_by_rows(left_ref[...], own_ref[...]) + rows_by_rows(right_ref[...], other_ref[...])
    out_ref[...] = total.astype(BF16)


def lower(left, right, own, other):
    rows, half = left.shape
    width = own.shape[0]
    step = 512
    cut = pl.BlockSpec((step, half), lambda i: (i, 1))
    return pl.pallas_call(
        down_kernel,
        grid=(width // step,),
        out_shape=jax.ShapeDtypeStruct((rows, width), BF16),
        in_specs=[whole((rows, half)), whole((rows, half)), cut, cut],
        out_specs=pl.BlockSpec((rows, step), lambda i: (0, i)),
        compiler_params=params(),
        cost_estimate=cost(4 * rows * width * half, 4 * width * half + 2 * rows * width),
    )(left, right, own, other)


def miss_kernel(ints_ref, got_ref, ref_ref, x_ref, t_ref, mod_ref, unit_ref, send_ref):
    first, live = own_slot(ints_ref)
    total = jnp.sum(got_ref[...].astype(F32), axis=0)
    gate = pick(first, mod_ref, 2)
    unit = 2.0 * (x_ref[...].astype(F32) - t_ref[...].astype(F32) + gate * total)
    unit = jnp.where(lax.broadcasted_iota(jnp.int32, unit.shape, 0) < live, unit, 0.0)
    unit_ref[...] = unit
    dy = (gate * unit).astype(BF16)
    for peer in range(send_ref.shape[0]):
        send_ref[peer, :BLK] = dy
        send_ref[peer, BLK:] = ref_ref[peer]


def miss(ints, got, part_ref, x_own, t_own, mod):
    groups, rows, width = got.shape
    return pl.pallas_call(
        miss_kernel,
        out_shape=[
            jax.ShapeDtypeStruct((rows, width), F32),
            jax.ShapeDtypeStruct((groups, 2 * rows, width), BF16),
        ],
        in_specs=[pl.BlockSpec(memory_space=SMEM)] + [pl.BlockSpec(memory_space=pltpu.VMEM)] * 5,
        compiler_params=params(),
        cost_estimate=cost(20 * rows * width, 8 * groups * rows * width),
    )(ints, got, part_ref, x_own, t_own, mod)


def back_kernel(
    ints_ref, got_ref, unit_ref, x_ref, t_ref, mod_ref, own_ref, other_ref, b_ref, so_ref, st_ref,
    do_ref, dt_ref, dlow_ref, send_ref, turned_scr, straight_scr,
):
    step = pl.program_id(0)
    core = ints_ref[5]
    width = got_ref.shape[2]
    size = so_ref.shape[1]
    half = size * pl.num_programs(0)
    b_own = b_ref[:, half_of(core, step, half, size)]
    b_other = b_ref[:, half_of(1 - core, step, half, size)]
    dy = got_ref[:, :BLK].reshape(CAP * BLK, width)
    d_own = (product(dy, own_ref[...]) * so_ref[...].astype(F32)).astype(BF16)
    d_other = (product(dy, other_ref[...]) * st_ref[...].astype(F32)).astype(BF16)
    do_ref[...] = d_own
    dt_ref[...] = d_other
    turned = rows_by_rows(b_own, d_own) + rows_by_rows(b_other, d_other)
    straight = rows_by_rows(d_own, b_own) + rows_by_rows(d_other, b_other)

    @pl.when(step == 0)
    def _():
        turned_scr[...] = turned
        straight_scr[...] = straight

    @pl.when(step > 0)
    def _():
        turned_scr[...] += turned
        straight_scr[...] += straight

    @pl.when(step == pl.num_programs(0) - 1)
    def _():
        rank = turned_scr.shape[0]
        dlow_ref[...] = straight_scr[...].astype(BF16)
        first, live = own_slot(ints_ref)
        base = x_ref[...].astype(F32) - t_ref[...].astype(F32)
        miss_ref = base + pick(first, mod_ref, 2) * jnp.sum(got_ref[:, BLK:].astype(F32), axis=0)
        miss_ref = jnp.where(lax.broadcasted_iota(jnp.int32, miss_ref.shape, 0) < live, miss_ref, 0.0)
        miss_pol = 0.5 * unit_ref[...]
        parts = jnp.sum((miss_pol - miss_ref) * (miss_pol + miss_ref), axis=1, keepdims=True)
        excess = jnp.broadcast_to(jnp.sum(parts, axis=0, keepdims=True), (NOTE, CAP * BLK))
        high = excess.astype(BF16)
        rest = excess - high.astype(F32)
        middle = rest.astype(BF16)
        lowest = rest - middle.astype(F32)
        line = lax.broadcasted_iota(jnp.int32, excess.shape, 0)
        note = jnp.where(line == 0, high.astype(F32), jnp.where(line == 1, middle.astype(F32), lowest)).astype(BF16)
        total = turned_scr[...].astype(BF16)
        for peer in range(send_ref.shape[0]):
            send_ref[peer, :rank] = total
            send_ref[peer, rank:] = note


def backward(ints, got, unit, x_own, t_own, mod, own, other, factor, s_own, s_other):
    groups, _, width = got.shape
    half = s_own.shape[1]
    rank = factor.shape[0]
    rows = CAP * BLK
    step = 256
    weight = pl.BlockSpec((width, step), lambda i: (0, i))
    cut = pl.BlockSpec((rows, step), lambda i: (0, i))
    block = whole((BLK, width))
    return pl.pallas_call(
        back_kernel,
        grid=(half // step,),
        out_shape=[
            jax.ShapeDtypeStruct((rows, half), BF16),
            jax.ShapeDtypeStruct((rows, half), BF16),
            jax.ShapeDtypeStruct((rows, rank), BF16),
            jax.ShapeDtypeStruct((groups, rank + NOTE, rows), BF16),
        ],
        in_specs=[
            pl.BlockSpec(memory_space=SMEM), whole(got.shape), block, block, block, whole(mod.shape),
            weight, weight, whole(factor.shape), cut, cut,
        ],
        out_specs=[cut, cut, whole((rows, rank)), whole((groups, rank + NOTE, rows))],
        scratch_shapes=[pltpu.VMEM((rank, rows), F32), pltpu.VMEM((rows, rank), F32)],
        compiler_params=params(),
        cost_estimate=cost(4 * rows * width * half, 4 * width * half + 12 * rows * half),
    )(ints, got, unit, x_own, t_own, mod, own, other, factor, s_own, s_other)


def factor_kernel(split_ref, do_ref, dt_ref, own_ref, other_ref):
    own_ref[...] = product(split_ref[...], do_ref[...])
    other_ref[...] = product(split_ref[...], dt_ref[...])


def factor_terms(split, d_own, d_other):
    lines, rows = split.shape
    half = d_own.shape[1]
    return pl.pallas_call(
        factor_kernel,
        out_shape=[jax.ShapeDtypeStruct((lines, half), F32)] * 2,
        compiler_params=params(),
        cost_estimate=cost(4 * lines * rows * half, 8 * lines * half),
    )(split, d_own, d_other)


def pile_kernel(
    ints_ref, got_ref, modded_ref, own_ref, other_ref, keep_ref, give_ref, facts_ref
):
    wins = ints_ref[0]
    core = ints_ref[5]
    groups, lines, rows = got_ref.shape
    rank = lines - NOTE
    half = own_ref.shape[1]
    gap_first = jnp.zeros((1, rows), F32)
    gap_second = jnp.zeros((1, rows), F32)
    for slot in range(groups):
        note = got_ref[slot, rank:].astype(F32)
        excess = note[0:1] + note[1:2] + note[2:3]
        gap_first += jnp.where(slot < wins, excess, 0.0)
        gap_second += jnp.where(slot < wins, 0.0, excess)
    width = modded_ref.shape[1]
    rows_first = (wins - 1) * BLK + ints_ref[2]
    rows_second = (ints_ref[1] - wins - 1) * BLK + ints_ref[3]
    scale_first = 1.0 / (width * jnp.full((1, rows), rows_first, jnp.int32).astype(F32))
    scale_second = 1.0 / (width * jnp.full((1, rows), rows_second, jnp.int32).astype(F32))
    inside = -BETA * (gap_first * scale_first - gap_second * scale_second)
    losses = jnp.maximum(-inside, 0.0) + jnp.log1p(jnp.exp(-jnp.abs(inside)))
    weight = BETA * LOSS_SCALE * jax.nn.sigmoid(-inside)
    first = weight * scale_first
    second = -weight * scale_second
    line = lax.broadcasted_iota(jnp.int32, facts_ref.shape, 0)
    facts_ref[...] = jnp.where(line == 0, losses, jnp.where(line == 1, first, second))
    slot = lax.broadcasted_iota(jnp.int32, (1, rows), 1) // BLK
    total = jnp.sum(got_ref[:, :rank].astype(F32), axis=0)
    dlow = (total * jnp.where(slot < wins, first, second)).astype(BF16)
    one = first[:, :1]
    two = second[:, :1]
    near = modded_ref[:, pl.ds(pl.multiple_of(core * half, 128), half)]
    far = modded_ref[:, pl.ds(pl.multiple_of((1 - core) * half, 128), half)]
    keep_ref[:rank] = one * own_ref[:rank] + two * own_ref[rank:]
    keep_ref[rank:] = product(dlow, near)
    give_ref[:rank] = (one * other_ref[:rank] + two * other_ref[rank:]).astype(BF16)
    give_ref[rank:] = product(dlow, far).astype(BF16)


def piles(ints, got, modded, b_own, b_other):
    lines, half = b_own.shape
    rows = got.shape[2]
    return pl.pallas_call(
        pile_kernel,
        out_shape=[
            jax.ShapeDtypeStruct((lines, half), F32),
            jax.ShapeDtypeStruct((lines, half), BF16),
            jax.ShapeDtypeStruct((8, rows), F32),
        ],
        in_specs=[pl.BlockSpec(memory_space=SMEM)] + [pl.BlockSpec(memory_space=pltpu.VMEM)] * 4,
        compiler_params=params(),
        cost_estimate=cost(2 * lines * half * rows, 16 * lines * half),
    )(ints, got, modded, b_own, b_other)


def dm_kernel(after_ref, do_ref, dt_ref, dlow_ref, own_ref, other_ref, a_ref, out_ref):
    total = rows_by_rows(do_ref[...], own_ref[...]) + rows_by_rows(dt_ref[...], other_ref[...])
    out_ref[...] = (total + product(dlow_ref[...], a_ref[...])).astype(BF16)


def dm_terms(after, d_own, d_other, dlow, own, other, a_turned):
    rows, half = d_own.shape
    width = own.shape[0]
    rank = dlow.shape[1]
    step = 512
    cut = pl.BlockSpec((step, half), lambda i: (i, 0))
    return pl.pallas_call(
        dm_kernel,
        grid=(width // step,),
        out_shape=jax.ShapeDtypeStruct((rows, width), BF16),
        in_specs=[
            pl.BlockSpec(memory_space=pl.ANY),
            whole((rows, half)),
            whole((rows, half)),
            whole((rows, rank)),
            cut,
            cut,
            pl.BlockSpec((rank, step), lambda i: (0, i)),
        ],
        out_specs=pl.BlockSpec((rows, step), lambda i: (0, i)),
        compiler_params=params(),
        cost_estimate=cost(4 * rows * width * half, 4 * width * half + 2 * rows * width),
    )(after, d_own, d_other, dlow, own, other, a_turned)


def token_kernel(ints_ref, one_ref, two_ref, three_ref, four_ref, x_ref, mod_ref, unit_ref, facts_ref, out_ref):
    total = one_ref[...].astype(F32) + two_ref[...].astype(F32)
    total = total + three_ref[...].astype(F32) + four_ref[...].astype(F32)
    normed, inverse = normalise(x_ref[...])
    first, _ = own_slot(ints_ref)
    coef = jnp.where(first, facts_ref[1:2, :1], facts_ref[2:3, :1])
    dn = total * (1.0 + pick(first, mod_ref, 1))
    mean_one = jnp.mean(dn, axis=-1, keepdims=True)
    mean_two = jnp.mean(dn * normed, axis=-1, keepdims=True)
    grad = coef * (unit_ref[...] + inverse * (dn - mean_one - normed * mean_two))
    out_ref[...] = grad.astype(BF16)


def token_gradient(ints, pieces, x_own, mod, unit, facts):
    rows, width = x_own.shape
    return pl.pallas_call(
        token_kernel,
        out_shape=jax.ShapeDtypeStruct((rows, width), BF16),
        in_specs=[pl.BlockSpec(memory_space=SMEM)] + [pl.BlockSpec(memory_space=pltpu.VMEM)] * 8,
        compiler_params=params(),
        cost_estimate=cost(20 * rows * width, 20 * rows * width),
    )(ints, *pieces, x_own, mod, unit, facts)


def per_device(
    tokens,
    targets,
    modulation,
    live_block_count,
    preferred_blocks,
    last_block_rows,
    up_rows,
    down_rows,
    factor_in,
    factor_out,
):
    width = tokens.shape[1]
    n_z, n_x, n_c, n_t = (lax.axis_size(a) for a in ("z", "x", "c", "t"))
    n_dp = n_z * n_x * n_c
    core = lax.axis_index("c")
    group = lax.axis_index("t")
    thin, hidden = up_rows.shape
    half = hidden // n_c
    rank = factor_in.shape[1]

    sent = jnp.stack([up_rows.reshape(thin, n_c, half), down_rows.reshape(thin, n_c, half)], axis=2)
    sent = sent.reshape(thin, n_c, 2 * half).transpose(1, 0, 2)
    sent = jnp.broadcast_to(sent[None], (n_x, n_c, thin, 2 * half)).reshape(n_x * n_c, thin, 2 * half)
    near = lax.all_to_all(sent, ("x", "c"), 0, 0, tiled=True).reshape(n_x * n_c * thin, 2 * half)
    own = lax.all_gather(near, "z", axis=0, tiled=True)

    ints = [preferred_blocks[0], live_block_count[0], last_block_rows[0, 0], last_block_rows[0, 1], group, core]
    ints = jnp.stack(ints).astype(jnp.int32)
    x_own = lax.dynamic_slice_in_dim(tokens, group * BLK, BLK, axis=0)
    t_own = lax.dynamic_slice_in_dim(targets, group * BLK, BLK, axis=0)
    mod = modulation.reshape(6, width)
    a_turned = factor_in.T
    modded, low, low_split = prepare(ints, tokens, mod, a_turned)

    own = after(own, [modded, low, low_split, x_own, t_own])
    other = lax.ppermute(own, "c", SWAP)

    pol_own, ref_own, slope_own = activate(False, ints, modded, low, own, factor_out)
    pol_other, ref_other, slope_other = activate(True, ints, modded, low, other, factor_out)
    part_pol = lower(pol_own, pol_other, own, other).reshape(CAP, BLK, width)
    got_pol = lax.all_to_all(part_pol, "t", 0, 0, tiled=True)
    part_ref = lower(ref_own, ref_other, own, other).reshape(CAP, BLK, width)

    unit, send = miss(ints, got_pol, part_ref, x_own, t_own, mod)
    down_own, down_other = own[:, half:], other[:, half:]
    send = after(send, [down_own, down_other])
    got_dy = lax.all_to_all(send, "t", 0, 0, tiled=True)
    d_own, d_other, dlow_part, send = backward(
        ints, got_dy, unit, x_own, t_own, mod, down_own, down_other, factor_out, slope_own, slope_other
    )
    got_low = lax.all_to_all(send, "t", 0, 0, tiled=True)
    b_own, b_other = factor_terms(low_split, d_own, d_other)
    keep, give, facts = piles(ints, got_low, modded, b_own, b_other)
    losses = facts[0, :1]
    pile = (keep + lax.ppermute(give, "c", SWAP).astype(F32)).astype(BF16)

    chips = n_z * n_x
    pieces = lax.all_to_all(pile.reshape(chips, 2 * rank // chips, half), CHIPS, 0, 0, tiled=True)
    dm_part = dm_terms(pile, d_own, d_other, dlow_part, own, other, a_turned).reshape(CAP, BLK, width)
    turns = [[(i, (i + step) % n_t) for i in range(n_t)] for step in range(n_t)]
    chunks = [lax.dynamic_index_in_dim(dm_part, (group + step) % n_t, 0, False) for step in range(n_t)]
    chunks = [chunks[0]] + [lax.ppermute(chunks[step], "t", turns[step]) for step in range(1, n_t)]
    total = (jnp.sum(pieces.astype(F32), axis=0) / n_dp).astype(BF16)
    total = after(total, chunks[1:])
    mine = spread(total, CHIPS, chips).reshape(2 * rank, half)
    grad_block = token_gradient(ints, chunks, x_own, mod, unit, facts)
    grad_tokens = lax.all_gather(grad_block, "t", axis=0, tiled=True)
    mine = after(mine, [grad_tokens])
    theirs = lax.ppermute(mine, "c", SWAP)
    ends = jnp.concatenate([mine, theirs], 1)
    flipped = jnp.concatenate([theirs, mine], 1)
    ends = jnp.where(core == 0, ends, flipped).astype(F32)
    sum_b = ends[:rank]
    sum_a = ends[rank:].T
    return losses, grad_tokens, sum_a, sum_b


def solution(mesh):
    n_dp, n_t = mesh.devices.shape
    fine = Mesh(mesh.devices.reshape(n_dp // 8, 4, 2, n_t), ("z", "x", "c", "t"))
    return jax.shard_map(
        per_device,
        mesh=fine,
        in_specs=(
            P(DP, None),
            P(DP, None),
            P(DP, None, None),
            P(DP),
            P(DP),
            P(DP, None),
            P(DP, "t"),
            P(DP, "t"),
            P(),
            P(None, "t"),
        ),
        out_specs=(P(DP), P(DP, None), P(), P(None, "t")),
        check_vma=False,
    )
```

```python
import functools

import jax
import jax.numpy as jnp
from jax import lax
from jax.experimental import pallas as pl
from jax.experimental.pallas import tpu as pltpu
from jax.sharding import Mesh
from jax.sharding import PartitionSpec as P

BLK = 64
CAP = 4
EPS = 1e-06
BETA = 20.0
LOSS_SCALE = 4096.0
ROOT = 0.7978845608028654
CUBE = 0.044715
BF16 = jnp.bfloat16
F32 = jnp.float32
DP = ("z", "x", "c")
CHIPS = ("z", "x")
SWAP = [(0, 1), (1, 0)]
NOTE = 16
VMEM_LIMIT = 40 * 1024 * 1024
SMEM = pltpu.SMEM


def gelu(pre):
    th = jnp.tanh(ROOT * (pre + CUBE * pre * pre * pre))
    return 0.5 * pre * (1.0 + th)


def gelu_and_slope(pre):
    square = pre * pre
    th = jnp.tanh(ROOT * (pre + CUBE * pre * square))
    half = 0.5 * (1.0 + th)
    slope = half + 0.5 * pre * (1.0 - th * th) * (ROOT * (1.0 + 3.0 * CUBE * square))
    return pre * half, slope


def rows_by_rows(left, right):
    return lax.dot_general(left, right, (((1,), (1,)), ((), ())), preferred_element_type=F32)


def product(left, right):
    return jnp.dot(left, right, preferred_element_type=F32)


def spread(value, axes, n):
    return lax.all_to_all(jnp.broadcast_to(value[None], (n, *value.shape)), axes, 0, 0, tiled=True)


def normalise(rows):
    wide = rows.astype(F32)
    center = wide - jnp.mean(wide, axis=-1, keepdims=True)
    inverse = lax.rsqrt(jnp.mean(center * center, axis=-1, keepdims=True) + EPS)
    return center * inverse, inverse


def params():
    return pltpu.CompilerParams(vmem_limit_bytes=VMEM_LIMIT)


def cost(flops, moved, tanh=0):
    return pl.CostEstimate(flops=flops, bytes_accessed=moved, transcendentals=tanh)


def whole(shape):
    return pl.BlockSpec(shape, lambda *_: (0,) * len(shape))


def input_kernel(wins_ref, x_ref, mod_ref, a_ref, modded_ref, low_ref, split_ref):
    wins = wins_ref[0]
    for slot in range(CAP):
        rows = slice(slot * BLK, (slot + 1) * BLK)
        normed, _ = normalise(x_ref[rows])
        first = slot < wins
        shift = jnp.where(first, mod_ref[0:1].astype(F32), mod_ref[3:4].astype(F32))
        scale = 1.0 + jnp.where(first, mod_ref[1:2].astype(F32), mod_ref[4:5].astype(F32))
        modded_ref[rows] = (normed * scale + shift).astype(BF16)
    modded = modded_ref[...]
    low_ref[...] = rows_by_rows(modded, a_ref[...]).astype(BF16)
    turned = rows_by_rows(a_ref[...], modded)
    second = lax.broadcasted_iota(jnp.int32, turned.shape, 1) // BLK >= wins
    rank = turned.shape[0]
    split_ref[:rank] = jnp.where(second, 0.0, turned).astype(BF16)
    split_ref[rank:] = jnp.where(second, turned, 0.0).astype(BF16)


def prepare(wins, tokens, mod, a_turned):
    rows, width = tokens.shape
    rank = a_turned.shape[0]
    return pl.pallas_call(
        input_kernel,
        out_shape=[
            jax.ShapeDtypeStruct((rows, width), BF16),
            jax.ShapeDtypeStruct((rows, rank), BF16),
            jax.ShapeDtypeStruct((2 * rank, rows), BF16),
        ],
        in_specs=[pl.BlockSpec(memory_space=SMEM)] + [pl.BlockSpec(memory_space=pltpu.VMEM)] * 3,
        compiler_params=params(),
        cost_estimate=cost(4 * rows * width * rank, 4 * rows * width),
    )(wins, tokens, mod, a_turned)


def own_slot(ints_ref):
    wins, count, slot = ints_ref[0], ints_ref[1], ints_ref[4]
    first = slot < wins
    last = jnp.where(first, wins - 1, count - 1)
    tail = jnp.where(first, ints_ref[2], ints_ref[3])
    return first, jnp.where(slot < count, jnp.where(slot == last, tail, BLK), 0)


def pick(first, ref, line):
    return jnp.where(first, ref[line : line + 1].astype(F32), ref[line + 3 : line + 4].astype(F32))


def after_kernel(*refs):
    del refs


def after(value, others):
    return pl.pallas_call(
        after_kernel,
        out_shape=jax.ShapeDtypeStruct(value.shape, value.dtype),
        in_specs=[pl.BlockSpec(memory_space=pl.ANY)] * (1 + len(others)),
        out_specs=pl.BlockSpec(memory_space=pl.ANY),
        input_output_aliases={0: 0},
    )(value, *others)


def half_of(core, step, half, size):
    return pl.ds(pl.multiple_of(core * half + step * size, 128), size)


def up_kernel(far, ints_ref, modded_ref, low_ref, up_ref, b_ref, pol_ref, ref_ref, slope_ref):
    core = 1 - ints_ref[5] if far else ints_ref[5]
    size = up_ref.shape[1]
    cut = half_of(core, pl.program_id(0), size * pl.num_programs(0), size)
    pre_ref = product(modded_ref[...], up_ref[...])
    pre_pol = pre_ref + product(low_ref[...], b_ref[:, cut])
    act, slope = gelu_and_slope(pre_pol)
    pol_ref[...] = act.astype(BF16)
    slope_ref[...] = slope.astype(BF16)
    ref_ref[...] = gelu(pre_ref).astype(BF16)


def activate(far, ints, modded, low, weights, factor):
    rows, width = modded.shape
    rank = factor.shape[0]
    half = factor.shape[1] // 2
    step = 256
    cut = pl.BlockSpec((rows, step), lambda i: (0, i))
    return pl.pallas_call(
        functools.partial(up_kernel, far),
        grid=(half // step,),
        out_shape=[
            jax.ShapeDtypeStruct((rows, half), BF16),
            jax.ShapeDtypeStruct((rows, half), BF16),
            jax.ShapeDtypeStruct((rows, half), BF16),
        ],
        in_specs=[
            pl.BlockSpec(memory_space=SMEM),
            whole((rows, width)),
            whole((rows, rank)),
            pl.BlockSpec((width, step), lambda i: (0, i)),
            whole(factor.shape),
        ],
        out_specs=[cut, cut, cut],
        compiler_params=params(),
        cost_estimate=cost(2 * rows * width * half, 2 * width * half + 10 * rows * half, 2 * rows * half),
    )(ints, modded, low, weights, factor)


def down_kernel(left_ref, right_ref, own_ref, other_ref, out_ref):
    total = rows_by_rows(left_ref[...], own_ref[...]) + rows_by_rows(right_ref[...], other_ref[...])
    out_ref[...] = total.astype(BF16)


def lower(left, right, own, other):
    rows, half = left.shape
    width = own.shape[0]
    step = 512
    cut = pl.BlockSpec((step, half), lambda i: (i, 0))
    return pl.pallas_call(
        down_kernel,
        grid=(width // step,),
        out_shape=jax.ShapeDtypeStruct((rows, width), BF16),
        in_specs=[whole((rows, half)), whole((rows, half)), cut, cut],
        out_specs=pl.BlockSpec((rows, step), lambda i: (0, i)),
        compiler_params=params(),
        cost_estimate=cost(4 * rows * width * half, 4 * width * half + 2 * rows * width),
    )(left, right, own, other)


def miss_kernel(ints_ref, got_ref, ref_ref, x_ref, t_ref, mod_ref, unit_ref, send_ref):
    first, live = own_slot(ints_ref)
    total = jnp.sum(got_ref[...].astype(F32), axis=0)
    gate = pick(first, mod_ref, 2)
    unit = 2.0 * (x_ref[...].astype(F32) - t_ref[...].astype(F32) + gate * total)
    unit = jnp.where(lax.broadcasted_iota(jnp.int32, unit.shape, 0) < live, unit, 0.0)
    unit_ref[...] = unit
    dy = (gate * unit).astype(BF16)
    for peer in range(send_ref.shape[0]):
        send_ref[peer, :BLK] = dy
        send_ref[peer, BLK:] = ref_ref[peer]


def miss(ints, got, part_ref, x_own, t_own, mod):
    groups, rows, width = got.shape
    return pl.pallas_call(
        miss_kernel,
        out_shape=[
            jax.ShapeDtypeStruct((rows, width), F32),
            jax.ShapeDtypeStruct((groups, 2 * rows, width), BF16),
        ],
        in_specs=[pl.BlockSpec(memory_space=SMEM)] + [pl.BlockSpec(memory_space=pltpu.VMEM)] * 5,
        compiler_params=params(),
        cost_estimate=cost(20 * rows * width, 8 * groups * rows * width),
    )(ints, got, part_ref, x_own, t_own, mod)


def back_kernel(
    ints_ref, got_ref, unit_ref, x_ref, t_ref, mod_ref, own_ref, other_ref, b_ref, so_ref, st_ref,
    do_ref, dt_ref, dlow_ref, send_ref, turned_scr, straight_scr,
):
    step = pl.program_id(0)
    core = ints_ref[5]
    width = got_ref.shape[2]
    size = so_ref.shape[1]
    half = size * pl.num_programs(0)
    b_own = b_ref[:, half_of(core, step, half, size)]
    b_other = b_ref[:, half_of(1 - core, step, half, size)]
    dy = got_ref[:, :BLK].reshape(CAP * BLK, width)
    d_own = (product(dy, own_ref[...]) * so_ref[...].astype(F32)).astype(BF16)
    d_other = (product(dy, other_ref[...]) * st_ref[...].astype(F32)).astype(BF16)
    do_ref[...] = d_own
    dt_ref[...] = d_other
    turned = rows_by_rows(b_own, d_own) + rows_by_rows(b_other, d_other)
    straight = rows_by_rows(d_own, b_own) + rows_by_rows(d_other, b_other)

    @pl.when(step == 0)
    def _():
        turned_scr[...] = turned
        straight_scr[...] = straight

    @pl.when(step > 0)
    def _():
        turned_scr[...] += turned
        straight_scr[...] += straight

    @pl.when(step == pl.num_programs(0) - 1)
    def _():
        rank = turned_scr.shape[0]
        dlow_ref[...] = straight_scr[...].astype(BF16)
        first, live = own_slot(ints_ref)
        base = x_ref[...].astype(F32) - t_ref[...].astype(F32)
        miss_ref = base + pick(first, mod_ref, 2) * jnp.sum(got_ref[:, BLK:].astype(F32), axis=0)
        miss_ref = jnp.where(lax.broadcasted_iota(jnp.int32, miss_ref.shape, 0) < live, miss_ref, 0.0)
        miss_pol = 0.5 * unit_ref[...]
        parts = jnp.sum((miss_pol - miss_ref) * (miss_pol + miss_ref), axis=1, keepdims=True)
        excess = jnp.broadcast_to(jnp.sum(parts, axis=0, keepdims=True), (NOTE, CAP * BLK))
        high = excess.astype(BF16)
        rest = excess - high.astype(F32)
        middle = rest.astype(BF16)
        lowest = rest - middle.astype(F32)
        line = lax.broadcasted_iota(jnp.int32, excess.shape, 0)
        note = jnp.where(line == 0, high.astype(F32), jnp.where(line == 1, middle.astype(F32), lowest)).astype(BF16)
        total = turned_scr[...].astype(BF16)
        for peer in range(send_ref.shape[0]):
            send_ref[peer, :rank] = total
            send_ref[peer, rank:] = note


def backward(ints, got, unit, x_own, t_own, mod, own, other, factor, s_own, s_other):
    groups, _, width = got.shape
    half = s_own.shape[1]
    rank = factor.shape[0]
    rows = CAP * BLK
    step = 256
    weight = pl.BlockSpec((width, step), lambda i: (0, i))
    cut = pl.BlockSpec((rows, step), lambda i: (0, i))
    block = whole((BLK, width))
    return pl.pallas_call(
        back_kernel,
        grid=(half // step,),
        out_shape=[
            jax.ShapeDtypeStruct((rows, half), BF16),
            jax.ShapeDtypeStruct((rows, half), BF16),
            jax.ShapeDtypeStruct((rows, rank), BF16),
            jax.ShapeDtypeStruct((groups, rank + NOTE, rows), BF16),
        ],
        in_specs=[
            pl.BlockSpec(memory_space=SMEM), whole(got.shape), block, block, block, whole(mod.shape),
            weight, weight, whole(factor.shape), cut, cut,
        ],
        out_specs=[cut, cut, whole((rows, rank)), whole((groups, rank + NOTE, rows))],
        scratch_shapes=[pltpu.VMEM((rank, rows), F32), pltpu.VMEM((rows, rank), F32)],
        compiler_params=params(),
        cost_estimate=cost(4 * rows * width * half, 4 * width * half + 12 * rows * half),
    )(ints, got, unit, x_own, t_own, mod, own, other, factor, s_own, s_other)


def factor_kernel(split_ref, do_ref, dt_ref, own_ref, other_ref):
    own_ref[...] = product(split_ref[...], do_ref[...])
    other_ref[...] = product(split_ref[...], dt_ref[...])


def factor_terms(split, d_own, d_other):
    lines, rows = split.shape
    half = d_own.shape[1]
    return pl.pallas_call(
        factor_kernel,
        out_shape=[jax.ShapeDtypeStruct((lines, half), F32)] * 2,
        compiler_params=params(),
        cost_estimate=cost(4 * lines * rows * half, 8 * lines * half),
    )(split, d_own, d_other)


def pile_kernel(
    ints_ref, got_ref, modded_ref, own_ref, other_ref, keep_ref, give_ref, facts_ref
):
    wins = ints_ref[0]
    core = ints_ref[5]
    groups, lines, rows = got_ref.shape
    rank = lines - NOTE
    half = own_ref.shape[1]
    gap_first = jnp.zeros((1, rows), F32)
    gap_second = jnp.zeros((1, rows), F32)
    for slot in range(groups):
        note = got_ref[slot, rank:].astype(F32)
        excess = note[0:1] + note[1:2] + note[2:3]
        gap_first += jnp.where(slot < wins, excess, 0.0)
        gap_second += jnp.where(slot < wins, 0.0, excess)
    width = modded_ref.shape[1]
    rows_first = (wins - 1) * BLK + ints_ref[2]
    rows_second = (ints_ref[1] - wins - 1) * BLK + ints_ref[3]
    scale_first = 1.0 / (width * jnp.full((1, rows), rows_first, jnp.int32).astype(F32))
    scale_second = 1.0 / (width * jnp.full((1, rows), rows_second, jnp.int32).astype(F32))
    inside = -BETA * (gap_first * scale_first - gap_second * scale_second)
    losses = jnp.maximum(-inside, 0.0) + jnp.log1p(jnp.exp(-jnp.abs(inside)))
    weight = BETA * LOSS_SCALE * jax.nn.sigmoid(-inside)
    first = weight * scale_first
    second = -weight * scale_second
    line = lax.broadcasted_iota(jnp.int32, facts_ref.shape, 0)
    facts_ref[...] = jnp.where(line == 0, losses, jnp.where(line == 1, first, second))
    slot = lax.broadcasted_iota(jnp.int32, (1, rows), 1) // BLK
    total = jnp.sum(got_ref[:, :rank].astype(F32), axis=0)
    dlow = (total * jnp.where(slot < wins, first, second)).astype(BF16)
    one = first[:, :1]
    two = second[:, :1]
    near = modded_ref[:, pl.ds(pl.multiple_of(core * half, 128), half)]
    far = modded_ref[:, pl.ds(pl.multiple_of((1 - core) * half, 128), half)]
    keep_ref[:rank] = one * own_ref[:rank] + two * own_ref[rank:]
    keep_ref[rank:] = product(dlow, near)
    give_ref[:rank] = (one * other_ref[:rank] + two * other_ref[rank:]).astype(BF16)
    give_ref[rank:] = product(dlow, far).astype(BF16)


def piles(ints, got, modded, b_own, b_other):
    lines, half = b_own.shape
    rows = got.shape[2]
    return pl.pallas_call(
        pile_kernel,
        out_shape=[
            jax.ShapeDtypeStruct((lines, half), F32),
            jax.ShapeDtypeStruct((lines, half), BF16),
            jax.ShapeDtypeStruct((8, rows), F32),
        ],
        in_specs=[pl.BlockSpec(memory_space=SMEM)] + [pl.BlockSpec(memory_space=pltpu.VMEM)] * 4,
        compiler_params=params(),
        cost_estimate=cost(2 * lines * half * rows, 16 * lines * half),
    )(ints, got, modded, b_own, b_other)


def dm_kernel(after_ref, do_ref, dt_ref, dlow_ref, own_ref, other_ref, a_ref, out_ref):
    total = rows_by_rows(do_ref[...], own_ref[...]) + rows_by_rows(dt_ref[...], other_ref[...])
    out_ref[...] = (total + product(dlow_ref[...], a_ref[...])).astype(BF16)


def dm_terms(after, d_own, d_other, dlow, own, other, a_turned):
    rows, half = d_own.shape
    width = own.shape[0]
    rank = dlow.shape[1]
    step = 512
    cut = pl.BlockSpec((step, half), lambda i: (i, 0))
    return pl.pallas_call(
        dm_kernel,
        grid=(width // step,),
        out_shape=jax.ShapeDtypeStruct((rows, width), BF16),
        in_specs=[
            pl.BlockSpec(memory_space=pl.ANY),
            whole((rows, half)),
            whole((rows, half)),
            whole((rows, rank)),
            cut,
            cut,
            pl.BlockSpec((rank, step), lambda i: (0, i)),
        ],
        out_specs=pl.BlockSpec((rows, step), lambda i: (0, i)),
        compiler_params=params(),
        cost_estimate=cost(4 * rows * width * half, 4 * width * half + 2 * rows * width),
    )(after, d_own, d_other, dlow, own, other, a_turned)


def token_kernel(ints_ref, one_ref, two_ref, three_ref, four_ref, x_ref, mod_ref, unit_ref, facts_ref, out_ref):
    total = one_ref[...].astype(F32) + two_ref[...].astype(F32)
    total = total + three_ref[...].astype(F32) + four_ref[...].astype(F32)
    normed, inverse = normalise(x_ref[...])
    first, _ = own_slot(ints_ref)
    coef = jnp.where(first, facts_ref[1:2, :1], facts_ref[2:3, :1])
    dn = total * (1.0 + pick(first, mod_ref, 1))
    mean_one = jnp.mean(dn, axis=-1, keepdims=True)
    mean_two = jnp.mean(dn * normed, axis=-1, keepdims=True)
    grad = coef * (unit_ref[...] + inverse * (dn - mean_one - normed * mean_two))
    out_ref[...] = grad.astype(BF16)


def token_gradient(ints, pieces, x_own, mod, unit, facts):
    rows, width = x_own.shape
    return pl.pallas_call(
        token_kernel,
        out_shape=jax.ShapeDtypeStruct((rows, width), BF16),
        in_specs=[pl.BlockSpec(memory_space=SMEM)] + [pl.BlockSpec(memory_space=pltpu.VMEM)] * 8,
        compiler_params=params(),
        cost_estimate=cost(20 * rows * width, 20 * rows * width),
    )(ints, *pieces, x_own, mod, unit, facts)


def per_device(
    tokens,
    targets,
    modulation,
    live_block_count,
    preferred_blocks,
    last_block_rows,
    up_rows,
    down_rows,
    factor_in,
    factor_out,
):
    width = tokens.shape[1]
    n_z, n_x, n_c, n_t = (lax.axis_size(a) for a in ("z", "x", "c", "t"))
    n_dp = n_z * n_x * n_c
    core = lax.axis_index("c")
    group = lax.axis_index("t")
    thin, hidden = up_rows.shape
    half = hidden // n_c
    rank = factor_in.shape[1]

    sent = down_rows.reshape(thin, n_c, half).transpose(1, 0, 2)
    sent = jnp.broadcast_to(sent[None], (n_x, n_c, thin, half)).reshape(n_x * n_c, thin, half)
    near = lax.all_to_all(sent, ("x", "c"), 0, 0, tiled=True)
    down_own = lax.all_gather(near.reshape(n_x * n_c * thin, half), "z", axis=0, tiled=True)

    up_rows, near = lax.optimization_barrier((up_rows, near))
    keep = lax.dynamic_slice_in_dim(up_rows, core * half, half, axis=1)
    got = lax.ppermute(lax.dynamic_slice_in_dim(up_rows, (1 - core) * half, half, axis=1), "c", SWAP)
    pair = jnp.where(core == 0, jnp.concatenate([keep, got], 0), jnp.concatenate([got, keep], 0))
    line = lax.all_gather(pair, "z", axis=0, tiled=True)

    ints = [preferred_blocks[0], live_block_count[0], last_block_rows[0, 0], last_block_rows[0, 1], group, core]
    ints = jnp.stack(ints).astype(jnp.int32)
    x_own = lax.dynamic_slice_in_dim(tokens, group * BLK, BLK, axis=0)
    t_own = lax.dynamic_slice_in_dim(targets, group * BLK, BLK, axis=0)
    mod = modulation.reshape(6, width)
    a_turned = factor_in.T
    modded, low, low_split = prepare(ints, tokens, mod, a_turned)

    blocks = after(spread(line, "x", n_x), [modded, low, low_split, x_own, t_own])
    up_own = blocks.reshape(n_x, n_z, n_c * thin, half).transpose(1, 0, 2, 3).reshape(width, half)
    up_other = lax.ppermute(up_own, "c", SWAP)
    down_other = lax.ppermute(down_own, "c", SWAP)

    pol_own, ref_own, slope_own = activate(False, ints, modded, low, up_own, factor_out)
    pol_other, ref_other, slope_other = activate(True, ints, modded, low, up_other, factor_out)
    part_pol = lower(pol_own, pol_other, down_own, down_other).reshape(CAP, BLK, width)
    got_pol = lax.all_to_all(part_pol, "t", 0, 0, tiled=True)
    part_ref = lower(ref_own, ref_other, down_own, down_other).reshape(CAP, BLK, width)

    unit, send = miss(ints, got_pol, part_ref, x_own, t_own, mod)
    got_dy = lax.all_to_all(send, "t", 0, 0, tiled=True)
    d_own, d_other, dlow_part, send = backward(
        ints, got_dy, unit, x_own, t_own, mod, down_own, down_other, factor_out, slope_own, slope_other
    )
    got_low = lax.all_to_all(send, "t", 0, 0, tiled=True)
    b_own, b_other = factor_terms(low_split, d_own, d_other)
    keep, give, facts = piles(ints, got_low, modded, b_own, b_other)
    losses = facts[0, :1]
    pile = (keep + lax.ppermute(give, "c", SWAP).astype(F32)).astype(BF16)

    chips = n_z * n_x
    pieces = lax.all_to_all(pile.reshape(chips, 2 * rank // chips, half), CHIPS, 0, 0, tiled=True)
    dm_part = dm_terms(pile, d_own, d_other, dlow_part, up_own, up_other, a_turned).reshape(CAP, BLK, width)
    turns = [[(i, (i + step) % n_t) for i in range(n_t)] for step in range(n_t)]
    chunks = [lax.dynamic_index_in_dim(dm_part, (group + step) % n_t, 0, False) for step in range(n_t)]
    chunks = [chunks[0]] + [lax.ppermute(chunks[step], "t", turns[step]) for step in range(1, n_t)]
    total = (jnp.sum(pieces.astype(F32), axis=0) / n_dp).astype(BF16)
    mine = spread(total, CHIPS, chips).reshape(2 * rank, half)
    grad_block = token_gradient(ints, chunks, x_own, mod, unit, facts)
    shares = [grad_block] + [lax.ppermute(grad_block, "t", turns[step]) for step in range(1, n_t)]
    shares = jnp.stack(shares)
    grad_tokens = jnp.concatenate(
        [lax.dynamic_index_in_dim(shares, (group - slot) % n_t, 0, False) for slot in range(n_t)], 0
    )
    theirs = lax.ppermute(mine, "c", SWAP)
    ends = jnp.concatenate([mine, theirs], 1)
    flipped = jnp.concatenate([theirs, mine], 1)
    ends = jnp.where(core == 0, ends, flipped).astype(F32)
    sum_b = ends[:rank]
    sum_a = ends[rank:].T
    return losses, grad_tokens, sum_a, sum_b


def solution(mesh):
    n_dp, n_t = mesh.devices.shape
    fine = Mesh(mesh.devices.reshape(n_dp // 8, 4, 2, n_t), ("z", "x", "c", "t"))
    return jax.shard_map(
        per_device,
        mesh=fine,
        in_specs=(
            P(DP, None),
            P(DP, None),
            P(DP, None, None),
            P(DP),
            P(DP),
            P(DP, None),
            P(DP, "t"),
            P(DP, "t"),
            P(),
            P(None, "t"),
        ),
        out_specs=(P(DP), P(DP, None), P(), P(None, "t")),
        check_vma=False,
    )
```

```python
import functools

import jax
import jax.numpy as jnp
from jax import lax
from jax.experimental import pallas as pl
from jax.experimental.pallas import tpu as pltpu
from jax.sharding import Mesh
from jax.sharding import PartitionSpec as P

BLK = 64
CAP = 4
EPS = 1e-06
BETA = 20.0
LOSS_SCALE = 4096.0
ROOT = 0.7978845608028654
CUBE = 0.044715
BF16 = jnp.bfloat16
F32 = jnp.float32
DP = ("z", "x", "c")
CHIPS = ("z", "x")
SWAP = [(0, 1), (1, 0)]
NOTE = 16
VMEM_LIMIT = 40 * 1024 * 1024
SMEM = pltpu.SMEM


def gelu(pre):
    th = jnp.tanh(ROOT * (pre + CUBE * pre * pre * pre))
    return 0.5 * pre * (1.0 + th)


def gelu_and_slope(pre):
    square = pre * pre
    th = jnp.tanh(ROOT * (pre + CUBE * pre * square))
    half = 0.5 * (1.0 + th)
    slope = half + 0.5 * pre * (1.0 - th * th) * (ROOT * (1.0 + 3.0 * CUBE * square))
    return pre * half, slope


def rows_by_rows(left, right):
    return lax.dot_general(left, right, (((1,), (1,)), ((), ())), preferred_element_type=F32)


def product(left, right):
    return jnp.dot(left, right, preferred_element_type=F32)


def spread(value, axes, n):
    return lax.all_to_all(jnp.broadcast_to(value[None], (n, *value.shape)), axes, 0, 0, tiled=True)


def normalise(rows):
    wide = rows.astype(F32)
    center = wide - jnp.mean(wide, axis=-1, keepdims=True)
    inverse = lax.rsqrt(jnp.mean(center * center, axis=-1, keepdims=True) + EPS)
    return center * inverse, inverse


def params():
    return pltpu.CompilerParams(vmem_limit_bytes=VMEM_LIMIT)


def cost(flops, moved, tanh=0):
    return pl.CostEstimate(flops=flops, bytes_accessed=moved, transcendentals=tanh)


def whole(shape):
    return pl.BlockSpec(shape, lambda *_: (0,) * len(shape))


def input_kernel(wins_ref, x_ref, mod_ref, a_ref, modded_ref, low_ref, split_ref):
    wins = wins_ref[0]
    for slot in range(CAP):
        rows = slice(slot * BLK, (slot + 1) * BLK)
        normed, _ = normalise(x_ref[rows])
        first = slot < wins
        shift = jnp.where(first, mod_ref[0:1].astype(F32), mod_ref[3:4].astype(F32))
        scale = 1.0 + jnp.where(first, mod_ref[1:2].astype(F32), mod_ref[4:5].astype(F32))
        modded_ref[rows] = (normed * scale + shift).astype(BF16)
    modded = modded_ref[...]
    low_ref[...] = rows_by_rows(modded, a_ref[...]).astype(BF16)
    turned = rows_by_rows(a_ref[...], modded)
    second = lax.broadcasted_iota(jnp.int32, turned.shape, 1) // BLK >= wins
    rank = turned.shape[0]
    split_ref[:rank] = jnp.where(second, 0.0, turned).astype(BF16)
    split_ref[rank:] = jnp.where(second, turned, 0.0).astype(BF16)


def prepare(wins, tokens, mod, a_turned):
    rows, width = tokens.shape
    rank = a_turned.shape[0]
    return pl.pallas_call(
        input_kernel,
        out_shape=[
            jax.ShapeDtypeStruct((rows, width), BF16),
            jax.ShapeDtypeStruct((rows, rank), BF16),
            jax.ShapeDtypeStruct((2 * rank, rows), BF16),
        ],
        in_specs=[pl.BlockSpec(memory_space=SMEM)] + [pl.BlockSpec(memory_space=pltpu.VMEM)] * 3,
        compiler_params=params(),
        cost_estimate=cost(4 * rows * width * rank, 4 * rows * width),
    )(wins, tokens, mod, a_turned)


def own_slot(ints_ref):
    wins, count, slot = ints_ref[0], ints_ref[1], ints_ref[4]
    first = slot < wins
    last = jnp.where(first, wins - 1, count - 1)
    tail = jnp.where(first, ints_ref[2], ints_ref[3])
    return first, jnp.where(slot < count, jnp.where(slot == last, tail, BLK), 0)


def pick(first, ref, line):
    return jnp.where(first, ref[line : line + 1].astype(F32), ref[line + 3 : line + 4].astype(F32))


def after_kernel(*refs):
    del refs


def after(value, others):
    return pl.pallas_call(
        after_kernel,
        out_shape=jax.ShapeDtypeStruct(value.shape, value.dtype),
        in_specs=[pl.BlockSpec(memory_space=pl.ANY)] * (1 + len(others)),
        out_specs=pl.BlockSpec(memory_space=pl.ANY),
        input_output_aliases={0: 0},
    )(value, *others)


def swapped(index, outer, inner, unit):
    first = sum((index >= k * inner * unit).astype(jnp.int32) for k in range(1, outer))
    rest = index - first * (inner * unit)
    second = sum((rest >= k * unit).astype(jnp.int32) for k in range(1, inner))
    return second * (outer * unit) + first * unit + rest - second * unit


def places(start, size, width, outer, inner, unit):
    column = swapped(lax.broadcasted_iota(jnp.int32, (1, size), 1) + start, outer, inner, unit)
    line = lax.broadcasted_iota(jnp.int32, (width, size), 0)
    return jnp.where(line == column, 1.0, 0.0).astype(BF16)


def reorder_kernel(order, modded_ref, a_ref, modded_out, a_out):
    size = modded_out.shape[1]
    turn = places(pl.program_id(0) * size, size, modded_ref.shape[1], *order)
    modded_out[...] = product(modded_ref[...], turn).astype(BF16)
    a_out[...] = product(a_ref[...], turn).astype(BF16)


def reorder(order, modded, a_turned):
    rows, width = modded.shape
    rank = a_turned.shape[0]
    step = 256
    cuts = [pl.BlockSpec((rows, step), lambda i: (0, i)), pl.BlockSpec((rank, step), lambda i: (0, i))]
    return pl.pallas_call(
        functools.partial(reorder_kernel, order),
        grid=(width // step,),
        out_shape=[jax.ShapeDtypeStruct((rows, width), BF16), jax.ShapeDtypeStruct((rank, width), BF16)],
        in_specs=[whole((rows, width)), whole((rank, width))],
        out_specs=cuts,
        compiler_params=params(),
        cost_estimate=cost(2 * (rows + rank) * width * width, 8 * rows * width),
    )(modded, a_turned)


def half_of(core, step, half, size):
    return pl.ds(pl.multiple_of(core * half + step * size, 128), size)


def up_kernel(far, ints_ref, modded_ref, low_ref, up_ref, b_ref, pol_ref, ref_ref, slope_ref):
    core = 1 - ints_ref[5] if far else ints_ref[5]
    size = up_ref.shape[1]
    cut = half_of(core, pl.program_id(0), size * pl.num_programs(0), size)
    pre_ref = product(modded_ref[...], up_ref[...])
    pre_pol = pre_ref + product(low_ref[...], b_ref[:, cut])
    act, slope = gelu_and_slope(pre_pol)
    pol_ref[...] = act.astype(BF16)
    slope_ref[...] = slope.astype(BF16)
    ref_ref[...] = gelu(pre_ref).astype(BF16)


def activate(far, ints, modded, low, weights, factor):
    rows, width = modded.shape
    rank = factor.shape[0]
    half = factor.shape[1] // 2
    step = 256
    cut = pl.BlockSpec((rows, step), lambda i: (0, i))
    return pl.pallas_call(
        functools.partial(up_kernel, far),
        grid=(half // step,),
        out_shape=[
            jax.ShapeDtypeStruct((rows, half), BF16),
            jax.ShapeDtypeStruct((rows, half), BF16),
            jax.ShapeDtypeStruct((rows, half), BF16),
        ],
        in_specs=[
            pl.BlockSpec(memory_space=SMEM),
            whole((rows, width)),
            whole((rows, rank)),
            pl.BlockSpec((width, step), lambda i: (0, i)),
            whole(factor.shape),
        ],
        out_specs=[cut, cut, cut],
        compiler_params=params(),
        cost_estimate=cost(2 * rows * width * half, 2 * width * half + 10 * rows * half, 2 * rows * half),
    )(ints, modded, low, weights, factor)


def down_kernel(left_ref, right_ref, own_ref, other_ref, out_ref):
    total = rows_by_rows(left_ref[...], own_ref[...]) + rows_by_rows(right_ref[...], other_ref[...])
    out_ref[...] = total.astype(BF16)


def lower(left, right, own, other):
    rows, half = left.shape
    width = own.shape[0]
    step = 512
    cut = pl.BlockSpec((step, half), lambda i: (i, 0))
    return pl.pallas_call(
        down_kernel,
        grid=(width // step,),
        out_shape=jax.ShapeDtypeStruct((rows, width), BF16),
        in_specs=[whole((rows, half)), whole((rows, half)), cut, cut],
        out_specs=pl.BlockSpec((rows, step), lambda i: (0, i)),
        compiler_params=params(),
        cost_estimate=cost(4 * rows * width * half, 4 * width * half + 2 * rows * width),
    )(left, right, own, other)


def miss_kernel(ints_ref, got_ref, ref_ref, x_ref, t_ref, mod_ref, unit_ref, send_ref):
    first, live = own_slot(ints_ref)
    total = jnp.sum(got_ref[...].astype(F32), axis=0)
    gate = pick(first, mod_ref, 2)
    unit = 2.0 * (x_ref[...].astype(F32) - t_ref[...].astype(F32) + gate * total)
    unit = jnp.where(lax.broadcasted_iota(jnp.int32, unit.shape, 0) < live, unit, 0.0)
    unit_ref[...] = unit
    dy = (gate * unit).astype(BF16)
    for peer in range(send_ref.shape[0]):
        send_ref[peer, :BLK] = dy
        send_ref[peer, BLK:] = ref_ref[peer]


def miss(ints, got, part_ref, x_own, t_own, mod):
    groups, rows, width = got.shape
    return pl.pallas_call(
        miss_kernel,
        out_shape=[
            jax.ShapeDtypeStruct((rows, width), F32),
            jax.ShapeDtypeStruct((groups, 2 * rows, width), BF16),
        ],
        in_specs=[pl.BlockSpec(memory_space=SMEM)] + [pl.BlockSpec(memory_space=pltpu.VMEM)] * 5,
        compiler_params=params(),
        cost_estimate=cost(20 * rows * width, 8 * groups * rows * width),
    )(ints, got, part_ref, x_own, t_own, mod)


def back_kernel(
    ints_ref, got_ref, unit_ref, x_ref, t_ref, mod_ref, own_ref, other_ref, b_ref, so_ref, st_ref,
    do_ref, dt_ref, dlow_ref, send_ref, turned_scr, straight_scr,
):
    step = pl.program_id(0)
    core = ints_ref[5]
    width = got_ref.shape[2]
    size = so_ref.shape[1]
    half = size * pl.num_programs(0)
    b_own = b_ref[:, half_of(core, step, half, size)]
    b_other = b_ref[:, half_of(1 - core, step, half, size)]
    dy = got_ref[:, :BLK].reshape(CAP * BLK, width)
    d_own = (product(dy, own_ref[...]) * so_ref[...].astype(F32)).astype(BF16)
    d_other = (product(dy, other_ref[...]) * st_ref[...].astype(F32)).astype(BF16)
    do_ref[...] = d_own
    dt_ref[...] = d_other
    turned = rows_by_rows(b_own, d_own) + rows_by_rows(b_other, d_other)
    straight = rows_by_rows(d_own, b_own) + rows_by_rows(d_other, b_other)

    @pl.when(step == 0)
    def _():
        turned_scr[...] = turned
        straight_scr[...] = straight

    @pl.when(step > 0)
    def _():
        turned_scr[...] += turned
        straight_scr[...] += straight

    @pl.when(step == pl.num_programs(0) - 1)
    def _():
        rank = turned_scr.shape[0]
        dlow_ref[...] = straight_scr[...].astype(BF16)
        first, live = own_slot(ints_ref)
        base = x_ref[...].astype(F32) - t_ref[...].astype(F32)
        miss_ref = base + pick(first, mod_ref, 2) * jnp.sum(got_ref[:, BLK:].astype(F32), axis=0)
        miss_ref = jnp.where(lax.broadcasted_iota(jnp.int32, miss_ref.shape, 0) < live, miss_ref, 0.0)
        miss_pol = 0.5 * unit_ref[...]
        parts = jnp.sum((miss_pol - miss_ref) * (miss_pol + miss_ref), axis=1, keepdims=True)
        excess = jnp.broadcast_to(jnp.sum(parts, axis=0, keepdims=True), (NOTE, CAP * BLK))
        high = excess.astype(BF16)
        rest = excess - high.astype(F32)
        middle = rest.astype(BF16)
        lowest = rest - middle.astype(F32)
        line = lax.broadcasted_iota(jnp.int32, excess.shape, 0)
        note = jnp.where(line == 0, high.astype(F32), jnp.where(line == 1, middle.astype(F32), lowest)).astype(BF16)
        total = turned_scr[...].astype(BF16)
        for peer in range(send_ref.shape[0]):
            send_ref[peer, :rank] = total
            send_ref[peer, rank:] = note


def backward(ints, got, unit, x_own, t_own, mod, own, other, factor, s_own, s_other):
    groups, _, width = got.shape
    half = s_own.shape[1]
    rank = factor.shape[0]
    rows = CAP * BLK
    step = 256
    weight = pl.BlockSpec((width, step), lambda i: (0, i))
    cut = pl.BlockSpec((rows, step), lambda i: (0, i))
    block = whole((BLK, width))
    return pl.pallas_call(
        back_kernel,
        grid=(half // step,),
        out_shape=[
            jax.ShapeDtypeStruct((rows, half), BF16),
            jax.ShapeDtypeStruct((rows, half), BF16),
            jax.ShapeDtypeStruct((rows, rank), BF16),
            jax.ShapeDtypeStruct((groups, rank + NOTE, rows), BF16),
        ],
        in_specs=[
            pl.BlockSpec(memory_space=SMEM), whole(got.shape), block, block, block, whole(mod.shape),
            weight, weight, whole(factor.shape), cut, cut,
        ],
        out_specs=[cut, cut, whole((rows, rank)), whole((groups, rank + NOTE, rows))],
        scratch_shapes=[pltpu.VMEM((rank, rows), F32), pltpu.VMEM((rows, rank), F32)],
        compiler_params=params(),
        cost_estimate=cost(4 * rows * width * half, 4 * width * half + 12 * rows * half),
    )(ints, got, unit, x_own, t_own, mod, own, other, factor, s_own, s_other)


def factor_kernel(split_ref, do_ref, dt_ref, own_ref, other_ref):
    own_ref[...] = product(split_ref[...], do_ref[...])
    other_ref[...] = product(split_ref[...], dt_ref[...])


def factor_terms(split, d_own, d_other):
    lines, rows = split.shape
    half = d_own.shape[1]
    return pl.pallas_call(
        factor_kernel,
        out_shape=[jax.ShapeDtypeStruct((lines, half), F32)] * 2,
        compiler_params=params(),
        cost_estimate=cost(4 * lines * rows * half, 8 * lines * half),
    )(split, d_own, d_other)


def pile_kernel(
    ints_ref, got_ref, modded_ref, own_ref, other_ref, keep_ref, give_ref, facts_ref
):
    wins = ints_ref[0]
    core = ints_ref[5]
    groups, lines, rows = got_ref.shape
    rank = lines - NOTE
    half = own_ref.shape[1]
    gap_first = jnp.zeros((1, rows), F32)
    gap_second = jnp.zeros((1, rows), F32)
    for slot in range(groups):
        note = got_ref[slot, rank:].astype(F32)
        excess = note[0:1] + note[1:2] + note[2:3]
        gap_first += jnp.where(slot < wins, excess, 0.0)
        gap_second += jnp.where(slot < wins, 0.0, excess)
    width = modded_ref.shape[1]
    rows_first = (wins - 1) * BLK + ints_ref[2]
    rows_second = (ints_ref[1] - wins - 1) * BLK + ints_ref[3]
    scale_first = 1.0 / (width * jnp.full((1, rows), rows_first, jnp.int32).astype(F32))
    scale_second = 1.0 / (width * jnp.full((1, rows), rows_second, jnp.int32).astype(F32))
    inside = -BETA * (gap_first * scale_first - gap_second * scale_second)
    losses = jnp.maximum(-inside, 0.0) + jnp.log1p(jnp.exp(-jnp.abs(inside)))
    weight = BETA * LOSS_SCALE * jax.nn.sigmoid(-inside)
    first = weight * scale_first
    second = -weight * scale_second
    line = lax.broadcasted_iota(jnp.int32, facts_ref.shape, 0)
    facts_ref[...] = jnp.where(line == 0, losses, jnp.where(line == 1, first, second))
    slot = lax.broadcasted_iota(jnp.int32, (1, rows), 1) // BLK
    total = jnp.sum(got_ref[:, :rank].astype(F32), axis=0)
    dlow = (total * jnp.where(slot < wins, first, second)).astype(BF16)
    one = first[:, :1]
    two = second[:, :1]
    near = modded_ref[:, pl.ds(pl.multiple_of(core * half, 128), half)]
    far = modded_ref[:, pl.ds(pl.multiple_of((1 - core) * half, 128), half)]
    keep_ref[:rank] = one * own_ref[:rank] + two * own_ref[rank:]
    keep_ref[rank:] = product(dlow, near)
    give_ref[:rank] = (one * other_ref[:rank] + two * other_ref[rank:]).astype(BF16)
    give_ref[rank:] = product(dlow, far).astype(BF16)


def piles(ints, got, modded, b_own, b_other):
    lines, half = b_own.shape
    rows = got.shape[2]
    return pl.pallas_call(
        pile_kernel,
        out_shape=[
            jax.ShapeDtypeStruct((lines, half), F32),
            jax.ShapeDtypeStruct((lines, half), BF16),
            jax.ShapeDtypeStruct((8, rows), F32),
        ],
        in_specs=[pl.BlockSpec(memory_space=SMEM)] + [pl.BlockSpec(memory_space=pltpu.VMEM)] * 4,
        compiler_params=params(),
        cost_estimate=cost(2 * lines * half * rows, 16 * lines * half),
    )(ints, got, modded, b_own, b_other)


def dm_kernel(order, after_ref, do_ref, dt_ref, dlow_ref, own_ref, other_ref, a_ref, out_ref, total_scr):
    step = pl.program_id(0)
    size = own_ref.shape[0]
    width = out_ref.shape[1]
    total = rows_by_rows(do_ref[...], own_ref[...]) + rows_by_rows(dt_ref[...], other_ref[...])
    total = total + product(dlow_ref[...], a_ref[...])
    total_scr[:, pl.ds(pl.multiple_of(step * size, 128), size)] = total.astype(BF16)

    @pl.when(step == pl.num_programs(0) - 1)
    def _():
        for start in range(0, width, 256):
            turn = places(start, 256, width, *order)
            out_ref[:, start : start + 256] = product(total_scr[...], turn).astype(BF16)


def dm_terms(order, after, d_own, d_other, dlow, own, other, a_order):
    rows, half = d_own.shape
    width = own.shape[0]
    rank = dlow.shape[1]
    step = 512
    cut = pl.BlockSpec((step, half), lambda i: (i, 0))
    return pl.pallas_call(
        functools.partial(dm_kernel, order),
        grid=(width // step,),
        out_shape=jax.ShapeDtypeStruct((rows, width), BF16),
        in_specs=[
            pl.BlockSpec(memory_space=pl.ANY),
            whole((rows, half)),
            whole((rows, half)),
            whole((rows, rank)),
            cut,
            cut,
            pl.BlockSpec((rank, step), lambda i: (0, i)),
        ],
        out_specs=whole((rows, width)),
        scratch_shapes=[pltpu.VMEM((rows, width), BF16)],
        compiler_params=params(),
        cost_estimate=cost(4 * rows * width * half, 4 * width * half + 2 * rows * width),
    )(after, d_own, d_other, dlow, own, other, a_order)


def token_kernel(ints_ref, one_ref, two_ref, three_ref, four_ref, x_ref, mod_ref, unit_ref, facts_ref, out_ref):
    total = one_ref[...].astype(F32) + two_ref[...].astype(F32)
    total = total + three_ref[...].astype(F32) + four_ref[...].astype(F32)
    normed, inverse = normalise(x_ref[...])
    first, _ = own_slot(ints_ref)
    coef = jnp.where(first, facts_ref[1:2, :1], facts_ref[2:3, :1])
    dn = total * (1.0 + pick(first, mod_ref, 1))
    mean_one = jnp.mean(dn, axis=-1, keepdims=True)
    mean_two = jnp.mean(dn * normed, axis=-1, keepdims=True)
    grad = coef * (unit_ref[...] + inverse * (dn - mean_one - normed * mean_two))
    out_ref[...] = grad.astype(BF16)


def token_gradient(ints, pieces, x_own, mod, unit, facts):
    rows, width = x_own.shape
    return pl.pallas_call(
        token_kernel,
        out_shape=jax.ShapeDtypeStruct((rows, width), BF16),
        in_specs=[pl.BlockSpec(memory_space=SMEM)] + [pl.BlockSpec(memory_space=pltpu.VMEM)] * 8,
        compiler_params=params(),
        cost_estimate=cost(20 * rows * width, 20 * rows * width),
    )(ints, *pieces, x_own, mod, unit, facts)


def per_device(
    tokens,
    targets,
    modulation,
    live_block_count,
    preferred_blocks,
    last_block_rows,
    up_rows,
    down_rows,
    factor_in,
    factor_out,
):
    width = tokens.shape[1]
    n_z, n_x, n_c, n_t = (lax.axis_size(a) for a in ("z", "x", "c", "t"))
    n_dp = n_z * n_x * n_c
    core = lax.axis_index("c")
    group = lax.axis_index("t")
    thin, hidden = up_rows.shape
    half = hidden // n_c
    rank = factor_in.shape[1]

    sent = down_rows.reshape(thin, n_c, half).transpose(1, 0, 2)
    sent = jnp.broadcast_to(sent[None], (n_x, n_c, thin, half)).reshape(n_x * n_c, thin, half)
    near = lax.all_to_all(sent, ("x", "c"), 0, 0, tiled=True)
    down_own = lax.all_gather(near.reshape(n_x * n_c * thin, half), "z", axis=0, tiled=True)

    up_rows, near = lax.optimization_barrier((up_rows, near))
    keep = lax.dynamic_slice_in_dim(up_rows, core * half, half, axis=1)
    got = lax.ppermute(lax.dynamic_slice_in_dim(up_rows, (1 - core) * half, half, axis=1), "c", SWAP)
    pair = jnp.where(core == 0, jnp.concatenate([keep, got], 0), jnp.concatenate([got, keep], 0))
    line = lax.all_gather(pair, "z", axis=0, tiled=True)

    ints = [preferred_blocks[0], live_block_count[0], last_block_rows[0, 0], last_block_rows[0, 1], group, core]
    ints = jnp.stack(ints).astype(jnp.int32)
    x_own = lax.dynamic_slice_in_dim(tokens, group * BLK, BLK, axis=0)
    t_own = lax.dynamic_slice_in_dim(targets, group * BLK, BLK, axis=0)
    mod = modulation.reshape(6, width)
    a_turned = factor_in.T
    modded, low, low_split = prepare(ints, tokens, mod, a_turned)

    modded_order, a_order = reorder((n_x, n_z, n_c * thin), modded, a_turned)
    blocks = after(spread(line, "x", n_x), [modded_order, a_order, low, low_split, x_own, t_own])
    up_own = blocks.reshape(width, half)
    up_other = lax.ppermute(up_own, "c", SWAP)
    down_other = lax.ppermute(down_own, "c", SWAP)

    pol_own, ref_own, slope_own = activate(False, ints, modded_order, low, up_own, factor_out)
    pol_other, ref_other, slope_other = activate(True, ints, modded_order, low, up_other, factor_out)
    part_pol = lower(pol_own, pol_other, down_own, down_other).reshape(CAP, BLK, width)
    got_pol = lax.all_to_all(part_pol, "t", 0, 0, tiled=True)
    part_ref = lower(ref_own, ref_other, down_own, down_other).reshape(CAP, BLK, width)

    unit, send = miss(ints, got_pol, part_ref, x_own, t_own, mod)
    got_dy = lax.all_to_all(send, "t", 0, 0, tiled=True)
    d_own, d_other, dlow_part, send = backward(
        ints, got_dy, unit, x_own, t_own, mod, down_own, down_other, factor_out, slope_own, slope_other
    )
    got_low = lax.all_to_all(send, "t", 0, 0, tiled=True)
    b_own, b_other = factor_terms(low_split, d_own, d_other)
    keep, give, facts = piles(ints, got_low, modded, b_own, b_other)
    losses = facts[0, :1]
    pile = (keep + lax.ppermute(give, "c", SWAP).astype(F32)).astype(BF16)

    chips = n_z * n_x
    pieces = lax.all_to_all(pile.reshape(chips, 2 * rank // chips, half), CHIPS, 0, 0, tiled=True)
    dm_part = dm_terms(
        (n_z, n_x, n_c * thin), pile, d_own, d_other, dlow_part, up_own, up_other, a_order
    ).reshape(CAP, BLK, width)
    turns = [[(i, (i + step) % n_t) for i in range(n_t)] for step in range(n_t)]
    chunks = [lax.dynamic_index_in_dim(dm_part, (group + step) % n_t, 0, False) for step in range(n_t)]
    chunks = [chunks[0]] + [lax.ppermute(chunks[step], "t", turns[step]) for step in range(1, n_t)]
    total = (jnp.sum(pieces.astype(F32), axis=0) / n_dp).astype(BF16)
    mine = spread(total, CHIPS, chips).reshape(2 * rank, half)
    grad_block = token_gradient(ints, chunks, x_own, mod, unit, facts)
    shares = [grad_block] + [lax.ppermute(grad_block, "t", turns[step]) for step in range(1, n_t)]
    shares = jnp.stack(shares)
    grad_tokens = jnp.concatenate(
        [lax.dynamic_index_in_dim(shares, (group - slot) % n_t, 0, False) for slot in range(n_t)], 0
    )
    theirs = lax.ppermute(mine, "c", SWAP)
    ends = jnp.concatenate([mine, theirs], 1)
    flipped = jnp.concatenate([theirs, mine], 1)
    ends = jnp.where(core == 0, ends, flipped).astype(F32)
    sum_b = ends[:rank]
    sum_a = ends[rank:].T
    return losses, grad_tokens, sum_a, sum_b


def solution(mesh):
    n_dp, n_t = mesh.devices.shape
    fine = Mesh(mesh.devices.reshape(n_dp // 8, 4, 2, n_t), ("z", "x", "c", "t"))
    return jax.shard_map(
        per_device,
        mesh=fine,
        in_specs=(
            P(DP, None),
            P(DP, None),
            P(DP, None, None),
            P(DP),
            P(DP),
            P(DP, None),
            P(DP, "t"),
            P(DP, "t"),
            P(),
            P(None, "t"),
        ),
        out_specs=(P(DP), P(DP, None), P(), P(None, "t")),
        check_vma=False,
    )
```

```python
import functools

import jax
import jax.numpy as jnp
from jax import lax
from jax.experimental import pallas as pl
from jax.experimental.pallas import tpu as pltpu
from jax.sharding import Mesh
from jax.sharding import PartitionSpec as P

BLK = 64
CAP = 4
EPS = 1e-06
BETA = 20.0
LOSS_SCALE = 4096.0
ROOT = 0.7978845608028654
CUBE = 0.044715
BF16 = jnp.bfloat16
F32 = jnp.float32
DP = ("z", "x", "c")
CHIPS = ("z", "x")
SWAP = [(0, 1), (1, 0)]
NOTE = 16
VMEM_LIMIT = 40 * 1024 * 1024
SMEM = pltpu.SMEM


def gelu(pre):
    th = jnp.tanh(ROOT * (pre + CUBE * pre * pre * pre))
    return 0.5 * pre * (1.0 + th)


def gelu_and_slope(pre):
    square = pre * pre
    th = jnp.tanh(ROOT * (pre + CUBE * pre * square))
    half = 0.5 * (1.0 + th)
    slope = half + 0.5 * pre * (1.0 - th * th) * (ROOT * (1.0 + 3.0 * CUBE * square))
    return pre * half, slope


def rows_by_rows(left, right):
    return lax.dot_general(left, right, (((1,), (1,)), ((), ())), preferred_element_type=F32)


def product(left, right):
    return jnp.dot(left, right, preferred_element_type=F32)


def spread(value, axes, n):
    return lax.all_to_all(jnp.broadcast_to(value[None], (n, *value.shape)), axes, 0, 0, tiled=True)


def normalise(rows):
    wide = rows.astype(F32)
    center = wide - jnp.mean(wide, axis=-1, keepdims=True)
    inverse = lax.rsqrt(jnp.mean(center * center, axis=-1, keepdims=True) + EPS)
    return center * inverse, inverse


def params():
    return pltpu.CompilerParams(vmem_limit_bytes=VMEM_LIMIT)


def cost(flops, moved, tanh=0):
    return pl.CostEstimate(flops=flops, bytes_accessed=moved, transcendentals=tanh)


def whole(shape):
    return pl.BlockSpec(shape, lambda *_: (0,) * len(shape))


def input_kernel(wins_ref, x_ref, mod_ref, a_ref, modded_ref, low_ref, split_ref):
    wins = wins_ref[0]
    for slot in range(CAP):
        rows = slice(slot * BLK, (slot + 1) * BLK)
        normed, _ = normalise(x_ref[rows])
        first = slot < wins
        shift = jnp.where(first, mod_ref[0:1].astype(F32), mod_ref[3:4].astype(F32))
        scale = 1.0 + jnp.where(first, mod_ref[1:2].astype(F32), mod_ref[4:5].astype(F32))
        modded_ref[rows] = (normed * scale + shift).astype(BF16)
    modded = modded_ref[...]
    low_ref[...] = rows_by_rows(modded, a_ref[...]).astype(BF16)
    turned = rows_by_rows(a_ref[...], modded)
    second = lax.broadcasted_iota(jnp.int32, turned.shape, 1) // BLK >= wins
    rank = turned.shape[0]
    split_ref[:rank] = jnp.where(second, 0.0, turned).astype(BF16)
    split_ref[rank:] = jnp.where(second, turned, 0.0).astype(BF16)


def prepare(wins, tokens, mod, a_turned):
    rows, width = tokens.shape
    rank = a_turned.shape[0]
    return pl.pallas_call(
        input_kernel,
        out_shape=[
            jax.ShapeDtypeStruct((rows, width), BF16),
            jax.ShapeDtypeStruct((rows, rank), BF16),
            jax.ShapeDtypeStruct((2 * rank, rows), BF16),
        ],
        in_specs=[pl.BlockSpec(memory_space=SMEM)] + [pl.BlockSpec(memory_space=pltpu.VMEM)] * 3,
        compiler_params=params(),
        cost_estimate=cost(4 * rows * width * rank, 4 * rows * width),
    )(wins, tokens, mod, a_turned)


def own_slot(ints_ref):
    wins, count, slot = ints_ref[0], ints_ref[1], ints_ref[4]
    first = slot < wins
    last = jnp.where(first, wins - 1, count - 1)
    tail = jnp.where(first, ints_ref[2], ints_ref[3])
    return first, jnp.where(slot < count, jnp.where(slot == last, tail, BLK), 0)


def pick(first, ref, line):
    return jnp.where(first, ref[line : line + 1].astype(F32), ref[line + 3 : line + 4].astype(F32))


def after_kernel(*refs):
    del refs


def after(value, others):
    return pl.pallas_call(
        after_kernel,
        out_shape=jax.ShapeDtypeStruct(value.shape, value.dtype),
        in_specs=[pl.BlockSpec(memory_space=pl.ANY)] * (1 + len(others)),
        out_specs=pl.BlockSpec(memory_space=pl.ANY),
        input_output_aliases={0: 0},
    )(value, *others)


def swapped(index, outer, inner, unit):
    first = sum((index >= k * inner * unit).astype(jnp.int32) for k in range(1, outer))
    rest = index - first * (inner * unit)
    second = sum((rest >= k * unit).astype(jnp.int32) for k in range(1, inner))
    return second * (outer * unit) + first * unit + rest - second * unit


def places(start, size, width, outer, inner, unit):
    column = swapped(lax.broadcasted_iota(jnp.int32, (1, size), 1) + start, outer, inner, unit)
    line = lax.broadcasted_iota(jnp.int32, (width, size), 0)
    return jnp.where(line == column, 1.0, 0.0).astype(BF16)


def reorder_kernel(order, modded_ref, a_ref, modded_out, a_out):
    size = modded_out.shape[1]
    turn = places(pl.program_id(0) * size, size, modded_ref.shape[1], *order)
    modded_out[...] = product(modded_ref[...], turn).astype(BF16)
    a_out[...] = product(a_ref[...], turn).astype(BF16)


def reorder(order, modded, a_turned):
    rows, width = modded.shape
    rank = a_turned.shape[0]
    step = 256
    cuts = [pl.BlockSpec((rows, step), lambda i: (0, i)), pl.BlockSpec((rank, step), lambda i: (0, i))]
    return pl.pallas_call(
        functools.partial(reorder_kernel, order),
        grid=(width // step,),
        out_shape=[jax.ShapeDtypeStruct((rows, width), BF16), jax.ShapeDtypeStruct((rank, width), BF16)],
        in_specs=[whole((rows, width)), whole((rank, width))],
        out_specs=cuts,
        compiler_params=params(),
        cost_estimate=cost(2 * (rows + rank) * width * width, 8 * rows * width),
    )(modded, a_turned)


def half_of(core, step, half, size):
    return pl.ds(pl.multiple_of(core * half + step * size, 128), size)


def up_kernel(far, ints_ref, modded_ref, low_ref, up_ref, b_ref, pol_ref, ref_ref, slope_ref):
    core = 1 - ints_ref[5] if far else ints_ref[5]
    size = up_ref.shape[1]
    cut = half_of(core, pl.program_id(0), size * pl.num_programs(0), size)
    pre_ref = product(modded_ref[...], up_ref[...])
    pre_pol = pre_ref + product(low_ref[...], b_ref[:, cut])
    act, slope = gelu_and_slope(pre_pol)
    pol_ref[...] = act.astype(BF16)
    slope_ref[...] = slope.astype(BF16)
    ref_ref[...] = gelu(pre_ref).astype(BF16)


def activate(far, ints, modded, low, weights, factor):
    rows, width = modded.shape
    rank = factor.shape[0]
    half = factor.shape[1] // 2
    step = 256
    cut = pl.BlockSpec((rows, step), lambda i: (0, i))
    return pl.pallas_call(
        functools.partial(up_kernel, far),
        grid=(half // step,),
        out_shape=[
            jax.ShapeDtypeStruct((rows, half), BF16),
            jax.ShapeDtypeStruct((rows, half), BF16),
            jax.ShapeDtypeStruct((rows, half), BF16),
        ],
        in_specs=[
            pl.BlockSpec(memory_space=SMEM),
            whole((rows, width)),
            whole((rows, rank)),
            pl.BlockSpec((width, step), lambda i: (0, i)),
            whole(factor.shape),
        ],
        out_specs=[cut, cut, cut],
        compiler_params=params(),
        cost_estimate=cost(2 * rows * width * half, 2 * width * half + 10 * rows * half, 2 * rows * half),
    )(ints, modded, low, weights, factor)


def down_kernel(left_ref, right_ref, own_ref, other_ref, out_ref):
    total = rows_by_rows(left_ref[...], own_ref[...]) + rows_by_rows(right_ref[...], other_ref[...])
    out_ref[...] = total.astype(BF16)


def lower(left, right, own, other):
    rows, half = left.shape
    width = own.shape[0]
    step = 512
    cut = pl.BlockSpec((step, half), lambda i: (i, 0))
    return pl.pallas_call(
        down_kernel,
        grid=(width // step,),
        out_shape=jax.ShapeDtypeStruct((rows, width), BF16),
        in_specs=[whole((rows, half)), whole((rows, half)), cut, cut],
        out_specs=pl.BlockSpec((rows, step), lambda i: (0, i)),
        compiler_params=params(),
        cost_estimate=cost(4 * rows * width * half, 4 * width * half + 2 * rows * width),
    )(left, right, own, other)


def miss_kernel(ints_ref, got_ref, ref_ref, x_ref, t_ref, mod_ref, unit_ref, send_ref):
    first, live = own_slot(ints_ref)
    total = jnp.sum(got_ref[...].astype(F32), axis=0)
    gate = pick(first, mod_ref, 2)
    unit = 2.0 * (x_ref[...].astype(F32) - t_ref[...].astype(F32) + gate * total)
    unit = jnp.where(lax.broadcasted_iota(jnp.int32, unit.shape, 0) < live, unit, 0.0)
    unit_ref[...] = unit
    dy = (gate * unit).astype(BF16)
    for peer in range(send_ref.shape[0]):
        send_ref[peer, :BLK] = dy
        send_ref[peer, BLK:] = ref_ref[peer]


def miss(ints, got, part_ref, x_own, t_own, mod):
    groups, rows, width = got.shape
    return pl.pallas_call(
        miss_kernel,
        out_shape=[
            jax.ShapeDtypeStruct((rows, width), F32),
            jax.ShapeDtypeStruct((groups, 2 * rows, width), BF16),
        ],
        in_specs=[pl.BlockSpec(memory_space=SMEM)] + [pl.BlockSpec(memory_space=pltpu.VMEM)] * 5,
        compiler_params=params(),
        cost_estimate=cost(20 * rows * width, 8 * groups * rows * width),
    )(ints, got, part_ref, x_own, t_own, mod)


def back_kernel(
    ints_ref, got_ref, unit_ref, x_ref, t_ref, mod_ref, own_ref, other_ref, b_ref, so_ref, st_ref,
    do_ref, dt_ref, dlow_ref, send_ref, turned_scr, straight_scr,
):
    step = pl.program_id(0)
    core = ints_ref[5]
    width = got_ref.shape[2]
    size = so_ref.shape[1]
    half = size * pl.num_programs(0)
    b_own = b_ref[:, half_of(core, step, half, size)]
    b_other = b_ref[:, half_of(1 - core, step, half, size)]
    dy = got_ref[:, :BLK].reshape(CAP * BLK, width)
    d_own = (product(dy, own_ref[...]) * so_ref[...].astype(F32)).astype(BF16)
    d_other = (product(dy, other_ref[...]) * st_ref[...].astype(F32)).astype(BF16)
    do_ref[...] = d_own
    dt_ref[...] = d_other
    turned = rows_by_rows(b_own, d_own) + rows_by_rows(b_other, d_other)
    straight = rows_by_rows(d_own, b_own) + rows_by_rows(d_other, b_other)

    @pl.when(step == 0)
    def _():
        turned_scr[...] = turned
        straight_scr[...] = straight

    @pl.when(step > 0)
    def _():
        turned_scr[...] += turned
        straight_scr[...] += straight

    @pl.when(step == pl.num_programs(0) - 1)
    def _():
        rank = turned_scr.shape[0]
        dlow_ref[...] = straight_scr[...].astype(BF16)
        first, live = own_slot(ints_ref)
        base = x_ref[...].astype(F32) - t_ref[...].astype(F32)
        miss_ref = base + pick(first, mod_ref, 2) * jnp.sum(got_ref[:, BLK:].astype(F32), axis=0)
        miss_ref = jnp.where(lax.broadcasted_iota(jnp.int32, miss_ref.shape, 0) < live, miss_ref, 0.0)
        miss_pol = 0.5 * unit_ref[...]
        parts = jnp.sum((miss_pol - miss_ref) * (miss_pol + miss_ref), axis=1, keepdims=True)
        excess = jnp.broadcast_to(jnp.sum(parts, axis=0, keepdims=True), (NOTE, CAP * BLK))
        high = excess.astype(BF16)
        rest = excess - high.astype(F32)
        middle = rest.astype(BF16)
        lowest = rest - middle.astype(F32)
        line = lax.broadcasted_iota(jnp.int32, excess.shape, 0)
        note = jnp.where(line == 0, high.astype(F32), jnp.where(line == 1, middle.astype(F32), lowest)).astype(BF16)
        total = turned_scr[...].astype(BF16)
        for peer in range(send_ref.shape[0]):
            send_ref[peer, :rank] = total
            send_ref[peer, rank:] = note


def backward(ints, got, unit, x_own, t_own, mod, own, other, factor, s_own, s_other):
    groups, _, width = got.shape
    half = s_own.shape[1]
    rank = factor.shape[0]
    rows = CAP * BLK
    step = 256
    weight = pl.BlockSpec((width, step), lambda i: (0, i))
    cut = pl.BlockSpec((rows, step), lambda i: (0, i))
    block = whole((BLK, width))
    return pl.pallas_call(
        back_kernel,
        grid=(half // step,),
        out_shape=[
            jax.ShapeDtypeStruct((rows, half), BF16),
            jax.ShapeDtypeStruct((rows, half), BF16),
            jax.ShapeDtypeStruct((rows, rank), BF16),
            jax.ShapeDtypeStruct((groups, rank + NOTE, rows), BF16),
        ],
        in_specs=[
            pl.BlockSpec(memory_space=SMEM), whole(got.shape), block, block, block, whole(mod.shape),
            weight, weight, whole(factor.shape), cut, cut,
        ],
        out_specs=[cut, cut, whole((rows, rank)), whole((groups, rank + NOTE, rows))],
        scratch_shapes=[pltpu.VMEM((rank, rows), F32), pltpu.VMEM((rows, rank), F32)],
        compiler_params=params(),
        cost_estimate=cost(4 * rows * width * half, 4 * width * half + 12 * rows * half),
    )(ints, got, unit, x_own, t_own, mod, own, other, factor, s_own, s_other)


def pile_kernel(ints_ref, got_ref, modded_ref, split_ref, do_ref, dt_ref, keep_ref, give_ref, facts_ref):
    wins = ints_ref[0]
    core = ints_ref[5]
    groups, lines, rows = got_ref.shape
    rank = lines - NOTE
    half = do_ref.shape[1]
    gap_first = jnp.zeros((1, rows), F32)
    gap_second = jnp.zeros((1, rows), F32)
    for slot in range(groups):
        note = got_ref[slot, rank:].astype(F32)
        excess = note[0:1] + note[1:2] + note[2:3]
        gap_first += jnp.where(slot < wins, excess, 0.0)
        gap_second += jnp.where(slot < wins, 0.0, excess)
    width = modded_ref.shape[1]
    rows_first = (wins - 1) * BLK + ints_ref[2]
    rows_second = (ints_ref[1] - wins - 1) * BLK + ints_ref[3]
    scale_first = 1.0 / (width * jnp.full((1, rows), rows_first, jnp.int32).astype(F32))
    scale_second = 1.0 / (width * jnp.full((1, rows), rows_second, jnp.int32).astype(F32))
    inside = -BETA * (gap_first * scale_first - gap_second * scale_second)
    losses = jnp.maximum(-inside, 0.0) + jnp.log1p(jnp.exp(-jnp.abs(inside)))
    weight = BETA * LOSS_SCALE * jax.nn.sigmoid(-inside)
    first = weight * scale_first
    second = -weight * scale_second
    line = lax.broadcasted_iota(jnp.int32, facts_ref.shape, 0)
    facts_ref[...] = jnp.where(line == 0, losses, jnp.where(line == 1, first, second))
    slot = lax.broadcasted_iota(jnp.int32, (1, rows), 1) // BLK
    total = jnp.sum(got_ref[:, :rank].astype(F32), axis=0)
    dlow = (total * jnp.where(slot < wins, first, second)).astype(BF16)
    one = first[:, :1]
    two = second[:, :1]
    near = modded_ref[:, pl.ds(pl.multiple_of(core * half, 128), half)]
    far = modded_ref[:, pl.ds(pl.multiple_of((1 - core) * half, 128), half)]
    b_own = product(split_ref[...], do_ref[...])
    b_other = product(split_ref[...], dt_ref[...])
    keep_ref[:rank] = one * b_own[:rank] + two * b_own[rank:]
    keep_ref[rank:] = product(dlow, near)
    give_ref[:rank] = (one * b_other[:rank] + two * b_other[rank:]).astype(BF16)
    give_ref[rank:] = product(dlow, far).astype(BF16)


def piles(ints, got, modded, split, d_own, d_other):
    lines = split.shape[0]
    half = d_own.shape[1]
    rows = got.shape[2]
    return pl.pallas_call(
        pile_kernel,
        out_shape=[
            jax.ShapeDtypeStruct((lines, half), F32),
            jax.ShapeDtypeStruct((lines, half), BF16),
            jax.ShapeDtypeStruct((8, rows), F32),
        ],
        in_specs=[pl.BlockSpec(memory_space=SMEM)] + [pl.BlockSpec(memory_space=pltpu.VMEM)] * 5,
        compiler_params=params(),
        cost_estimate=cost(6 * lines * half * rows, 16 * lines * half),
    )(ints, got, modded, split, d_own, d_other)


def dm_kernel(order, after_ref, do_ref, dt_ref, dlow_ref, own_ref, other_ref, a_ref, out_ref, total_scr):
    step = pl.program_id(0)
    size = own_ref.shape[0]
    width = out_ref.shape[1]
    total = rows_by_rows(do_ref[...], own_ref[...]) + rows_by_rows(dt_ref[...], other_ref[...])
    total = total + product(dlow_ref[...], a_ref[...])
    total_scr[:, pl.ds(pl.multiple_of(step * size, 128), size)] = total.astype(BF16)

    @pl.when(step == pl.num_programs(0) - 1)
    def _():
        for start in range(0, width, 256):
            turn = places(start, 256, width, *order)
            out_ref[:, start : start + 256] = product(total_scr[...], turn).astype(BF16)


def dm_terms(order, after, d_own, d_other, dlow, own, other, a_order):
    rows, half = d_own.shape
    width = own.shape[0]
    rank = dlow.shape[1]
    step = 512
    cut = pl.BlockSpec((step, half), lambda i: (i, 0))
    return pl.pallas_call(
        functools.partial(dm_kernel, order),
        grid=(width // step,),
        out_shape=jax.ShapeDtypeStruct((rows, width), BF16),
        in_specs=[
            pl.BlockSpec(memory_space=pl.ANY),
            whole((rows, half)),
            whole((rows, half)),
            whole((rows, rank)),
            cut,
            cut,
            pl.BlockSpec((rank, step), lambda i: (0, i)),
        ],
        out_specs=whole((rows, width)),
        scratch_shapes=[pltpu.VMEM((rows, width), BF16)],
        compiler_params=params(),
        cost_estimate=cost(4 * rows * width * half, 4 * width * half + 2 * rows * width),
    )(after, d_own, d_other, dlow, own, other, a_order)


def token_kernel(ints_ref, one_ref, two_ref, three_ref, four_ref, x_ref, mod_ref, unit_ref, facts_ref, out_ref):
    total = one_ref[...].astype(F32) + two_ref[...].astype(F32)
    total = total + three_ref[...].astype(F32) + four_ref[...].astype(F32)
    normed, inverse = normalise(x_ref[...])
    first, _ = own_slot(ints_ref)
    coef = jnp.where(first, facts_ref[1:2, :1], facts_ref[2:3, :1])
    dn = total * (1.0 + pick(first, mod_ref, 1))
    mean_one = jnp.mean(dn, axis=-1, keepdims=True)
    mean_two = jnp.mean(dn * normed, axis=-1, keepdims=True)
    grad = coef * (unit_ref[...] + inverse * (dn - mean_one - normed * mean_two))
    out_ref[...] = grad.astype(BF16)


def token_gradient(ints, pieces, x_own, mod, unit, facts):
    rows, width = x_own.shape
    return pl.pallas_call(
        token_kernel,
        out_shape=jax.ShapeDtypeStruct((rows, width), BF16),
        in_specs=[pl.BlockSpec(memory_space=SMEM)] + [pl.BlockSpec(memory_space=pltpu.VMEM)] * 8,
        compiler_params=params(),
        cost_estimate=cost(20 * rows * width, 20 * rows * width),
    )(ints, *pieces, x_own, mod, unit, facts)


def per_device(
    tokens,
    targets,
    modulation,
    live_block_count,
    preferred_blocks,
    last_block_rows,
    up_rows,
    down_rows,
    factor_in,
    factor_out,
):
    width = tokens.shape[1]
    n_z, n_x, n_c, n_t = (lax.axis_size(a) for a in ("z", "x", "c", "t"))
    n_dp = n_z * n_x * n_c
    core = lax.axis_index("c")
    group = lax.axis_index("t")
    thin, hidden = up_rows.shape
    half = hidden // n_c
    rank = factor_in.shape[1]

    sent = down_rows.reshape(thin, n_c, half).transpose(1, 0, 2)
    sent = jnp.broadcast_to(sent[None], (n_x, n_c, thin, half)).reshape(n_x * n_c, thin, half)
    near = lax.all_to_all(sent, ("x", "c"), 0, 0, tiled=True)
    down_own = lax.all_gather(near.reshape(n_x * n_c * thin, half), "z", axis=0, tiled=True)

    up_rows, near = lax.optimization_barrier((up_rows, near))
    keep = lax.dynamic_slice_in_dim(up_rows, core * half, half, axis=1)
    got = lax.ppermute(lax.dynamic_slice_in_dim(up_rows, (1 - core) * half, half, axis=1), "c", SWAP)
    pair = jnp.where(core == 0, jnp.concatenate([keep, got], 0), jnp.concatenate([got, keep], 0))
    line = lax.all_gather(pair, "z", axis=0, tiled=True)

    ints = [preferred_blocks[0], live_block_count[0], last_block_rows[0, 0], last_block_rows[0, 1], group, core]
    ints = jnp.stack(ints).astype(jnp.int32)
    x_own = lax.dynamic_slice_in_dim(tokens, group * BLK, BLK, axis=0)
    t_own = lax.dynamic_slice_in_dim(targets, group * BLK, BLK, axis=0)
    mod = modulation.reshape(6, width)
    a_turned = factor_in.T
    modded, low, low_split = prepare(ints, tokens, mod, a_turned)

    modded_order, a_order = reorder((n_x, n_z, n_c * thin), modded, a_turned)
    blocks = after(spread(line, "x", n_x), [modded_order, a_order, low, low_split, x_own, t_own])
    up_own = blocks.reshape(width, half)
    up_other = lax.ppermute(up_own, "c", SWAP)
    down_other = lax.ppermute(down_own, "c", SWAP)

    pol_own, ref_own, slope_own = activate(False, ints, modded_order, low, up_own, factor_out)
    pol_other, ref_other, slope_other = activate(True, ints, modded_order, low, up_other, factor_out)
    part_pol = lower(pol_own, pol_other, down_own, down_other).reshape(CAP, BLK, width)
    got_pol = lax.all_to_all(part_pol, "t", 0, 0, tiled=True)
    part_ref = lower(ref_own, ref_other, down_own, down_other).reshape(CAP, BLK, width)

    unit, send = miss(ints, got_pol, part_ref, x_own, t_own, mod)
    got_dy = lax.all_to_all(send, "t", 0, 0, tiled=True)
    d_own, d_other, dlow_part, send = backward(
        ints, got_dy, unit, x_own, t_own, mod, down_own, down_other, factor_out, slope_own, slope_other
    )
    got_low = lax.all_to_all(send, "t", 0, 0, tiled=True)
    keep, give, facts = piles(ints, got_low, modded, low_split, d_own, d_other)
    losses = facts[0, :1]
    pile = (keep + lax.ppermute(give, "c", SWAP).astype(F32)).astype(BF16)

    chips = n_z * n_x
    pieces = lax.all_to_all(pile.reshape(chips, 2 * rank // chips, half), CHIPS, 0, 0, tiled=True)
    dm_part = dm_terms(
        (n_z, n_x, n_c * thin), pile, d_own, d_other, dlow_part, up_own, up_other, a_order
    ).reshape(CAP, BLK, width)
    turns = [[(i, (i + step) % n_t) for i in range(n_t)] for step in range(n_t)]
    chunks = [lax.dynamic_index_in_dim(dm_part, (group + step) % n_t, 0, False) for step in range(n_t)]
    chunks = [chunks[0]] + [lax.ppermute(chunks[step], "t", turns[step]) for step in range(1, n_t)]
    total = (jnp.sum(pieces.astype(F32), axis=0) / n_dp).astype(BF16)
    mine = spread(total, CHIPS, chips).reshape(2 * rank, half)
    grad_block = token_gradient(ints, chunks, x_own, mod, unit, facts)
    shares = [grad_block] + [lax.ppermute(grad_block, "t", turns[step]) for step in range(1, n_t)]
    shares = jnp.stack(shares)
    grad_tokens = jnp.concatenate(
        [lax.dynamic_index_in_dim(shares, (group - slot) % n_t, 0, False) for slot in range(n_t)], 0
    )
    theirs = lax.ppermute(mine, "c", SWAP)
    ends = jnp.concatenate([mine, theirs], 1)
    flipped = jnp.concatenate([theirs, mine], 1)
    ends = jnp.where(core == 0, ends, flipped).astype(F32)
    sum_b = ends[:rank]
    sum_a = ends[rank:].T
    return losses, grad_tokens, sum_a, sum_b


def solution(mesh):
    n_dp, n_t = mesh.devices.shape
    fine = Mesh(mesh.devices.reshape(n_dp // 8, 4, 2, n_t), ("z", "x", "c", "t"))
    return jax.shard_map(
        per_device,
        mesh=fine,
        in_specs=(
            P(DP, None),
            P(DP, None),
            P(DP, None, None),
            P(DP),
            P(DP),
            P(DP, None),
            P(DP, "t"),
            P(DP, "t"),
            P(),
            P(None, "t"),
        ),
        out_specs=(P(DP), P(DP, None), P(), P(None, "t")),
        check_vma=False,
    )
```

```python
import functools

import jax
import jax.numpy as jnp
from jax import lax
from jax.experimental import pallas as pl
from jax.experimental.pallas import tpu as pltpu
from jax.sharding import Mesh
from jax.sharding import PartitionSpec as P

BLK = 64
CAP = 4
EPS = 1e-06
BETA = 20.0
LOSS_SCALE = 4096.0
ROOT = 0.7978845608028654
CUBE = 0.044715
BF16 = jnp.bfloat16
F32 = jnp.float32
DP = ("z", "x", "c")
CHIPS = ("z", "x")
SWAP = [(0, 1), (1, 0)]
NOTE = 16
VMEM_LIMIT = 40 * 1024 * 1024
SMEM = pltpu.SMEM


def gelu(pre):
    th = jnp.tanh(ROOT * (pre + CUBE * pre * pre * pre))
    return 0.5 * pre * (1.0 + th)


def gelu_and_slope(pre):
    square = pre * pre
    th = jnp.tanh(ROOT * (pre + CUBE * pre * square))
    half = 0.5 * (1.0 + th)
    slope = half + 0.5 * pre * (1.0 - th * th) * (ROOT * (1.0 + 3.0 * CUBE * square))
    return pre * half, slope


def rows_by_rows(left, right):
    return lax.dot_general(left, right, (((1,), (1,)), ((), ())), preferred_element_type=F32)


def product(left, right):
    return jnp.dot(left, right, preferred_element_type=F32)


def spread(value, axes, n):
    return lax.all_to_all(jnp.broadcast_to(value[None], (n, *value.shape)), axes, 0, 0, tiled=True)


def normalise(rows):
    wide = rows.astype(F32)
    center = wide - jnp.mean(wide, axis=-1, keepdims=True)
    inverse = lax.rsqrt(jnp.mean(center * center, axis=-1, keepdims=True) + EPS)
    return center * inverse, inverse


def params():
    return pltpu.CompilerParams(vmem_limit_bytes=VMEM_LIMIT)


def cost(flops, moved, tanh=0):
    return pl.CostEstimate(flops=flops, bytes_accessed=moved, transcendentals=tanh)


def whole(shape):
    return pl.BlockSpec(shape, lambda *_: (0,) * len(shape))


def input_kernel(wins_ref, x_ref, mod_ref, a_ref, modded_ref, low_ref, split_ref):
    wins = wins_ref[0]
    for slot in range(CAP):
        rows = slice(slot * BLK, (slot + 1) * BLK)
        normed, _ = normalise(x_ref[rows])
        first = slot < wins
        shift = jnp.where(first, mod_ref[0:1].astype(F32), mod_ref[3:4].astype(F32))
        scale = 1.0 + jnp.where(first, mod_ref[1:2].astype(F32), mod_ref[4:5].astype(F32))
        modded_ref[rows] = (normed * scale + shift).astype(BF16)
    modded = modded_ref[...]
    low_ref[...] = rows_by_rows(modded, a_ref[...]).astype(BF16)
    turned = rows_by_rows(a_ref[...], modded)
    second = lax.broadcasted_iota(jnp.int32, turned.shape, 1) // BLK >= wins
    rank = turned.shape[0]
    split_ref[:rank] = jnp.where(second, 0.0, turned).astype(BF16)
    split_ref[rank:] = jnp.where(second, turned, 0.0).astype(BF16)


def prepare(wins, tokens, mod, a_turned):
    rows, width = tokens.shape
    rank = a_turned.shape[0]
    return pl.pallas_call(
        input_kernel,
        out_shape=[
            jax.ShapeDtypeStruct((rows, width), BF16),
            jax.ShapeDtypeStruct((rows, rank), BF16),
            jax.ShapeDtypeStruct((2 * rank, rows), BF16),
        ],
        in_specs=[pl.BlockSpec(memory_space=SMEM)] + [pl.BlockSpec(memory_space=pltpu.VMEM)] * 3,
        compiler_params=params(),
        cost_estimate=cost(4 * rows * width * rank, 4 * rows * width),
    )(wins, tokens, mod, a_turned)


def own_slot(ints_ref):
    wins, count, slot = ints_ref[0], ints_ref[1], ints_ref[4]
    first = slot < wins
    last = jnp.where(first, wins - 1, count - 1)
    tail = jnp.where(first, ints_ref[2], ints_ref[3])
    return first, jnp.where(slot < count, jnp.where(slot == last, tail, BLK), 0)


def pick(first, ref, line):
    return jnp.where(first, ref[line : line + 1].astype(F32), ref[line + 3 : line + 4].astype(F32))


def after_kernel(*refs):
    del refs


def after(value, others):
    return pl.pallas_call(
        after_kernel,
        out_shape=jax.ShapeDtypeStruct(value.shape, value.dtype),
        in_specs=[pl.BlockSpec(memory_space=pl.ANY)] * (1 + len(others)),
        out_specs=pl.BlockSpec(memory_space=pl.ANY),
        input_output_aliases={0: 0},
    )(value, *others)


def half_of(core, step, half, size):
    return pl.ds(pl.multiple_of(core * half + step * size, 128), size)


def up_kernel(far, ints_ref, modded_ref, low_ref, up_ref, b_ref, pol_ref, ref_ref, slope_ref):
    core = 1 - ints_ref[5] if far else ints_ref[5]
    size = up_ref.shape[1]
    cut = half_of(core, pl.program_id(0), size * pl.num_programs(0), size)
    pre_ref = product(modded_ref[...], up_ref[...])
    pre_pol = pre_ref + product(low_ref[...], b_ref[:, cut])
    act, slope = gelu_and_slope(pre_pol)
    pol_ref[...] = act.astype(BF16)
    slope_ref[...] = slope.astype(BF16)
    ref_ref[...] = gelu(pre_ref).astype(BF16)


def activate(far, ints, modded, low, weights, factor):
    rows, width = modded.shape
    rank = factor.shape[0]
    half = factor.shape[1] // 2
    step = 256
    cut = pl.BlockSpec((rows, step), lambda i: (0, i))
    return pl.pallas_call(
        functools.partial(up_kernel, far),
        grid=(half // step,),
        out_shape=[
            jax.ShapeDtypeStruct((rows, half), BF16),
            jax.ShapeDtypeStruct((rows, half), BF16),
            jax.ShapeDtypeStruct((rows, half), BF16),
        ],
        in_specs=[
            pl.BlockSpec(memory_space=SMEM),
            whole((rows, width)),
            whole((rows, rank)),
            pl.BlockSpec((width, step), lambda i: (0, i)),
            whole(factor.shape),
        ],
        out_specs=[cut, cut, cut],
        compiler_params=params(),
        cost_estimate=cost(2 * rows * width * half, 2 * width * half + 10 * rows * half, 2 * rows * half),
    )(ints, modded, low, weights, factor)


def down_kernel(left_ref, right_ref, own_ref, other_ref, out_ref):
    total = rows_by_rows(left_ref[...], own_ref[...]) + rows_by_rows(right_ref[...], other_ref[...])
    out_ref[...] = total.astype(BF16)


def lower(left, right, own, other):
    rows, half = left.shape
    width = own.shape[0]
    step = 512
    cut = pl.BlockSpec((step, half), lambda i: (i, 0))
    return pl.pallas_call(
        down_kernel,
        grid=(width // step,),
        out_shape=jax.ShapeDtypeStruct((rows, width), BF16),
        in_specs=[whole((rows, half)), whole((rows, half)), cut, cut],
        out_specs=pl.BlockSpec((rows, step), lambda i: (0, i)),
        compiler_params=params(),
        cost_estimate=cost(4 * rows * width * half, 4 * width * half + 2 * rows * width),
    )(left, right, own, other)


def miss_kernel(ints_ref, got_ref, ref_ref, x_ref, t_ref, mod_ref, unit_ref, send_ref):
    first, live = own_slot(ints_ref)
    total = jnp.sum(got_ref[...].astype(F32), axis=0)
    gate = pick(first, mod_ref, 2)
    unit = 2.0 * (x_ref[...].astype(F32) - t_ref[...].astype(F32) + gate * total)
    unit = jnp.where(lax.broadcasted_iota(jnp.int32, unit.shape, 0) < live, unit, 0.0)
    unit_ref[...] = unit
    dy = (gate * unit).astype(BF16)
    for peer in range(send_ref.shape[0]):
        send_ref[peer, :BLK] = dy
        send_ref[peer, BLK:] = ref_ref[peer]


def miss(ints, got, part_ref, x_own, t_own, mod):
    groups, rows, width = got.shape
    return pl.pallas_call(
        miss_kernel,
        out_shape=[
            jax.ShapeDtypeStruct((rows, width), F32),
            jax.ShapeDtypeStruct((groups, 2 * rows, width), BF16),
        ],
        in_specs=[pl.BlockSpec(memory_space=SMEM)] + [pl.BlockSpec(memory_space=pltpu.VMEM)] * 5,
        compiler_params=params(),
        cost_estimate=cost(20 * rows * width, 8 * groups * rows * width),
    )(ints, got, part_ref, x_own, t_own, mod)


def back_kernel(
    ints_ref, got_ref, unit_ref, x_ref, t_ref, mod_ref, own_ref, other_ref, b_ref, so_ref, st_ref,
    do_ref, dt_ref, dlow_ref, send_ref, turned_scr, straight_scr,
):
    step = pl.program_id(0)
    core = ints_ref[5]
    width = got_ref.shape[2]
    size = so_ref.shape[1]
    half = size * pl.num_programs(0)
    b_own = b_ref[:, half_of(core, step, half, size)]
    b_other = b_ref[:, half_of(1 - core, step, half, size)]
    dy = got_ref[:, :BLK].reshape(CAP * BLK, width)
    d_own = (product(dy, own_ref[...]) * so_ref[...].astype(F32)).astype(BF16)
    d_other = (product(dy, other_ref[...]) * st_ref[...].astype(F32)).astype(BF16)
    do_ref[...] = d_own
    dt_ref[...] = d_other
    turned = rows_by_rows(b_own, d_own) + rows_by_rows(b_other, d_other)
    straight = rows_by_rows(d_own, b_own) + rows_by_rows(d_other, b_other)

    @pl.when(step == 0)
    def _():
        turned_scr[...] = turned
        straight_scr[...] = straight

    @pl.when(step > 0)
    def _():
        turned_scr[...] += turned
        straight_scr[...] += straight

    @pl.when(step == pl.num_programs(0) - 1)
    def _():
        rank = turned_scr.shape[0]
        dlow_ref[...] = straight_scr[...].astype(BF16)
        first, live = own_slot(ints_ref)
        base = x_ref[...].astype(F32) - t_ref[...].astype(F32)
        miss_ref = base + pick(first, mod_ref, 2) * jnp.sum(got_ref[:, BLK:].astype(F32), axis=0)
        miss_ref = jnp.where(lax.broadcasted_iota(jnp.int32, miss_ref.shape, 0) < live, miss_ref, 0.0)
        miss_pol = 0.5 * unit_ref[...]
        parts = jnp.sum((miss_pol - miss_ref) * (miss_pol + miss_ref), axis=1, keepdims=True)
        excess = jnp.broadcast_to(jnp.sum(parts, axis=0, keepdims=True), (NOTE, CAP * BLK))
        high = excess.astype(BF16)
        rest = excess - high.astype(F32)
        middle = rest.astype(BF16)
        lowest = rest - middle.astype(F32)
        line = lax.broadcasted_iota(jnp.int32, excess.shape, 0)
        note = jnp.where(line == 0, high.astype(F32), jnp.where(line == 1, middle.astype(F32), lowest)).astype(BF16)
        total = turned_scr[...].astype(BF16)
        for peer in range(send_ref.shape[0]):
            send_ref[peer, :rank] = total
            send_ref[peer, rank:] = note


def backward(ints, got, unit, x_own, t_own, mod, own, other, factor, s_own, s_other):
    groups, _, width = got.shape
    half = s_own.shape[1]
    rank = factor.shape[0]
    rows = CAP * BLK
    step = 256
    weight = pl.BlockSpec((width, step), lambda i: (0, i))
    cut = pl.BlockSpec((rows, step), lambda i: (0, i))
    block = whole((BLK, width))
    return pl.pallas_call(
        back_kernel,
        grid=(half // step,),
        out_shape=[
            jax.ShapeDtypeStruct((rows, half), BF16),
            jax.ShapeDtypeStruct((rows, half), BF16),
            jax.ShapeDtypeStruct((rows, rank), BF16),
            jax.ShapeDtypeStruct((groups, rank + NOTE, rows), BF16),
        ],
        in_specs=[
            pl.BlockSpec(memory_space=SMEM), whole(got.shape), block, block, block, whole(mod.shape),
            weight, weight, whole(factor.shape), cut, cut,
        ],
        out_specs=[cut, cut, whole((rows, rank)), whole((groups, rank + NOTE, rows))],
        scratch_shapes=[pltpu.VMEM((rank, rows), F32), pltpu.VMEM((rows, rank), F32)],
        compiler_params=params(),
        cost_estimate=cost(4 * rows * width * half, 4 * width * half + 12 * rows * half),
    )(ints, got, unit, x_own, t_own, mod, own, other, factor, s_own, s_other)


def pile_kernel(ints_ref, got_ref, modded_ref, split_ref, do_ref, dt_ref, keep_ref, give_ref, facts_ref):
    wins = ints_ref[0]
    core = ints_ref[5]
    groups, lines, rows = got_ref.shape
    rank = lines - NOTE
    half = do_ref.shape[1]
    gap_first = jnp.zeros((1, rows), F32)
    gap_second = jnp.zeros((1, rows), F32)
    for slot in range(groups):
        note = got_ref[slot, rank:].astype(F32)
        excess = note[0:1] + note[1:2] + note[2:3]
        gap_first += jnp.where(slot < wins, excess, 0.0)
        gap_second += jnp.where(slot < wins, 0.0, excess)
    width = modded_ref.shape[1]
    rows_first = (wins - 1) * BLK + ints_ref[2]
    rows_second = (ints_ref[1] - wins - 1) * BLK + ints_ref[3]
    scale_first = 1.0 / (width * jnp.full((1, rows), rows_first, jnp.int32).astype(F32))
    scale_second = 1.0 / (width * jnp.full((1, rows), rows_second, jnp.int32).astype(F32))
    inside = -BETA * (gap_first * scale_first - gap_second * scale_second)
    losses = jnp.maximum(-inside, 0.0) + jnp.log1p(jnp.exp(-jnp.abs(inside)))
    weight = BETA * LOSS_SCALE * jax.nn.sigmoid(-inside)
    first = weight * scale_first
    second = -weight * scale_second
    line = lax.broadcasted_iota(jnp.int32, facts_ref.shape, 0)
    facts_ref[...] = jnp.where(line == 0, losses, jnp.where(line == 1, first, second))
    slot = lax.broadcasted_iota(jnp.int32, (1, rows), 1) // BLK
    total = jnp.sum(got_ref[:, :rank].astype(F32), axis=0)
    dlow = (total * jnp.where(slot < wins, first, second)).astype(BF16)
    one = first[:, :1]
    two = second[:, :1]
    near = modded_ref[:, pl.ds(pl.multiple_of(core * half, 128), half)]
    far = modded_ref[:, pl.ds(pl.multiple_of((1 - core) * half, 128), half)]
    b_own = product(split_ref[...], do_ref[...])
    b_other = product(split_ref[...], dt_ref[...])
    keep_ref[:rank] = one * b_own[:rank] + two * b_own[rank:]
    keep_ref[rank:] = product(dlow, near)
    give_ref[:rank] = (one * b_other[:rank] + two * b_other[rank:]).astype(BF16)
    give_ref[rank:] = product(dlow, far).astype(BF16)


def piles(ints, got, modded, split, d_own, d_other):
    lines = split.shape[0]
    half = d_own.shape[1]
    rows = got.shape[2]
    return pl.pallas_call(
        pile_kernel,
        out_shape=[
            jax.ShapeDtypeStruct((lines, half), F32),
            jax.ShapeDtypeStruct((lines, half), BF16),
            jax.ShapeDtypeStruct((8, rows), F32),
        ],
        in_specs=[pl.BlockSpec(memory_space=SMEM)] + [pl.BlockSpec(memory_space=pltpu.VMEM)] * 5,
        compiler_params=params(),
        cost_estimate=cost(6 * lines * half * rows, 16 * lines * half),
    )(ints, got, modded, split, d_own, d_other)


def dm_kernel(after_ref, do_ref, dt_ref, dlow_ref, own_ref, other_ref, a_ref, out_ref):
    total = rows_by_rows(do_ref[...], own_ref[...]) + rows_by_rows(dt_ref[...], other_ref[...])
    out_ref[...] = (total + product(dlow_ref[...], a_ref[...])).astype(BF16)


def dm_terms(after, d_own, d_other, dlow, own, other, a_turned):
    rows, half = d_own.shape
    width = own.shape[0]
    rank = dlow.shape[1]
    step = 512
    cut = pl.BlockSpec((step, half), lambda i: (i, 0))
    return pl.pallas_call(
        dm_kernel,
        grid=(width // step,),
        out_shape=jax.ShapeDtypeStruct((rows, width), BF16),
        in_specs=[
            pl.BlockSpec(memory_space=pl.ANY),
            whole((rows, half)),
            whole((rows, half)),
            whole((rows, rank)),
            cut,
            cut,
            pl.BlockSpec((rank, step), lambda i: (0, i)),
        ],
        out_specs=pl.BlockSpec((rows, step), lambda i: (0, i)),
        compiler_params=params(),
        cost_estimate=cost(4 * rows * width * half, 4 * width * half + 2 * rows * width),
    )(after, d_own, d_other, dlow, own, other, a_turned)


def token_kernel(ints_ref, one_ref, two_ref, three_ref, four_ref, x_ref, mod_ref, unit_ref, facts_ref, out_ref):
    total = one_ref[...].astype(F32) + two_ref[...].astype(F32)
    total = total + three_ref[...].astype(F32) + four_ref[...].astype(F32)
    normed, inverse = normalise(x_ref[...])
    first, _ = own_slot(ints_ref)
    coef = jnp.where(first, facts_ref[1:2, :1], facts_ref[2:3, :1])
    dn = total * (1.0 + pick(first, mod_ref, 1))
    mean_one = jnp.mean(dn, axis=-1, keepdims=True)
    mean_two = jnp.mean(dn * normed, axis=-1, keepdims=True)
    grad = coef * (unit_ref[...] + inverse * (dn - mean_one - normed * mean_two))
    out_ref[...] = grad.astype(BF16)


def token_gradient(ints, pieces, x_own, mod, unit, facts):
    rows, width = x_own.shape
    return pl.pallas_call(
        token_kernel,
        out_shape=jax.ShapeDtypeStruct((rows, width), BF16),
        in_specs=[pl.BlockSpec(memory_space=SMEM)] + [pl.BlockSpec(memory_space=pltpu.VMEM)] * 8,
        compiler_params=params(),
        cost_estimate=cost(20 * rows * width, 20 * rows * width),
    )(ints, *pieces, x_own, mod, unit, facts)


def per_device(
    tokens,
    targets,
    modulation,
    live_block_count,
    preferred_blocks,
    last_block_rows,
    up_rows,
    down_rows,
    factor_in,
    factor_out,
):
    width = tokens.shape[1]
    n_z, n_x, n_c, n_t = (lax.axis_size(a) for a in ("z", "x", "c", "t"))
    n_dp = n_z * n_x * n_c
    core = lax.axis_index("c")
    group = lax.axis_index("t")
    thin, hidden = up_rows.shape
    half = hidden // n_c
    rank = factor_in.shape[1]

    sent = down_rows.reshape(thin, n_c, half).transpose(1, 0, 2)
    sent = jnp.broadcast_to(sent[None], (n_x, n_c, thin, half)).reshape(n_x * n_c, thin, half)
    near = lax.all_to_all(sent, ("x", "c"), 0, 0, tiled=True)
    down_own = lax.all_gather(near.reshape(n_x * n_c * thin, half), "z", axis=0, tiled=True)

    up_rows, near = lax.optimization_barrier((up_rows, near))
    keep = lax.dynamic_slice_in_dim(up_rows, core * half, half, axis=1)
    got = lax.ppermute(lax.dynamic_slice_in_dim(up_rows, (1 - core) * half, half, axis=1), "c", SWAP)
    pair = jnp.where(core == 0, jnp.concatenate([keep, got], 0), jnp.concatenate([got, keep], 0))
    line = lax.all_gather(pair, "z", axis=0, tiled=True)

    ints = [preferred_blocks[0], live_block_count[0], last_block_rows[0, 0], last_block_rows[0, 1], group, core]
    ints = jnp.stack(ints).astype(jnp.int32)
    x_own = lax.dynamic_slice_in_dim(tokens, group * BLK, BLK, axis=0)
    t_own = lax.dynamic_slice_in_dim(targets, group * BLK, BLK, axis=0)
    mod = modulation.reshape(6, width)
    a_turned = factor_in.T
    modded, low, low_split = prepare(ints, tokens, mod, a_turned)

    blocks = after(spread(line, "x", n_x), [modded, low, low_split, x_own, t_own])
    up_own = blocks.reshape(n_x, n_z, n_c * thin, half).transpose(1, 0, 2, 3).reshape(width, half)
    up_other = lax.ppermute(up_own, "c", SWAP)
    down_other = lax.ppermute(down_own, "c", SWAP)

    pol_own, ref_own, slope_own = activate(False, ints, modded, low, up_own, factor_out)
    pol_other, ref_other, slope_other = activate(True, ints, modded, low, up_other, factor_out)
    part_pol = lower(pol_own, pol_other, down_own, down_other).reshape(CAP, BLK, width)
    got_pol = lax.all_to_all(part_pol, "t", 0, 0, tiled=True)
    part_ref = lower(ref_own, ref_other, down_own, down_other).reshape(CAP, BLK, width)

    unit, send = miss(ints, got_pol, part_ref, x_own, t_own, mod)
    got_dy = lax.all_to_all(send, "t", 0, 0, tiled=True)
    d_own, d_other, dlow_part, send = backward(
        ints, got_dy, unit, x_own, t_own, mod, down_own, down_other, factor_out, slope_own, slope_other
    )
    got_low = lax.all_to_all(send, "t", 0, 0, tiled=True)
    keep, give, facts = piles(ints, got_low, modded, low_split, d_own, d_other)
    losses = facts[0, :1]
    pile = (keep + lax.ppermute(give, "c", SWAP).astype(F32)).astype(BF16)

    chips = n_z * n_x
    pieces = lax.all_to_all(pile.reshape(chips, 2 * rank // chips, half), CHIPS, 0, 0, tiled=True)
    dm_part = dm_terms(pile, d_own, d_other, dlow_part, up_own, up_other, a_turned).reshape(CAP, BLK, width)
    turns = [[(i, (i + step) % n_t) for i in range(n_t)] for step in range(n_t)]
    chunks = [lax.dynamic_index_in_dim(dm_part, (group + step) % n_t, 0, False) for step in range(n_t)]
    chunks = [chunks[0]] + [lax.ppermute(chunks[step], "t", turns[step]) for step in range(1, n_t)]
    total = (jnp.sum(pieces.astype(F32), axis=0) / n_dp).astype(BF16)
    mine = spread(total, CHIPS, chips).reshape(2 * rank, half)
    grad_block = token_gradient(ints, chunks, x_own, mod, unit, facts)
    shares = [grad_block] + [lax.ppermute(grad_block, "t", turns[step]) for step in range(1, n_t)]
    shares = jnp.stack(shares)
    grad_tokens = jnp.concatenate(
        [lax.dynamic_index_in_dim(shares, (group - slot) % n_t, 0, False) for slot in range(n_t)], 0
    )
    theirs = lax.ppermute(mine, "c", SWAP)
    ends = jnp.concatenate([mine, theirs], 1)
    flipped = jnp.concatenate([theirs, mine], 1)
    ends = jnp.where(core == 0, ends, flipped).astype(F32)
    sum_b = ends[:rank]
    sum_a = ends[rank:].T
    return losses, grad_tokens, sum_a, sum_b


def solution(mesh):
    n_dp, n_t = mesh.devices.shape
    fine = Mesh(mesh.devices.reshape(n_dp // 8, 4, 2, n_t), ("z", "x", "c", "t"))
    return jax.shard_map(
        per_device,
        mesh=fine,
        in_specs=(
            P(DP, None),
            P(DP, None),
            P(DP, None, None),
            P(DP),
            P(DP),
            P(DP, None),
            P(DP, "t"),
            P(DP, "t"),
            P(),
            P(None, "t"),
        ),
        out_specs=(P(DP), P(DP, None), P(), P(None, "t")),
        check_vma=False,
    )
```
